32 devices in a mesh: row: 4 (over y, core), col: 8 (over z, x).
Axes of the slice: x: 2, y: 2, z: 4, core: 2. Of those that a mesh axis runs over, the one named last changes fastest.
Arguments:
- node_features: bfloat16 [8192, 512], P('col', 'row'), may hold values from -6 to 6
- layer_weight: bfloat16 [512, 512], replicated, may hold values from -0.25 to 0.25
- tile_values: bfloat16 [4, 8, 96, 128, 128], P('row', 'col')
- tile_coords: int32 [4, 8, 96, 2], P('row', 'col'), may hold values from 0 to 15, as said below
- tile_count: int32 [4, 8], P('row', 'col'), may hold values from 32 to 96, as said below
- cotangent: bfloat16 [8192, 512], P(('row', 'col')), may hold values from -6 to 6
Outputs:
- hidden: bfloat16 [8192, 512], P(('row', 'col'))
- grad_weight: float32 [512, 512], replicated
- grad_features: bfloat16 [8192, 512], P('col', 'row')
The draws below stay inside these ranges and needn't reach their ends.
Inputs may be any that keep to these rules, and one draw needn't show every extreme that they name: `tile_coords`: entry 0 of a slot is its destination tile within the destination block, below 16; entry 1 its source tile within the source block, below 8; the slots of one block pair name distinct positions. `tile_count`: slots at or beyond the count hold arbitrary tiles that are not part of the adjacency.
All inputs are finite; a program needn't handle non-finite values.
Results may differ from the reference program's by a relative error of at most 0.0054.
Values may be sent and summed in bfloat16 or wider, within the bound.
No kernel may reach another device: no remote copies, remote signals or barrier semaphores. Data moves between devices by JAX's collectives and lax.ppermute only.
A program may use at most 128 MiB of HBM per device.

```python
import math
import jax
import jax.numpy as jnp
from jax import lax

F = 512
TILE = 128
NODE_DEV = 256
TILES_DEV = 96
NODES = 8192
BLOCK_R = 2048
BLOCK_C = 1024
N_ROW = 4
N_COL = 8


def draw_tile_values(key, part):
    key = jax.random.fold_in(key, 11)
    key_live, key_size = jax.random.split(key, 2)
    shape = (N_ROW, N_COL, TILES_DEV, TILE, TILE)
    live = (jax.random.uniform(key_live, shape, jnp.float32) < 0.35).astype(jnp.float32)
    magnitude = jnp.exp(jax.random.uniform(key_size, shape, jnp.float32, math.log(0.5), math.log(2.0)))
    second = 1.2
    scale = (0.35 * second * TILES_DEV * TILE * TILE / NODE_DEV) ** (-0.5)
    return (live * magnitude * scale).astype(jnp.bfloat16)


def draw_tile_coords(key, part):
    key = jax.random.fold_in(key, 12)
    dest_tiles = NODE_DEV * N_COL // TILE
    source_tiles = NODE_DEV * N_ROW // TILE
    positions = dest_tiles * source_tiles
    keys = jax.random.split(key, N_ROW * N_COL)
    chosen = jax.vmap(lambda one_key: jax.random.permutation(one_key, positions)[:TILES_DEV])(keys)
    chosen = chosen.astype(jnp.int32)
    coords = jnp.stack([chosen // source_tiles, chosen % source_tiles], axis=-1)
    return coords.reshape(N_ROW, N_COL, TILES_DEV, 2).astype(jnp.int32)


def draw_tile_count(key, part):
    key = jax.random.fold_in(key, 13)
    counts = jax.random.randint(key, (N_ROW, N_COL), TILES_DEV // 3, TILES_DEV + 1, jnp.int32)
    counts = counts.at[0, 0].set(TILES_DEV)
    counts = counts.at[0, 1].set(TILES_DEV // 3)
    return counts


def level_of(key, shape, shards, least, top_value):
    loudness = 1.0
    for position, blocks in shards:
        draws = jax.random.uniform(jax.random.fold_in(jax.random.fold_in(key, 6), position), (blocks,), jnp.float32, least / len(shards), top_value / len(shards))
        loudness = loudness * jnp.repeat(jnp.exp(draws), shape[position] // blocks).reshape((-1,) + (1,) * (len(shape) - 1 - position))
    return loudness


def bell_draw(stream_key, dims, deviation, bound, cuts=(), kind=jnp.bfloat16):
    drawn = jax.random.normal(stream_key, dims, jnp.float32) * deviation
    if len(cuts) > 0:
        drawn = level_of(stream_key, dims, cuts, -0.22, 0.18) * drawn
    return jnp.clip(drawn, min=-bound, max=bound).astype(kind)


def setup_inputs(seed: int = 0) -> dict:
    splits = jax.random.split(jax.random.key(seed), 7)
    node_features = bell_draw(splits[0], (NODES, F), 1.0, 6.0, ((0, 8), (1, 4)))
    layer_weight = bell_draw(splits[1], (F, F), F ** -0.5, 0.25)
    tile_values = draw_tile_values(jax.random.fold_in(splits[6], 71), 0)
    tile_coords = draw_tile_coords(jax.random.fold_in(splits[6], 71), 0)
    tile_count = draw_tile_count(jax.random.fold_in(splits[6], 71), 0)
    cotangent = bell_draw(splits[5], (NODES, F), 1.0, 6.0, ((0, 32),))
    return dict(node_features=node_features, layer_weight=layer_weight, tile_values=tile_values, tile_coords=tile_coords, tile_count=tile_count, cotangent=cotangent)


def forward_block(tiles, coords, live_count, source_rows):
    slots = tiles.shape[0]
    gathered_rows = source_rows.reshape(BLOCK_C // TILE, TILE, F)[coords[:, 1]]
    product = jnp.einsum('tab,tbk->tak', tiles.astype(jnp.float32), gathered_rows.astype(jnp.float32))
    is_live = jnp.arange(slots) < live_count
    product = jnp.where(is_live[:, None, None], product, jnp.float32(0.0))
    summed = jax.ops.segment_sum(product, coords[:, 0], num_segments=BLOCK_R // TILE)
    return summed.reshape(BLOCK_R, F)


def backward_block(tiles, coords, live_count, dest_rows):
    slots = tiles.shape[0]
    gathered_rows = dest_rows.reshape(BLOCK_R // TILE, TILE, F)[coords[:, 0]]
    product = jnp.einsum('tab,tak->tbk', tiles.astype(jnp.float32), gathered_rows.astype(jnp.float32))
    is_live = jnp.arange(slots) < live_count
    product = jnp.where(is_live[:, None, None], product, jnp.float32(0.0))
    summed = jax.ops.segment_sum(product, coords[:, 1], num_segments=BLOCK_C // TILE)
    return summed.reshape(BLOCK_C, F)


def reference(node_features, layer_weight, tile_values, tile_coords, tile_count, cotangent):
    pairs = N_ROW * N_COL

    def forward_pair(index, totals):
        dest = (index // N_COL).astype(jnp.int32)
        source = (index % N_COL).astype(jnp.int32)
        source_rows = lax.dynamic_slice_in_dim(node_features, (source * BLOCK_C).astype(jnp.int32), BLOCK_C, 0)
        term = forward_block(tile_values[dest, source], tile_coords[dest, source], tile_count[dest, source], source_rows)
        current = lax.dynamic_slice_in_dim(totals, (dest * BLOCK_R).astype(jnp.int32), BLOCK_R, 0)
        return lax.dynamic_update_slice_in_dim(totals, current + term, (dest * BLOCK_R).astype(jnp.int32), 0)

    summed = lax.fori_loop(0, pairs, forward_pair, jnp.zeros((NODES, F), jnp.float32))
    aggregated = summed.astype(jnp.bfloat16)
    pre_act = jnp.dot(aggregated, layer_weight, preferred_element_type=jnp.float32)
    hidden = jax.nn.elu(pre_act).astype(jnp.bfloat16)
    slope = jnp.where(pre_act > 0, jnp.float32(1.0), jnp.exp(jnp.minimum(pre_act, 0.0)))
    grad_pre = (cotangent.astype(jnp.float32) * slope).astype(jnp.bfloat16)
    grad_weight = jnp.dot(aggregated.T, grad_pre, preferred_element_type=jnp.float32)
    grad_agg = jnp.dot(grad_pre, layer_weight.T, preferred_element_type=jnp.float32).astype(jnp.bfloat16)

    def backward_pair(index, totals):
        dest = (index // N_COL).astype(jnp.int32)
        source = (index % N_COL).astype(jnp.int32)
        dest_rows = lax.dynamic_slice_in_dim(grad_agg, (dest * BLOCK_R).astype(jnp.int32), BLOCK_R, 0)
        term = backward_block(tile_values[dest, source], tile_coords[dest, source], tile_count[dest, source], dest_rows)
        current = lax.dynamic_slice_in_dim(totals, (source * BLOCK_C).astype(jnp.int32), BLOCK_C, 0)
        return lax.dynamic_update_slice_in_dim(totals, current + term, (source * BLOCK_C).astype(jnp.int32), 0)

    back = lax.fori_loop(0, pairs, backward_pair, jnp.zeros((NODES, F), jnp.float32))
    return hidden, grad_weight, back.astype(jnp.bfloat16)
```

```python
import functools
import math

import jax
import jax.numpy as jnp
from jax import lax
from jax.experimental import pallas as pl
from jax.experimental.pallas import tpu as pltpu
from jax.sharding import PartitionSpec as P

F32 = jnp.float32
BF16 = jnp.bfloat16
MIB = 1024 * 1024
COST, COST_S, COST_W, COST_M = 4_000_000_000, 1_000_000_000, 4_000_000_000, 4_000_000_000
SMEM = pl.BlockSpec(memory_space=pltpu.SMEM)
VMEM = pl.BlockSpec(memory_space=pltpu.VMEM)
ANYWHERE = pl.BlockSpec(memory_space=pl.ANY)


def call(kernel, out_shape, in_specs, operands, scratch=(), limit=16, before=(), cost=0):
    many = isinstance(out_shape, (tuple, list))
    count = len(operands)

    def run(*refs):
        kernel(*refs[:count], *refs[count + len(before) :])

    return pl.pallas_call(
        run,
        out_shape=tuple(out_shape) if many else out_shape,
        in_specs=list(in_specs) + [ANYWHERE] * len(before),
        out_specs=(VMEM,) * len(out_shape) if many else VMEM,
        scratch_shapes=list(scratch),
        compiler_params=pltpu.CompilerParams(vmem_limit_bytes=limit * MIB),
        cost_estimate=pl.CostEstimate(flops=cost, bytes_accessed=0, transcendentals=0),
    )(*operands, *before)


def place_tiles(
    outer,
    shard_tiles,
    count_ref,
    me_ref,
    coords_hbm,
    tiles_ref,
    features_hbm,
    near_ref,
    far_ref,
    features_ref,
    away_ref,
    coords_ref,
    tile_sem,
    in_sems,
):
    slots, tile, _ = tiles_ref.shape
    coords_copy = pltpu.make_async_copy(coords_hbm, coords_ref, in_sems.at[0])
    features_copy = pltpu.make_async_copy(features_hbm, features_ref, in_sems.at[1])
    coords_copy.start()
    features_copy.start()
    me = me_ref[0]
    count = count_ref[0]
    near_ref[...] = jnp.zeros_like(near_ref)
    far_ref[...] = jnp.zeros_like(far_ref)
    coords_copy.wait()
    shift = shard_tiles.bit_length() - 1

    def start(t, carry):
        dest = coords_ref[0, t]
        rel = lax.shift_right_logical(dest, shift) ^ me
        place, bit = 0, 2
        while bit <= outer:
            moved = (outer // bit).bit_length() - bit.bit_length()
            taken = rel & bit
            place = place | (
                lax.shift_left(taken, moved) if moved >= 0 else lax.shift_right_logical(taken, -moved)
            )
            bit *= 2
        row = lax.shift_left(place, shift) | (dest & (shard_tiles - 1))
        rows = pl.ds(pl.multiple_of(row * tile, tile), tile)
        cols = pl.ds(pl.multiple_of(coords_ref[1, t] * tile, tile), tile)

        @pl.when((rel & 1) == 0)
        def _():
            pltpu.make_async_copy(tiles_ref.at[t], near_ref.at[rows, cols], tile_sem).start()

        @pl.when((rel & 1) != 0)
        def _():
            pltpu.make_async_copy(tiles_ref.at[t], far_ref.at[rows, cols], tile_sem).start()

        return carry

    lax.fori_loop(0, count, start, 0)
    some = 1
    while some <= slots:

        @pl.when((count & some) != 0)
        def _():
            part = tiles_ref.at[pl.ds(0, some)]
            pltpu.make_async_copy(part, part, tile_sem).wait()

        some *= 2
    features_copy.wait()
    step = math.gcd(far_ref.shape[0], 256)
    for row in range(0, far_ref.shape[0], step):
        rows = pl.ds(row, step)
        away = jnp.dot(far_ref[rows, :], features_ref[...], preferred_element_type=F32)
        away_ref[rows, :] = away.astype(away_ref.dtype)


def dense_blocks(tiles, coords, count, me, features, outer, shard_rows, limit):
    slots, tile, _ = tiles.shape
    block_c, width = features.shape
    half_rows = outer * shard_rows
    return call(
        functools.partial(place_tiles, outer, shard_rows // tile),
        (
            jax.ShapeDtypeStruct((half_rows, block_c), tiles.dtype),
            jax.ShapeDtypeStruct((half_rows, block_c), tiles.dtype),
            jax.ShapeDtypeStruct(features.shape, BF16),
            jax.ShapeDtypeStruct((half_rows, width), BF16),
        ),
        [SMEM, SMEM, ANYWHERE, pl.BlockSpec(memory_space=pltpu.HBM), ANYWHERE],
        (count, me, coords, tiles, features),
        [
            pltpu.SMEM(coords.shape, jnp.int32),
            pltpu.SemaphoreType.DMA,
            pltpu.SemaphoreType.DMA((2,)),
        ],
        limit,
    )


def copy_whole(in_ref, out_ref):
    out_ref[...] = in_ref[...]


def products(unit, near_ref, far_ref, *refs):
    chunk_refs, away_refs, kept_refs = refs[:4], refs[4:6], refs[6:9]
    last_keep_ref, last_send_ref, all_ref = refs[9:]
    width = chunk_refs[0].shape[1]
    for i, chunk in enumerate(chunk_refs):
        all_ref[:, i * width : (i + 1) * width] = chunk[...]
    half_rows = near_ref.shape[0]
    step = math.gcd(unit, 256)

    def put_last(block, row, values):
        shard = row // unit
        rows = pl.ds(shard // 2 * unit + row % unit, step)
        if shard % 2 == 0:
            last_keep_ref[block, rows, :] = values
        else:
            last_send_ref[block, rows, :] = values.astype(last_send_ref.dtype)

    for row in range(0, half_rows, step):
        rows = pl.ds(row, step)
        away = jnp.dot(far_ref[rows, :], all_ref[:, width:], preferred_element_type=F32)
        for i, out in enumerate(away_refs):
            out[rows, :] = away[:, i * width : (i + 1) * width].astype(out.dtype)
        put_last(1, row, away[:, 2 * width :])
    for row in range(0, half_rows, step):
        rows = pl.ds(row, step)
        kept = jnp.dot(near_ref[rows, :], all_ref[...], preferred_element_type=F32)
        for i, out in enumerate(kept_refs):
            out[rows, :] = kept[:, i * width : (i + 1) * width]
        put_last(0, row, kept[:, 3 * width :])


def all_products(near, far, features, unit, limit):
    half_rows, block_c = near.shape
    width = features[0].shape[1]
    away = jax.ShapeDtypeStruct((half_rows, width), BF16)
    kept = jax.ShapeDtypeStruct((half_rows, width), F32)
    last = (2, half_rows // 2, width)
    outs = call(
        functools.partial(products, unit),
        [away] * 2 + [kept] * 3 + [jax.ShapeDtypeStruct(last, F32), jax.ShapeDtypeStruct(last, BF16)],
        [VMEM] * 6,
        (near, far, *features),
        [pltpu.VMEM((block_c, 4 * width), BF16)],
        limit,
    )
    return outs[:2], outs[2:5], outs[5], outs[6]


def add_and_halve(unit, kept_ref, came_ref, keep_ref, send_ref):
    rows = keep_ref.shape[-2]
    first, second = pl.ds(0, rows), pl.ds(rows, rows)
    if len(kept_ref.shape) == 2:
        keep_ref[...] = kept_ref[first, :] + came_ref[first, :].astype(F32)
        send_ref[...] = (kept_ref[second, :] + came_ref[second, :].astype(F32)).astype(send_ref.dtype)
        return
    for i in range(kept_ref.shape[0]):
        for j in range(rows // unit):
            here = pl.ds(j * unit, unit)
            even, odd = pl.ds(2 * j * unit, unit), pl.ds((2 * j + 1) * unit, unit)
            keep_ref[i, here, :] = kept_ref[i, even, :] + came_ref[i, even, :].astype(F32)
            total = kept_ref[i, odd, :] + came_ref[i, odd, :].astype(F32)
            send_ref[i, here, :] = total.astype(send_ref.dtype)


def halved(kept, came, unit, before):
    shape = kept.shape[:-2] + (kept.shape[-2] // 2, kept.shape[-1])
    return call(
        functools.partial(add_and_halve, unit),
        (jax.ShapeDtypeStruct(shape, F32), jax.ShapeDtypeStruct(shape, BF16)),
        [VMEM] * 2,
        (kept, came),
        before=before,
    )


def add_and_part(kept_ref, came_ref, keep_ref, *send_refs):
    rows = keep_ref.shape[0]
    keep_ref[...] = kept_ref[:rows, :] + came_ref[:rows, :].astype(F32)
    for i, out in enumerate(send_refs):
        part = pl.ds((i + 1) * rows, rows)
        out[...] = (kept_ref[part, :] + came_ref[part, :].astype(F32)).astype(out.dtype)


def parted(kept, came, count, before):
    shape = (kept.shape[0] // count, kept.shape[1])
    outs = call(
        add_and_part,
        [jax.ShapeDtypeStruct(shape, F32)] + [jax.ShapeDtypeStruct(shape, BF16)] * (count - 1),
        [VMEM] * 2,
        (kept, came),
        before=before,
    )
    return outs[0], outs[1:]


def add_pair(kept_ref, came_ref, keep_ref, send_ref):
    keep_ref[...] = kept_ref[0] + came_ref[0].astype(F32)
    send_ref[...] = (kept_ref[1] + came_ref[1].astype(F32)).astype(send_ref.dtype)


def join_two(first_ref, second_ref, out_ref):
    out_ref[pl.ds(0, first_ref.shape[0])] = first_ref[...]
    out_ref[pl.ds(first_ref.shape[0], first_ref.shape[0])] = second_ref[...]


def joined(first, second, before, cost=0):
    shape = (2 * first.shape[0],) + first.shape[1:]
    return call(
        join_two,
        jax.ShapeDtypeStruct(shape, first.dtype),
        [VMEM] * 2,
        (first, second),
        before=before,
        cost=cost,
    )


def mark(out_ref):
    out_ref[...] = jnp.zeros_like(out_ref)


def marked(*before, cost=0):
    return call(mark, jax.ShapeDtypeStruct((8, 128), F32), [], (), before=before, cost=cost)


def order_rows(owners, me_ref, weight_ref, out_ref):
    part = weight_ref.shape[0] // len(owners)
    for i, rels in enumerate(owners):
        piece = part // len(rels)
        for j, rel in enumerate(rels):
            source = pl.ds(pl.multiple_of((me_ref[0] ^ rel) * piece, piece), piece)
            out_ref[pl.ds(i * part + j * piece, piece), :] = weight_ref[source, :]


def dense_layer(counts, out_groups, *refs):
    total_refs, refs = refs[: sum(counts)], refs[sum(counts) :]
    rows_ref, cotangent_ref, hidden_ref, agg_ref, grad_pre_ref = refs[:5]
    grad_refs = refs[5:]
    part = rows_ref.shape[0] // len(counts)
    at = 0
    for i, count in enumerate(counts):
        total = total_refs[at][...]
        for ref in total_refs[at + 1 : at + count]:
            total = total + ref[...].astype(F32)
        agg_ref[:, i * part : (i + 1) * part] = total.astype(agg_ref.dtype)
        at += count
    pre_act = jnp.dot(agg_ref[...], rows_ref[...], preferred_element_type=F32)
    slope = jnp.exp(jnp.minimum(pre_act, 0.0))
    positive = pre_act > 0
    hidden_ref[...] = jnp.where(positive, pre_act, slope - 1.0).astype(hidden_ref.dtype)
    slope = jnp.where(positive, F32(1.0), slope)
    grad_pre = (cotangent_ref[...].astype(F32) * slope).astype(grad_pre_ref.dtype)
    grad_pre_ref[...] = grad_pre
    for members, out in zip(out_groups, grad_refs):
        for j, i in enumerate(members):
            out[0, pl.ds(j * part, part), :] = lax.dot_general(
                rows_ref[pl.ds(i * part, part), :],
                grad_pre,
                (((1,), (1,)), ((), ())),
                preferred_element_type=F32,
            ).astype(out.dtype)


def layer(totals, out_groups, weight_rows, cotangent, before):
    shard_rows, width = cotangent.shape
    part = width // len(totals)
    whole = jax.ShapeDtypeStruct((shard_rows, width), BF16)
    grads = [jax.ShapeDtypeStruct((1, len(m) * part, shard_rows), BF16) for m in out_groups]
    counts = [len(terms) for terms in totals]
    outs = call(
        functools.partial(dense_layer, counts, out_groups),
        [whole] * 3 + grads,
        [VMEM] * (sum(counts) + 2),
        (*[term for terms in totals for term in terms], weight_rows, cotangent),
        before=before,
    )
    return outs[0], outs[1], outs[2], outs[3:]


def back_products(count, near_ref, far_ref, *refs):
    rows_refs, out_refs, (left_ref, right_ref) = refs[:count], refs[count:-2], refs[-2:]
    shard_rows = rows_refs[0].shape[2]
    for k in range(left_ref.shape[1] // shard_rows):
        cols = pl.ds(k * shard_rows, shard_rows)
        if count == 2:
            left_ref[:, cols] = rows_refs[0][k]
            right_ref[:, cols] = rows_refs[1][k]
        else:
            left_ref[:, cols] = rows_refs[0][2 * k]
            right_ref[:, cols] = rows_refs[0][2 * k + 1]
    block_c = near_ref.shape[1]
    step = math.gcd(block_c, 256)
    part = out_refs[0].shape[0]
    for col in range(0, block_c, step):
        cols = pl.ds(col, step)
        total = jnp.dot(left_ref[...], near_ref[:, cols], preferred_element_type=F32)
        total = total + jnp.dot(right_ref[...], far_ref[:, cols], preferred_element_type=F32)
        for i, out in enumerate(out_refs):
            out[:, cols] = total[i * part : (i + 1) * part, :].astype(out.dtype)


def back_of(near, far, rows, dtypes, limit, before, cost=0):
    height = rows[0].shape[1]
    shape = (height // len(dtypes), near.shape[1])
    return call(
        functools.partial(back_products, len(rows)),
        [jax.ShapeDtypeStruct(shape, dtype) for dtype in dtypes],
        [VMEM] * (2 + len(rows)),
        (near, far, *rows),
        [pltpu.VMEM((height, near.shape[0]), BF16)] * 2,
        limit,
        before=before,
        cost=cost,
    )


def add_parts(places, own_ref, came_ref, *out_refs):
    piece = out_refs[0].shape[0]
    for place, out in zip(places, out_refs):
        rows = pl.ds(place * piece, piece)
        out[...] = (own_ref[rows, :] + came_ref[rows, :].astype(F32)).astype(out.dtype)


def parts_to_send(own, came, places, piece, before):
    shape = jax.ShapeDtypeStruct((piece, own.shape[1]), BF16)
    return call(
        functools.partial(add_parts, places),
        [shape] * len(places),
        [VMEM] * 2,
        (own, came),
        before=before,
    )


def finish(own_ref, came_ref, *refs):
    out_ref = refs[-1]
    piece = out_ref.shape[1]
    total = own_ref[:piece, :] + came_ref[:piece, :].astype(F32)
    for ref in refs[:-1]:
        total = total + ref[...].astype(F32)
    out_ref[...] = total.T.astype(out_ref.dtype)


def weight_terms(places, agg_ref, grad_pre_ref, *out_refs):
    width = agg_ref.shape[1]
    piece = width // sum(len(group) for group in places)
    for group, out in zip(places, out_refs):
        for i, place in enumerate(group):
            term = lax.dot_general(
                agg_ref[:, place * piece : (place + 1) * piece],
                grad_pre_ref[...],
                (((0,), (0,)), ((), ())),
                preferred_element_type=F32,
            )
            out[pl.ds(i * piece, piece), :] = term.astype(out.dtype)


def add_and_split(side_ref, kept_ref, came_ref, keep_ref, send_ref, total_ref):
    total_ref[...] = kept_ref[...] + came_ref[...]
    half = keep_ref.shape[1]
    side = side_ref[0] & 1
    for k in range(keep_ref.shape[0]):
        mine = pl.ds(pl.multiple_of((2 * k + side) * half, half), half)
        other = pl.ds(pl.multiple_of((2 * k + 1 - side) * half, half), half)
        keep_ref[k] = total_ref[mine, :]
        send_ref[k] = total_ref[other, :].astype(send_ref.dtype)


def add_and_spread(kept_ref, came_ref, keep_ref, *send_refs):
    keep_ref[...] = kept_ref[0] + came_ref[0].astype(F32)
    for k, out in enumerate(send_refs):
        out[...] = (kept_ref[k + 1] + came_ref[k + 1].astype(F32)).astype(out.dtype)


def add_all(*refs):
    terms = [ref[...].astype(F32) for ref in refs[:-1]]
    while len(terms) > 1:
        terms = [sum(terms[i + 1 : i + 2], terms[i]) for i in range(0, len(terms), 2)]
    refs[-1][...] = terms[0].astype(refs[-1].dtype)


def sum_of(terms, dtype, before, cost=0):
    return call(
        add_all,
        jax.ShapeDtypeStruct(terms[0].shape, dtype),
        [VMEM] * len(terms),
        tuple(terms),
        before=before,
        cost=cost,
    )


def stack_all(*refs):
    for i, ref in enumerate(refs[:-1]):
        refs[-1][i] = ref[...]


def place_shares(me_ref, side_ref, own_ref, other_ref, out_ref):
    half = own_ref.shape[2]
    for inner, ref in ((0, own_ref), (1, other_ref)):
        for turn in range(2):
            side = (side_ref[0] ^ turn) & 1
            for k in range(ref.shape[1]):
                place = (me_ref[0] ^ (2 * k + inner)) * 2 + side
                out_ref[pl.ds(pl.multiple_of(place * half, half), half), :] = ref[turn, k].astype(
                    out_ref.dtype
                )


def body(node_features, layer_weight, tile_values, tile_coords, tile_count, cotangent):
    n_row = lax.axis_size("row")
    n_col = lax.axis_size("col")
    ro, co = n_row // 2, n_col // 2
    my_row = lax.axis_index("row").astype(jnp.int32).reshape(1)
    my_col = lax.axis_index("col").astype(jnp.int32).reshape(1)
    shard_rows, width = cotangent.shape
    block_c, piece = node_features.shape
    limit = 12 + (4 * co * shard_rows * block_c) // MIB

    def swap(v, axis, bit):
        size = n_row if axis == "row" else n_col
        return lax.ppermute(v, axis, [(i, i ^ bit) for i in range(size)])

    halves = (range(0, ro // 2), range(ro // 2, ro))
    chunks = [(h, i) for h in range(2) for i in range(2)]
    owners = [[2 * k + i for k in halves[h]] for h, i in chunks]
    flat = [rel for rels in owners for rel in rels]

    features = []
    for h, inner in chunks:
        if inner == 0:
            parts = [swap(node_features, "row", 2 * k) if k else node_features for k in halves[h]]
            features.append(jnp.concatenate(parts, axis=1) if len(parts) > 1 else parts[0])
        else:
            features.append(None)
    features[1] = swap(features[0], "row", 1)
    near, far, own_features, first_away = dense_blocks(
        tile_values[0, 0],
        pltpu.with_memory_space_constraint(tile_coords[0, 0].T, pltpu.HBM),
        tile_count.reshape(-1),
        my_col,
        pltpu.with_memory_space_constraint(features[0], pltpu.HBM),
        co,
        shard_rows,
        max(limit, 48),
    )
    held = call(
        copy_whole,
        jax.ShapeDtypeStruct(features[2].shape, BF16),
        [VMEM],
        (features[2],),
        before=(first_away,),
    )
    features[3] = swap(held, "row", 1)
    features[0] = own_features
    away, kept, last_keep, last_send = all_products(near, far, features, shard_rows, limit)

    stages = co.bit_length() - 1
    reversed_bits = [sum(((p >> i) & 1) << (stages - 1 - i) for i in range(stages)) for p in range(co)]
    keeps = [*kept, last_keep]
    cames = [swap(v, "col", 1) for v in (first_away, *away)] + [swap(last_send, "col", n_col // 2)]
    totals = [None] * 4
    done = [0, 0, 0, 1]
    turns = [0, 1, 0, 3, 2, 1, 3] if stages == 2 else ([0, 1, 3] * stages + [2])
    weight_rows = call(
        functools.partial(order_rows, owners),
        jax.ShapeDtypeStruct(layer_weight.shape, BF16),
        [SMEM, VMEM],
        (my_row, layer_weight),
        before=(last_keep,),
    )
    last = weight_rows
    for i in turns:
        before = [last]
        if stages == 2 and i == 3 and done[3] == 1:
            before.append(cames[0])
        if i == 2:
            own, sends = parted(keeps[2], cames[2], co, before)
            last = sends[0]
            totals[2] = [own] + [
                swap(send, "col", 2 * reversed_bits[p + 1]) for p, send in enumerate(sends)
            ]
        elif i == 3 and done[3] == stages:
            shape = keeps[3].shape[1:]
            own, last = call(
                add_pair,
                (jax.ShapeDtypeStruct(shape, F32), jax.ShapeDtypeStruct(shape, BF16)),
                [VMEM] * 2,
                (keeps[3], cames[3]),
                before=before,
            )
            totals[3] = [own, swap(last, "col", 1)]
        else:
            keeps[i], last = halved(keeps[i], cames[i], shard_rows, before)
            done[i] += 1
            cames[i] = swap(last, "col", 1 << done[i] if i < 3 else n_col >> done[i])
            totals[i] = [keeps[i], cames[i]]

    out_groups = ((3,), (2,), (1, 0))
    hidden, agg, grad_pre, grads = layer(
        totals, out_groups, weight_rows, cotangent, (marked(last, cames[1]),)
    )

    places = [[flat.index(2 * k + inner) for k in range(ro)] for inner in range(2)]
    term_shape = (width // 2, width)
    weight_kept, weight_send = call(
        functools.partial(weight_terms, places),
        (jax.ShapeDtypeStruct(term_shape, F32), jax.ShapeDtypeStruct(term_shape, F32)),
        [VMEM] * 2,
        (agg, grad_pre),
    )
    state = {"w": [weight_kept, swap(weight_send, "row", 1)], "last": weight_send}

    def order(*more):
        return [state["last"], *more]

    half_share = (ro, piece // 2, width)

    def weight_core():
        keep, send = call(
            add_and_split,
            (jax.ShapeDtypeStruct(half_share, F32), jax.ShapeDtypeStruct(half_share, BF16)),
            [SMEM, VMEM, VMEM],
            (my_col, *state["w"]),
            [pltpu.VMEM((ro * piece, width), F32)],
            before=order(),
        )
        state["last"] = send
        state["w"] = [keep, swap(send, "col", 1)]

    def weight_side():
        shape = half_share[1:]
        outs = call(
            add_and_spread,
            [jax.ShapeDtypeStruct(shape, F32)] + [jax.ShapeDtypeStruct(shape, BF16)] * (ro - 1),
            [VMEM] * 2,
            tuple(state["w"]),
            before=order(),
        )
        state["last"] = outs[0]
        state["w"] = [outs[0]] + [swap(v, "row", 2 * (k + 1)) for k, v in enumerate(outs[1:])]

    def weight_line():
        total = sum_of(state["w"], BF16, order())
        state["last"] = total
        state["w"] = [total] + [swap(total, "col", 2 * k) for k in range(1, co)]

    def weight_sum():
        total = sum_of(state["w"], BF16, order(), COST_W)
        state["last"] = total
        state["w"] = [total] + [swap(total, "row", 2 * k) for k in range(1, ro)]

    def weight_stack(axis):
        total = call(
            stack_all,
            jax.ShapeDtypeStruct((len(state["w"]),) + state["w"][0].shape, BF16),
            [VMEM] * len(state["w"]),
            tuple(state["w"]),
            before=order(),
        )
        state["last"] = total
        state["w"] = [total, swap(total, axis, 1)]

    rows = {"C": grads[0], "A": grads[1], "M": grads[2]}
    bits = {"C": n_col // 2, "A": 1, "M": n_col // 2}
    came_rows = {name: swap(rows[name], "col", bits[name]) for name in rows}
    backs = {}

    def join(name, cost=0):
        first, second = rows[name], came_rows[name]
        bit = n_col // 2 if name == "A" and bits[name] == 1 else bits[name] // 2
        bits[name] = bit
        rows[name] = state["last"] = joined(first, second, order(), cost)
        if not (name == "A" and bit == 1):
            came_rows[name] = swap(rows[name], "col", bit)

    def back(members, pair, cost=0, more=()):
        dtypes = [BF16 if chunk[1] else F32 for chunk in members]
        outs = back_of(near, far, pair, dtypes, limit, order(*more), cost)
        state["last"] = outs[0]
        for chunk, out in zip(members, outs):
            backs[chunk] = swap(out, "row", 1) if chunk[1] else out

    arrived = []

    def send_parts(h):
        sent = [p for p, k in enumerate(halves[h]) if k > 0]
        if sent:
            parts = parts_to_send(backs[h, 0], backs[h, 1], sent, piece, order())
            state["last"] = parts[0]
            arrived.extend(swap(v, "row", 2 * halves[h][p]) for p, v in zip(sent, parts))

    weight_core()
    join("A")
    join("C")
    weight_side()
    join("M")
    for _ in range(stages - 1):
        join("C")
    weight_line()
    for _ in range(stages - 1):
        join("A", COST)
    back([(1, 1)], (rows["C"], came_rows["C"]))
    for _ in range(stages - 1):
        join("M")
    weight_sum()
    weight_stack("col")
    join("A", COST_S)
    back([(1, 0)], (rows["A"],))
    send_parts(1)
    back([(0, 1), (0, 0)], (rows["M"], came_rows["M"]), COST_M)
    weight_stack("row")
    send_parts(0)
    state["last"] = marked(state["last"], *arrived, cost=COST)
    grad_features = call(
        finish,
        jax.ShapeDtypeStruct((block_c, piece), BF16),
        [VMEM] * (2 + len(arrived)),
        (backs[0, 0], backs[0, 1], *arrived),
        before=order(),
    )
    grad_weight = call(
        place_shares,
        jax.ShapeDtypeStruct((width, width), F32),
        [SMEM, SMEM, VMEM, VMEM],
        (my_row, my_col, *state["w"]),
    )
    return (hidden, grad_weight, grad_features)


def solution(mesh):
    in_specs = (
        P("col", "row"),
        P(),
        P("row", "col", None, None, None),
        P("row", "col", None, None),
        P("row", "col"),
        P(("row", "col"), None),
    )
    out_specs = (P(("row", "col"), None), P(), P("col", "row"))
    return jax.shard_map(body, mesh=mesh, in_specs=in_specs, out_specs=out_specs, check_vma=False)
```

```python
import functools
import math

import jax
import jax.numpy as jnp
from jax import lax
from jax.experimental import pallas as pl
from jax.experimental.pallas import tpu as pltpu
from jax.sharding import PartitionSpec as P

F32 = jnp.float32
BF16 = jnp.bfloat16
MIB = 1024 * 1024
COST_F = 1_000_000_000
COST, COST_S, COST_W, COST_M = 4_000_000_000, 1_000_000_000, 4_000_000_000, 4_000_000_000
SMEM = pl.BlockSpec(memory_space=pltpu.SMEM)
VMEM = pl.BlockSpec(memory_space=pltpu.VMEM)
ANYWHERE = pl.BlockSpec(memory_space=pl.ANY)


def call(kernel, out_shape, in_specs, operands, scratch=(), limit=16, before=(), cost=0):
    many = isinstance(out_shape, (tuple, list))
    count = len(operands)

    def run(*refs):
        kernel(*refs[:count], *refs[count + len(before) :])

    return pl.pallas_call(
        run,
        out_shape=tuple(out_shape) if many else out_shape,
        in_specs=list(in_specs) + [ANYWHERE] * len(before),
        out_specs=(VMEM,) * len(out_shape) if many else VMEM,
        scratch_shapes=list(scratch),
        compiler_params=pltpu.CompilerParams(vmem_limit_bytes=limit * MIB),
        cost_estimate=pl.CostEstimate(flops=cost, bytes_accessed=0, transcendentals=0),
    )(*operands, *before)


def place_tiles(
    outer,
    shard_tiles,
    count_ref,
    me_ref,
    row_ref,
    coords_hbm,
    tiles_ref,
    features_hbm,
    near_ref,
    far_ref,
    features_ref,
    away_ref,
    coords_ref,
    tile_sem,
    in_sems,
):
    slots, tile, _ = tiles_ref.shape
    coords_copy = pltpu.make_async_copy(coords_hbm, coords_ref, in_sems.at[0])
    features_copy = pltpu.make_async_copy(features_hbm, features_ref, in_sems.at[1])
    coords_copy.start()
    features_copy.start()
    me = me_ref[0]
    count = count_ref[0]
    near_ref[...] = jnp.zeros_like(near_ref)
    far_ref[...] = jnp.zeros_like(far_ref)
    coords_copy.wait()
    shift = shard_tiles.bit_length() - 1

    def start(t, carry):
        dest = coords_ref[0, t]
        rel = lax.shift_right_logical(dest, shift) ^ me
        place, bit = 0, 2
        while bit <= outer:
            moved = (outer // bit).bit_length() - bit.bit_length()
            taken = rel & bit
            place = place | (
                lax.shift_left(taken, moved) if moved >= 0 else lax.shift_right_logical(taken, -moved)
            )
            bit *= 2
        row = lax.shift_left(place, shift) | (dest & (shard_tiles - 1))
        rows = pl.ds(pl.multiple_of(row * tile, tile), tile)
        cols = pl.ds(pl.multiple_of(coords_ref[1, t] * tile, tile), tile)

        @pl.when((rel & 1) == 0)
        def _():
            pltpu.make_async_copy(tiles_ref.at[t], near_ref.at[rows, cols], tile_sem).start()

        @pl.when((rel & 1) != 0)
        def _():
            pltpu.make_async_copy(tiles_ref.at[t], far_ref.at[rows, cols], tile_sem).start()

        return carry

    lax.fori_loop(0, count, start, 0)
    some = 1
    while some <= slots:

        @pl.when((count & some) != 0)
        def _():
            part = tiles_ref.at[pl.ds(0, some)]
            pltpu.make_async_copy(part, part, tile_sem).wait()

        some *= 2
    features_copy.wait()
    step = math.gcd(far_ref.shape[0], 256)
    for row in range(0, far_ref.shape[0], step):
        rows = pl.ds(row, step)
        away = jnp.dot(far_ref[rows, :], features_ref[...], preferred_element_type=F32)
        away_ref[rows, :] = away.astype(away_ref.dtype)


def dense_blocks(tiles, coords, count, me, row, features, outer, shard_rows, limit):
    slots, tile, _ = tiles.shape
    block_c, width = features.shape
    half_rows = outer * shard_rows
    return call(
        functools.partial(place_tiles, outer, shard_rows // tile),
        (
            jax.ShapeDtypeStruct((half_rows, block_c), tiles.dtype),
            jax.ShapeDtypeStruct((half_rows, block_c), tiles.dtype),
            jax.ShapeDtypeStruct(features.shape, BF16),
            jax.ShapeDtypeStruct((half_rows, width), BF16),
        ),
        [SMEM, SMEM, SMEM, ANYWHERE, pl.BlockSpec(memory_space=pltpu.HBM), ANYWHERE],
        (count, me, row, coords, tiles, features),
        [
            pltpu.SMEM(coords.shape, jnp.int32),
            pltpu.SemaphoreType.DMA,
            pltpu.SemaphoreType.DMA((2,)),
        ],
        limit,
    )


def products(near_ref, far_ref, *refs):
    count = len(refs) // 3
    chunk_refs, away_refs = refs[:count], refs[count : 2 * count - 1]
    kept_refs, all_ref = refs[2 * count - 1 : -1], refs[-1]
    width = chunk_refs[0].shape[1]
    for i, chunk in enumerate(chunk_refs):
        all_ref[:, i * width : (i + 1) * width] = chunk[...]
    half_rows = near_ref.shape[0]
    step = math.gcd(half_rows, 256)
    for row in range(0, half_rows, step):
        rows = pl.ds(row, step)
        away = jnp.dot(far_ref[rows, :], all_ref[:, width:], preferred_element_type=F32)
        for i, out in enumerate(away_refs):
            out[rows, :] = away[:, i * width : (i + 1) * width].astype(out.dtype)
    for row in range(0, half_rows, step):
        rows = pl.ds(row, step)
        kept = jnp.dot(near_ref[rows, :], all_ref[...], preferred_element_type=F32)
        for i, out in enumerate(kept_refs):
            out[rows, :] = kept[:, i * width : (i + 1) * width]


def all_products(near, far, features, limit):
    half_rows, block_c = near.shape
    width = features[0].shape[1]
    count = len(features)
    away = jax.ShapeDtypeStruct((half_rows, width), BF16)
    kept = jax.ShapeDtypeStruct((half_rows, width), F32)
    outs = call(
        products,
        [away] * (count - 1) + [kept] * count,
        [VMEM] * (2 + count),
        (near, far, *features),
        [pltpu.VMEM((block_c, count * width), BF16)],
        limit,
    )
    return outs[: count - 1], outs[count - 1 :]


def both_products(near_ref, far_ref, chunk_ref, keep_ref, send_ref):
    half_rows = near_ref.shape[0]
    step = math.gcd(half_rows // 2, 256)
    for block, ref in ((1, far_ref), (0, near_ref)):
        for row in range(0, half_rows, step):
            values = jnp.dot(ref[pl.ds(row, step), :], chunk_ref[...], preferred_element_type=F32)
            if row < half_rows // 2:
                keep_ref[block, pl.ds(row, step), :] = values
            else:
                rows = pl.ds(row - half_rows // 2, step)
                send_ref[block, rows, :] = values.astype(send_ref.dtype)


def last_products(near, far, chunk, limit, before):
    shape = (2, near.shape[0] // 2, chunk.shape[1])
    return call(
        both_products,
        (jax.ShapeDtypeStruct(shape, F32), jax.ShapeDtypeStruct(shape, BF16)),
        [VMEM] * 3,
        (near, far, chunk),
        (),
        limit,
        before=before,
    )


def add_and_halve(kept_ref, came_ref, keep_ref, send_ref):
    rows = keep_ref.shape[0]
    keep_ref[...] = kept_ref[:rows, :] + came_ref[:rows, :].astype(F32)
    send_ref[...] = (kept_ref[rows:, :] + came_ref[rows:, :].astype(F32)).astype(send_ref.dtype)


def halved(kept, came, before, cost=0):
    shape = (kept.shape[0] // 2, kept.shape[1])
    return call(
        add_and_halve,
        (jax.ShapeDtypeStruct(shape, F32), jax.ShapeDtypeStruct(shape, BF16)),
        [VMEM] * 2,
        (kept, came),
        before=before,
        cost=cost,
    )


def add_and_part(kept_ref, came_ref, keep_ref, *send_refs):
    rows = keep_ref.shape[0]
    keep_ref[...] = kept_ref[:rows, :] + came_ref[:rows, :].astype(F32)
    for i, out in enumerate(send_refs):
        part = pl.ds((i + 1) * rows, rows)
        out[...] = (kept_ref[part, :] + came_ref[part, :].astype(F32)).astype(out.dtype)


def parted(kept, came, count, before):
    shape = (kept.shape[0] // count, kept.shape[1])
    outs = call(
        add_and_part,
        [jax.ShapeDtypeStruct(shape, F32)] + [jax.ShapeDtypeStruct(shape, BF16)] * (count - 1),
        [VMEM] * 2,
        (kept, came),
        before=before,
    )
    return outs[0], outs[1:]


def add_pair(kept_ref, came_ref, keep_ref, send_ref):
    keep_ref[...] = kept_ref[0] + came_ref[0].astype(F32)
    send_ref[...] = (kept_ref[1] + came_ref[1].astype(F32)).astype(send_ref.dtype)


def join_two(first_ref, second_ref, out_ref):
    out_ref[pl.ds(0, first_ref.shape[0])] = first_ref[...]
    out_ref[pl.ds(first_ref.shape[0], first_ref.shape[0])] = second_ref[...]


def joined(first, second, before, cost=0):
    shape = (2 * first.shape[0],) + first.shape[1:]
    return call(
        join_two,
        jax.ShapeDtypeStruct(shape, first.dtype),
        [VMEM] * 2,
        (first, second),
        before=before,
        cost=cost,
    )


def join_and_part(first_ref, second_ref, *out_refs):
    count = first_ref.shape[0]
    at = 0
    for out in out_refs:
        rows = pl.ds(at, out.shape[1])
        at += out.shape[1]
        for k in range(count):
            out[k] = first_ref[k, rows, :]
            out[count + k] = second_ref[k, rows, :]


def joined_parts(first, second, heights, before):
    count, _, shard_rows = first.shape
    shapes = [jax.ShapeDtypeStruct((2 * count, height, shard_rows), first.dtype) for height in heights]
    return call(join_and_part, shapes, [VMEM] * 2, (first, second), before=before)


def mark(out_ref):
    out_ref[...] = jnp.zeros_like(out_ref)


def marked(*before, cost=0):
    return call(mark, jax.ShapeDtypeStruct((8, 128), F32), [], (), before=before, cost=cost)


def order_rows(owners, me_ref, weight_ref, out_ref):
    part = weight_ref.shape[0] // len(owners)
    for i, rels in enumerate(owners):
        piece = part // len(rels)
        for j, rel in enumerate(rels):
            source = pl.ds(pl.multiple_of((me_ref[0] ^ rel) * piece, piece), piece)
            out_ref[pl.ds(i * part + j * piece, piece), :] = weight_ref[source, :]


def dense_layer(counts, out_groups, *refs):
    total_refs, refs = refs[: sum(counts)], refs[sum(counts) :]
    rows_ref, cotangent_ref, hidden_ref, agg_ref, grad_pre_ref = refs[:5]
    grad_refs = refs[5:]
    part = rows_ref.shape[0] // len(counts)
    at = 0
    for i, count in enumerate(counts):
        total = total_refs[at][...]
        for ref in total_refs[at + 1 : at + count]:
            total = total + ref[...].astype(F32)
        agg_ref[:, i * part : (i + 1) * part] = total.astype(agg_ref.dtype)
        at += count
    pre_act = jnp.dot(agg_ref[...], rows_ref[...], preferred_element_type=F32)
    slope = jnp.exp(jnp.minimum(pre_act, 0.0))
    positive = pre_act > 0
    hidden_ref[...] = jnp.where(positive, pre_act, slope - 1.0).astype(hidden_ref.dtype)
    slope = jnp.where(positive, F32(1.0), slope)
    grad_pre = (cotangent_ref[...].astype(F32) * slope).astype(grad_pre_ref.dtype)
    grad_pre_ref[...] = grad_pre
    for members, out in zip(out_groups, grad_refs):
        for j, i in enumerate(members):
            out[0, pl.ds(j * part, part), :] = lax.dot_general(
                rows_ref[pl.ds(i * part, part), :],
                grad_pre,
                (((1,), (1,)), ((), ())),
                preferred_element_type=F32,
            ).astype(out.dtype)


def layer(totals, out_groups, weight_rows, cotangent, before):
    shard_rows, width = cotangent.shape
    part = width // len(totals)
    whole = jax.ShapeDtypeStruct((shard_rows, width), BF16)
    grads = [jax.ShapeDtypeStruct((1, len(m) * part, shard_rows), BF16) for m in out_groups]
    counts = [len(terms) for terms in totals]
    outs = call(
        functools.partial(dense_layer, counts, out_groups),
        [whole] * 3 + grads,
        [VMEM] * (sum(counts) + 2),
        (*[term for terms in totals for term in terms], weight_rows, cotangent),
        before=before,
    )
    return outs[0], outs[1], outs[2], outs[3:]


def back_products(count, near_ref, far_ref, *refs):
    rows_refs, out_refs, (left_ref, right_ref) = refs[:count], refs[count:-2], refs[-2:]
    shard_rows = rows_refs[0].shape[2]
    for k in range(left_ref.shape[1] // shard_rows):
        cols = pl.ds(k * shard_rows, shard_rows)
        if count == 2:
            left_ref[:, cols] = rows_refs[0][k]
            right_ref[:, cols] = rows_refs[1][k]
        else:
            place = k // 2 * 4 + k % 2
            left_ref[:, cols] = rows_refs[0][place]
            right_ref[:, cols] = rows_refs[0][place + 2]
    block_c = near_ref.shape[1]
    step = math.gcd(block_c, 256)
    part = out_refs[0].shape[0]
    for col in range(0, block_c, step):
        cols = pl.ds(col, step)
        total = jnp.dot(left_ref[...], near_ref[:, cols], preferred_element_type=F32)
        total = total + jnp.dot(right_ref[...], far_ref[:, cols], preferred_element_type=F32)
        for i, out in enumerate(out_refs):
            out[:, cols] = total[i * part : (i + 1) * part, :].astype(out.dtype)


def back_of(near, far, rows, dtypes, limit, before, cost=0):
    height = rows[0].shape[1]
    shape = (height // len(dtypes), near.shape[1])
    return call(
        functools.partial(back_products, len(rows)),
        [jax.ShapeDtypeStruct(shape, dtype) for dtype in dtypes],
        [VMEM] * (2 + len(rows)),
        (near, far, *rows),
        [pltpu.VMEM((height, near.shape[0]), BF16)] * 2,
        limit,
        before=before,
        cost=cost,
    )


def add_parts(places, own_ref, came_ref, *out_refs):
    piece = out_refs[0].shape[0]
    for place, out in zip(places, out_refs):
        rows = pl.ds(place * piece, piece)
        out[...] = (own_ref[rows, :] + came_ref[rows, :].astype(F32)).astype(out.dtype)


def parts_to_send(own, came, places, piece, before):
    shape = jax.ShapeDtypeStruct((piece, own.shape[1]), BF16)
    return call(
        functools.partial(add_parts, places),
        [shape] * len(places),
        [VMEM] * 2,
        (own, came),
        before=before,
    )


def finish(own_ref, came_ref, *refs):
    out_ref = refs[-1]
    piece = out_ref.shape[1]
    total = own_ref[:piece, :] + came_ref[:piece, :].astype(F32)
    for ref in refs[:-1]:
        total = total + ref[...].astype(F32)
    out_ref[...] = total.T.astype(out_ref.dtype)


def weight_terms(places, agg_ref, grad_pre_ref, *out_refs):
    width = agg_ref.shape[1]
    piece = width // sum(len(group) for group in places)
    for group, out in zip(places, out_refs):
        for i, place in enumerate(group):
            term = lax.dot_general(
                agg_ref[:, place * piece : (place + 1) * piece],
                grad_pre_ref[...],
                (((0,), (0,)), ((), ())),
                preferred_element_type=F32,
            )
            out[pl.ds(i * piece, piece), :] = term.astype(out.dtype)


def add_and_split(side_ref, kept_ref, came_ref, keep_ref, send_ref, total_ref):
    total_ref[...] = kept_ref[...] + came_ref[...]
    half = keep_ref.shape[1]
    side = side_ref[0] & 1
    for k in range(keep_ref.shape[0]):
        mine = pl.ds(pl.multiple_of((2 * k + side) * half, half), half)
        other = pl.ds(pl.multiple_of((2 * k + 1 - side) * half, half), half)
        keep_ref[k] = total_ref[mine, :]
        send_ref[k] = total_ref[other, :].astype(send_ref.dtype)


def add_and_spread(kept_ref, came_ref, keep_ref, *send_refs):
    keep_ref[...] = kept_ref[0] + came_ref[0].astype(F32)
    for k, out in enumerate(send_refs):
        out[...] = (kept_ref[k + 1] + came_ref[k + 1].astype(F32)).astype(out.dtype)


def add_all(*refs):
    terms = [ref[...].astype(F32) for ref in refs[:-1]]
    while len(terms) > 1:
        terms = [sum(terms[i + 1 : i + 2], terms[i]) for i in range(0, len(terms), 2)]
    refs[-1][...] = terms[0].astype(refs[-1].dtype)


def sum_of(terms, dtype, before, cost=0):
    return call(
        add_all,
        jax.ShapeDtypeStruct(terms[0].shape, dtype),
        [VMEM] * len(terms),
        tuple(terms),
        before=before,
        cost=cost,
    )


def stack_all(*refs):
    for i, ref in enumerate(refs[:-1]):
        refs[-1][i] = ref[...]


def place_shares(me_ref, side_ref, own_ref, other_ref, out_ref):
    half = own_ref.shape[2]
    for inner, ref in ((0, own_ref), (1, other_ref)):
        for turn in range(2):
            side = (side_ref[0] ^ turn) & 1
            for k in range(ref.shape[1]):
                place = (me_ref[0] ^ (2 * k + inner)) * 2 + side
                out_ref[pl.ds(pl.multiple_of(place * half, half), half), :] = ref[turn, k].astype(
                    out_ref.dtype
                )


def body(node_features, layer_weight, tile_values, tile_coords, tile_count, cotangent):
    n_row = lax.axis_size("row")
    n_col = lax.axis_size("col")
    ro, co = n_row // 2, n_col // 2
    my_row = lax.axis_index("row").astype(jnp.int32).reshape(1)
    my_col = lax.axis_index("col").astype(jnp.int32).reshape(1)
    shard_rows, width = cotangent.shape
    block_c, piece = node_features.shape
    limit = 12 + (4 * co * shard_rows * block_c) // MIB

    def swap(v, axis, bit):
        size = n_row if axis == "row" else n_col
        return lax.ppermute(v, axis, [(i, i ^ bit) for i in range(size)])

    halves = (range(0, ro // 2), range(ro // 2, ro))
    chunks = [(h, i) for h in range(2) for i in range(2)]
    owners = [[2 * k + i for k in halves[h]] for h, i in chunks]
    flat = [rel for rels in owners for rel in rels]

    features = []
    for rels in owners:
        parts = [swap(node_features, "row", rel) if rel else node_features for rel in rels]
        features.append(jnp.concatenate(parts, axis=1) if len(parts) > 1 else parts[0])
    near, far, own_features, first_away = dense_blocks(
        tile_values[0, 0],
        pltpu.with_memory_space_constraint(tile_coords[0, 0].T, pltpu.HBM),
        tile_count.reshape(-1),
        my_col,
        my_row,
        pltpu.with_memory_space_constraint(features[0], pltpu.HBM),
        co,
        shard_rows,
        max(limit, 48),
    )
    features[0] = own_features
    away, kept = all_products(near, far, features[:3], limit)
    last_keep, last_send = last_products(near, far, features[3], limit, (kept[0],))

    keeps = [*kept, last_keep]
    cames = [swap(v, "col", 1) for v in (first_away, *away)] + [swap(last_send, "col", 2)]
    stages = co.bit_length() - 1
    done = [0] * 4
    turns = [0, 1, 3, 0, 2, 1, 3, 2] if stages == 2 else [0, 1, 2, 3] * stages
    weight_rows = call(
        functools.partial(order_rows, owners),
        jax.ShapeDtypeStruct(layer_weight.shape, BF16),
        [SMEM, VMEM],
        (my_row, layer_weight),
        before=(last_keep,),
    )
    last = weight_rows
    for i in turns:
        before = [last]
        if stages == 2 and done[i] == 1 and i == 3:
            before.append(cames[0])
        if stages == 2 and done[i] == 1 and i == 2:
            before.append(cames[1])
        if i == 3 and done[3] == 0:
            shape = keeps[3].shape[1:]
            keeps[3], last = call(
                add_pair,
                (jax.ShapeDtypeStruct(shape, F32), jax.ShapeDtypeStruct(shape, BF16)),
                [VMEM] * 2,
                (keeps[3], cames[3]),
                before=before,
            )
            bit = 1
        else:
            cost = COST_F if i in (1, 2) and done[i] == 0 else 0
            keeps[i], last = halved(keeps[i], cames[i], before, cost)
            bit = 2 << done[i]
        done[i] += 1
        cames[i] = swap(last, "col", bit)
    totals = [[keep, came] for keep, came in zip(keeps, cames)]

    out_groups = ((3,), (2, 1, 0))
    hidden, agg, grad_pre, grads = layer(
        totals, out_groups, weight_rows, cotangent, (last,)
    )

    places = [[flat.index(2 * k + inner) for k in range(ro)] for inner in range(2)]
    term_shape = (width // 2, width)
    weight_kept, weight_send = call(
        functools.partial(weight_terms, places),
        (jax.ShapeDtypeStruct(term_shape, F32), jax.ShapeDtypeStruct(term_shape, F32)),
        [VMEM] * 2,
        (agg, grad_pre),
    )
    state = {"w": [weight_kept, swap(weight_send, "row", 1)], "last": weight_send}

    def order(*more):
        return [state["last"], *more]

    half_share = (ro, piece // 2, width)

    def weight_core():
        keep, send = call(
            add_and_split,
            (jax.ShapeDtypeStruct(half_share, F32), jax.ShapeDtypeStruct(half_share, BF16)),
            [SMEM, VMEM, VMEM],
            (my_col, *state["w"]),
            [pltpu.VMEM((ro * piece, width), F32)],
            before=order(),
        )
        state["last"] = send
        state["w"] = [keep, swap(send, "col", 1)]

    def weight_side():
        shape = half_share[1:]
        outs = call(
            add_and_spread,
            [jax.ShapeDtypeStruct(shape, F32)] + [jax.ShapeDtypeStruct(shape, BF16)] * (ro - 1),
            [VMEM] * 2,
            tuple(state["w"]),
            before=order(),
        )
        state["last"] = outs[0]
        state["w"] = [outs[0]] + [swap(v, "row", 2 * (k + 1)) for k, v in enumerate(outs[1:])]

    def weight_line():
        total = sum_of(state["w"], BF16, order())
        state["last"] = total
        state["w"] = [total] + [swap(total, "col", 2 * k) for k in range(1, co)]

    def weight_sum():
        total = sum_of(state["w"], BF16, order(), COST_W)
        state["last"] = total
        state["w"] = [total] + [swap(total, "row", 2 * k) for k in range(1, ro)]

    def weight_stack(axis):
        total = call(
            stack_all,
            jax.ShapeDtypeStruct((len(state["w"]),) + state["w"][0].shape, BF16),
            [VMEM] * len(state["w"]),
            tuple(state["w"]),
            before=order(),
        )
        state["last"] = total
        state["w"] = [total, swap(total, axis, 1)]

    top = n_col // 2
    rows = {"C": grads[0], "AM": grads[1]}
    came_rows = {name: swap(rows[name], "col", top) for name in rows}
    bits = {"C": top, "A": 2 * top, "M": top}
    backs = {}

    def part():
        height = grads[0].shape[1]
        heights = (height, 2 * height)
        outs = joined_parts(rows["AM"], came_rows["AM"], heights, order())
        state["last"] = outs[0]
        rows["A"], rows["M"] = outs
        came_rows["A"] = swap(rows["A"], "col", 1)
        came_rows["M"] = swap(rows["M"], "col", top // 2)
        bits["M"] = top // 2

    def join(name, cost=0):
        rows[name] = state["last"] = joined(rows[name], came_rows[name], order(), cost)
        bits[name] //= 2
        if name == "A" and bits[name] == top:
            bits[name] //= 2
        if not (name == "A" and bits[name] == 1):
            came_rows[name] = swap(rows[name], "col", bits[name])

    def back(members, pair, cost=0, more=()):
        dtypes = [BF16 if chunk[1] else F32 for chunk in members]
        outs = back_of(near, far, pair, dtypes, limit, order(*more), cost)
        state["last"] = outs[0]
        for chunk, out in zip(members, outs):
            backs[chunk] = swap(out, "row", 1) if chunk[1] else out

    arrived = []

    def send_parts(h):
        sent = [p for p, k in enumerate(halves[h]) if k > 0]
        if sent:
            parts = parts_to_send(backs[h, 0], backs[h, 1], sent, piece, order())
            state["last"] = parts[0]
            arrived.extend(swap(v, "row", 2 * halves[h][p]) for p, v in zip(sent, parts))

    weight_core()
    join("C")
    weight_side()
    for _ in range(stages - 1):
        join("C")
    part()
    weight_line()
    back([(1, 1)], (rows["C"], came_rows["C"]))
    for _ in range(stages - 1):
        join("M")
    for _ in range(stages - 1):
        join("A")
    weight_sum()
    weight_stack("col")
    join("A", COST_S)
    back([(1, 0)], (rows["A"],))
    send_parts(1)
    back([(0, 1), (0, 0)], (rows["M"], came_rows["M"]), COST_M)
    weight_stack("row")
    send_parts(0)
    state["last"] = marked(state["last"], *arrived, cost=COST)
    grad_features = call(
        finish,
        jax.ShapeDtypeStruct((block_c, piece), BF16),
        [VMEM] * (2 + len(arrived)),
        (backs[0, 0], backs[0, 1], *arrived),
        before=order(),
    )
    grad_weight = call(
        place_shares,
        jax.ShapeDtypeStruct((width, width), F32),
        [SMEM, SMEM, VMEM, VMEM],
        (my_row, my_col, *state["w"]),
    )
    return (hidden, grad_weight, grad_features)


def solution(mesh):
    in_specs = (
        P("col", "row"),
        P(),
        P("row", "col", None, None, None),
        P("row", "col", None, None),
        P("row", "col"),
        P(("row", "col"), None),
    )
    out_specs = (P(("row", "col"), None), P(), P("col", "row"))
    return jax.shard_map(body, mesh=mesh, in_specs=in_specs, out_specs=out_specs, check_vma=False)
```

```python
import functools
import math

import jax
import jax.numpy as jnp
from jax import lax
from jax.experimental import pallas as pl
from jax.experimental.pallas import tpu as pltpu
from jax.sharding import PartitionSpec as P

F32 = jnp.float32
BF16 = jnp.bfloat16
MIB = 1024 * 1024
COST_F = 1_000_000_000
COST, COST_S, COST_W, COST_M = 4_000_000_000, 1_000_000_000, 4_000_000_000, 4_000_000_000
SMEM = pl.BlockSpec(memory_space=pltpu.SMEM)
VMEM = pl.BlockSpec(memory_space=pltpu.VMEM)
ANYWHERE = pl.BlockSpec(memory_space=pl.ANY)


def call(kernel, out_shape, in_specs, operands, scratch=(), limit=16, before=(), cost=0):
    many = isinstance(out_shape, (tuple, list))
    count = len(operands)

    def run(*refs):
        kernel(*refs[:count], *refs[count + len(before) :])

    return pl.pallas_call(
        run,
        out_shape=tuple(out_shape) if many else out_shape,
        in_specs=list(in_specs) + [ANYWHERE] * len(before),
        out_specs=(VMEM,) * len(out_shape) if many else VMEM,
        scratch_shapes=list(scratch),
        compiler_params=pltpu.CompilerParams(vmem_limit_bytes=limit * MIB),
        cost_estimate=pl.CostEstimate(flops=cost, bytes_accessed=0, transcendentals=0),
    )(*operands, *before)


def place_tiles(
    outer,
    shard_tiles,
    count_ref,
    me_ref,
    row_ref,
    coords_hbm,
    tiles_ref,
    features_hbm,
    near_ref,
    far_ref,
    features_ref,
    away_ref,
    coords_ref,
    tile_sem,
    in_sems,
):
    slots, tile, _ = tiles_ref.shape
    coords_copy = pltpu.make_async_copy(coords_hbm, coords_ref, in_sems.at[0])
    features_copy = pltpu.make_async_copy(features_hbm, features_ref, in_sems.at[1])
    coords_copy.start()
    features_copy.start()
    me = me_ref[0]
    count = count_ref[0]
    near_ref[...] = jnp.zeros_like(near_ref)
    far_ref[...] = jnp.zeros_like(far_ref)
    coords_copy.wait()
    shift = shard_tiles.bit_length() - 1

    def start(t, carry):
        dest = coords_ref[0, t]
        rel = lax.shift_right_logical(dest, shift) ^ me
        place, bit = 0, 2
        while bit <= outer:
            moved = (outer // bit).bit_length() - bit.bit_length()
            taken = rel & bit
            place = place | (
                lax.shift_left(taken, moved) if moved >= 0 else lax.shift_right_logical(taken, -moved)
            )
            bit *= 2
        row = lax.shift_left(place, shift) | (dest & (shard_tiles - 1))
        rows = pl.ds(pl.multiple_of(row * tile, tile), tile)
        cols = pl.ds(pl.multiple_of(coords_ref[1, t] * tile, tile), tile)

        @pl.when((rel & 1) == 0)
        def _():
            pltpu.make_async_copy(tiles_ref.at[t], near_ref.at[rows, cols], tile_sem).start()

        @pl.when((rel & 1) != 0)
        def _():
            pltpu.make_async_copy(tiles_ref.at[t], far_ref.at[rows, cols], tile_sem).start()

        return carry

    lax.fori_loop(0, count, start, 0)
    some = 1
    while some <= slots:

        @pl.when((count & some) != 0)
        def _():
            part = tiles_ref.at[pl.ds(0, some)]
            pltpu.make_async_copy(part, part, tile_sem).wait()

        some *= 2
    features_copy.wait()
    step = math.gcd(far_ref.shape[0], 256)
    for row in range(0, far_ref.shape[0], step):
        rows = pl.ds(row, step)
        away = jnp.dot(far_ref[rows, :], features_ref[...], preferred_element_type=F32)
        away_ref[rows, :] = away.astype(away_ref.dtype)


def dense_blocks(tiles, coords, count, me, row, features, outer, shard_rows, limit):
    slots, tile, _ = tiles.shape
    block_c, width = features.shape
    half_rows = outer * shard_rows
    return call(
        functools.partial(place_tiles, outer, shard_rows // tile),
        (
            jax.ShapeDtypeStruct((half_rows, block_c), tiles.dtype),
            jax.ShapeDtypeStruct((half_rows, block_c), tiles.dtype),
            jax.ShapeDtypeStruct(features.shape, BF16),
            jax.ShapeDtypeStruct((half_rows, width), BF16),
        ),
        [SMEM, SMEM, SMEM, ANYWHERE, pl.BlockSpec(memory_space=pltpu.HBM), ANYWHERE],
        (count, me, row, coords, tiles, features),
        [
            pltpu.SMEM(coords.shape, jnp.int32),
            pltpu.SemaphoreType.DMA,
            pltpu.SemaphoreType.DMA((2,)),
        ],
        limit,
    )


def products(near_ref, far_ref, *refs):
    count = len(refs) // 3
    chunk_refs, away_refs = refs[:count], refs[count : 2 * count - 1]
    kept_refs, all_ref = refs[2 * count - 1 : -1], refs[-1]
    width = chunk_refs[0].shape[1]
    for i, chunk in enumerate(chunk_refs):
        all_ref[:, i * width : (i + 1) * width] = chunk[...]
    half_rows = near_ref.shape[0]
    step = math.gcd(half_rows, 256)
    for row in range(0, half_rows, step):
        rows = pl.ds(row, step)
        away = jnp.dot(far_ref[rows, :], all_ref[:, width:], preferred_element_type=F32)
        for i, out in enumerate(away_refs):
            out[rows, :] = away[:, i * width : (i + 1) * width].astype(out.dtype)
    for row in range(0, half_rows, step):
        rows = pl.ds(row, step)
        kept = jnp.dot(near_ref[rows, :], all_ref[...], preferred_element_type=F32)
        for i, out in enumerate(kept_refs):
            out[rows, :] = kept[:, i * width : (i + 1) * width]


def all_products(near, far, features, limit):
    half_rows, block_c = near.shape
    width = features[0].shape[1]
    count = len(features)
    away = jax.ShapeDtypeStruct((half_rows, width), BF16)
    kept = jax.ShapeDtypeStruct((half_rows, width), F32)
    outs = call(
        products,
        [away] * (count - 1) + [kept] * count,
        [VMEM] * (2 + count),
        (near, far, *features),
        [pltpu.VMEM((block_c, count * width), BF16)],
        limit,
    )
    return outs[: count - 1], outs[count - 1 :]


def one_product(near_ref, far_ref, chunk_ref, away_ref, kept_ref):
    half_rows = near_ref.shape[0]
    step = math.gcd(half_rows, 256)
    for ref, out in ((far_ref, away_ref), (near_ref, kept_ref)):
        for row in range(0, half_rows, step):
            rows = pl.ds(row, step)
            values = jnp.dot(ref[rows, :], chunk_ref[...], preferred_element_type=F32)
            out[rows, :] = values.astype(out.dtype)


def last_products(near, far, chunk, limit, before):
    shape = (near.shape[0], chunk.shape[1])
    return call(
        one_product,
        (jax.ShapeDtypeStruct(shape, BF16), jax.ShapeDtypeStruct(shape, F32)),
        [VMEM] * 3,
        (near, far, chunk),
        (),
        limit,
        before=before,
    )


def add_and_halve(kept_ref, came_ref, keep_ref, send_ref):
    rows = keep_ref.shape[0]
    keep_ref[...] = kept_ref[:rows, :] + came_ref[:rows, :].astype(F32)
    send_ref[...] = (kept_ref[rows:, :] + came_ref[rows:, :].astype(F32)).astype(send_ref.dtype)


def halved(kept, came, before, cost=0):
    shape = (kept.shape[0] // 2, kept.shape[1])
    return call(
        add_and_halve,
        (jax.ShapeDtypeStruct(shape, F32), jax.ShapeDtypeStruct(shape, BF16)),
        [VMEM] * 2,
        (kept, came),
        before=before,
        cost=cost,
    )


def add_and_part(kept_ref, came_ref, keep_ref, *send_refs):
    rows = keep_ref.shape[0]
    keep_ref[...] = kept_ref[:rows, :] + came_ref[:rows, :].astype(F32)
    for i, out in enumerate(send_refs):
        part = pl.ds((i + 1) * rows, rows)
        out[...] = (kept_ref[part, :] + came_ref[part, :].astype(F32)).astype(out.dtype)


def parted(kept, came, count, before):
    shape = (kept.shape[0] // count, kept.shape[1])
    outs = call(
        add_and_part,
        [jax.ShapeDtypeStruct(shape, F32)] + [jax.ShapeDtypeStruct(shape, BF16)] * (count - 1),
        [VMEM] * 2,
        (kept, came),
        before=before,
    )
    return outs[0], outs[1:]


def join_two(first_ref, second_ref, out_ref):
    out_ref[pl.ds(0, first_ref.shape[0])] = first_ref[...]
    out_ref[pl.ds(first_ref.shape[0], first_ref.shape[0])] = second_ref[...]


def joined(first, second, before, cost=0):
    shape = (2 * first.shape[0],) + first.shape[1:]
    return call(
        join_two,
        jax.ShapeDtypeStruct(shape, first.dtype),
        [VMEM] * 2,
        (first, second),
        before=before,
        cost=cost,
    )


def join_and_part(first_ref, second_ref, *out_refs):
    count = first_ref.shape[0]
    at = 0
    for out in out_refs:
        rows = pl.ds(at, out.shape[1])
        at += out.shape[1]
        for k in range(count):
            out[k] = first_ref[k, rows, :]
            out[count + k] = second_ref[k, rows, :]


def joined_parts(first, second, heights, before):
    count, _, shard_rows = first.shape
    shapes = [jax.ShapeDtypeStruct((2 * count, height, shard_rows), first.dtype) for height in heights]
    return call(join_and_part, shapes, [VMEM] * 2, (first, second), before=before)


def mark(out_ref):
    out_ref[...] = jnp.zeros_like(out_ref)


def marked(*before, cost=0):
    return call(mark, jax.ShapeDtypeStruct((8, 128), F32), [], (), before=before, cost=cost)


def order_rows(owners, me_ref, weight_ref, out_ref):
    part = weight_ref.shape[0] // len(owners)
    for i, rels in enumerate(owners):
        piece = part // len(rels)
        for j, rel in enumerate(rels):
            source = pl.ds(pl.multiple_of((me_ref[0] ^ rel) * piece, piece), piece)
            out_ref[pl.ds(i * part + j * piece, piece), :] = weight_ref[source, :]


def dense_layer(counts, out_groups, *refs):
    total_refs, refs = refs[: sum(counts)], refs[sum(counts) :]
    rows_ref, cotangent_ref, hidden_ref, agg_ref, grad_pre_ref = refs[:5]
    grad_refs = refs[5:]
    part = rows_ref.shape[0] // len(counts)
    at = 0
    for i, count in enumerate(counts):
        total = total_refs[at][...]
        for ref in total_refs[at + 1 : at + count]:
            total = total + ref[...].astype(F32)
        agg_ref[:, i * part : (i + 1) * part] = total.astype(agg_ref.dtype)
        at += count
    pre_act = jnp.dot(agg_ref[...], rows_ref[...], preferred_element_type=F32)
    slope = jnp.exp(jnp.minimum(pre_act, 0.0))
    positive = pre_act > 0
    hidden_ref[...] = jnp.where(positive, pre_act, slope - 1.0).astype(hidden_ref.dtype)
    slope = jnp.where(positive, F32(1.0), slope)
    grad_pre = (cotangent_ref[...].astype(F32) * slope).astype(grad_pre_ref.dtype)
    grad_pre_ref[...] = grad_pre
    for members, out in zip(out_groups, grad_refs):
        for j, i in enumerate(members):
            out[0, pl.ds(j * part, part), :] = lax.dot_general(
                rows_ref[pl.ds(i * part, part), :],
                grad_pre,
                (((1,), (1,)), ((), ())),
                preferred_element_type=F32,
            ).astype(out.dtype)


def layer(totals, out_groups, weight_rows, cotangent, before):
    shard_rows, width = cotangent.shape
    part = width // len(totals)
    whole = jax.ShapeDtypeStruct((shard_rows, width), BF16)
    grads = [jax.ShapeDtypeStruct((1, len(m) * part, shard_rows), BF16) for m in out_groups]
    counts = [len(terms) for terms in totals]
    outs = call(
        functools.partial(dense_layer, counts, out_groups),
        [whole] * 3 + grads,
        [VMEM] * (sum(counts) + 2),
        (*[term for terms in totals for term in terms], weight_rows, cotangent),
        before=before,
    )
    return outs[0], outs[1], outs[2], outs[3:]


def back_products(count, near_ref, far_ref, *refs):
    rows_refs, out_refs, (left_ref, right_ref) = refs[:count], refs[count:-2], refs[-2:]
    shard_rows = rows_refs[0].shape[2]
    for k in range(left_ref.shape[1] // shard_rows):
        cols = pl.ds(k * shard_rows, shard_rows)
        if count == 2:
            left_ref[:, cols] = rows_refs[0][k]
            right_ref[:, cols] = rows_refs[1][k]
        else:
            left_ref[:, cols] = rows_refs[0][2 * k]
            right_ref[:, cols] = rows_refs[0][2 * k + 1]
    block_c = near_ref.shape[1]
    step = math.gcd(block_c, 256)
    part = out_refs[0].shape[0]
    for col in range(0, block_c, step):
        cols = pl.ds(col, step)
        total = jnp.dot(left_ref[...], near_ref[:, cols], preferred_element_type=F32)
        total = total + jnp.dot(right_ref[...], far_ref[:, cols], preferred_element_type=F32)
        for i, out in enumerate(out_refs):
            out[:, cols] = total[i * part : (i + 1) * part, :].astype(out.dtype)


def back_of(near, far, rows, dtypes, limit, before, cost=0):
    height = rows[0].shape[1]
    shape = (height // len(dtypes), near.shape[1])
    return call(
        functools.partial(back_products, len(rows)),
        [jax.ShapeDtypeStruct(shape, dtype) for dtype in dtypes],
        [VMEM] * (2 + len(rows)),
        (near, far, *rows),
        [pltpu.VMEM((height, near.shape[0]), BF16)] * 2,
        limit,
        before=before,
        cost=cost,
    )


def add_parts(places, own_ref, came_ref, *out_refs):
    piece = out_refs[0].shape[0]
    for place, out in zip(places, out_refs):
        rows = pl.ds(place * piece, piece)
        out[...] = (own_ref[rows, :] + came_ref[rows, :].astype(F32)).astype(out.dtype)


def parts_to_send(own, came, places, piece, before):
    shape = jax.ShapeDtypeStruct((piece, own.shape[1]), BF16)
    return call(
        functools.partial(add_parts, places),
        [shape] * len(places),
        [VMEM] * 2,
        (own, came),
        before=before,
    )


def finish(own_ref, came_ref, *refs):
    out_ref = refs[-1]
    piece = out_ref.shape[1]
    total = own_ref[:piece, :] + came_ref[:piece, :].astype(F32)
    for ref in refs[:-1]:
        total = total + ref[...].astype(F32)
    out_ref[...] = total.T.astype(out_ref.dtype)


def weight_terms(places, agg_ref, grad_pre_ref, *out_refs):
    width = agg_ref.shape[1]
    piece = width // sum(len(group) for group in places)
    for group, out in zip(places, out_refs):
        for i, place in enumerate(group):
            term = lax.dot_general(
                agg_ref[:, place * piece : (place + 1) * piece],
                grad_pre_ref[...],
                (((0,), (0,)), ((), ())),
                preferred_element_type=F32,
            )
            out[pl.ds(i * piece, piece), :] = term.astype(out.dtype)


def add_and_split(side_ref, kept_ref, came_ref, keep_ref, send_ref, total_ref):
    total_ref[...] = kept_ref[...] + came_ref[...]
    half = keep_ref.shape[1]
    side = side_ref[0] & 1
    for k in range(keep_ref.shape[0]):
        mine = pl.ds(pl.multiple_of((2 * k + side) * half, half), half)
        other = pl.ds(pl.multiple_of((2 * k + 1 - side) * half, half), half)
        keep_ref[k] = total_ref[mine, :]
        send_ref[k] = total_ref[other, :].astype(send_ref.dtype)


def add_and_spread(kept_ref, came_ref, keep_ref, *send_refs):
    keep_ref[...] = kept_ref[0] + came_ref[0].astype(F32)
    for k, out in enumerate(send_refs):
        out[...] = (kept_ref[k + 1] + came_ref[k + 1].astype(F32)).astype(out.dtype)


def add_all(*refs):
    terms = [ref[...].astype(F32) for ref in refs[:-1]]
    while len(terms) > 1:
        terms = [sum(terms[i + 1 : i + 2], terms[i]) for i in range(0, len(terms), 2)]
    refs[-1][...] = terms[0].astype(refs[-1].dtype)


def sum_of(terms, dtype, before, cost=0):
    return call(
        add_all,
        jax.ShapeDtypeStruct(terms[0].shape, dtype),
        [VMEM] * len(terms),
        tuple(terms),
        before=before,
        cost=cost,
    )


def stack_all(*refs):
    for i, ref in enumerate(refs[:-1]):
        refs[-1][i] = ref[...]


def place_shares(me_ref, side_ref, own_ref, other_ref, out_ref):
    half = own_ref.shape[2]
    for inner, ref in ((0, own_ref), (1, other_ref)):
        for turn in range(2):
            side = (side_ref[0] ^ turn) & 1
            for k in range(ref.shape[1]):
                place = (me_ref[0] ^ (2 * k + inner)) * 2 + side
                out_ref[pl.ds(pl.multiple_of(place * half, half), half), :] = ref[turn, k].astype(
                    out_ref.dtype
                )


def body(node_features, layer_weight, tile_values, tile_coords, tile_count, cotangent):
    n_row = lax.axis_size("row")
    n_col = lax.axis_size("col")
    ro, co = n_row // 2, n_col // 2
    my_row = lax.axis_index("row").astype(jnp.int32).reshape(1)
    my_col = lax.axis_index("col").astype(jnp.int32).reshape(1)
    shard_rows, width = cotangent.shape
    block_c, piece = node_features.shape
    limit = 12 + (4 * co * shard_rows * block_c) // MIB

    def swap(v, axis, bit):
        size = n_row if axis == "row" else n_col
        return lax.ppermute(v, axis, [(i, i ^ bit) for i in range(size)])

    halves = (range(0, ro // 2), range(ro // 2, ro))
    chunks = [(h, i) for h in range(2) for i in range(2)]
    owners = [[2 * k + i for k in halves[h]] for h, i in chunks]
    flat = [rel for rels in owners for rel in rels]

    features = []
    for rels in owners:
        parts = [swap(node_features, "row", rel) if rel else node_features for rel in rels]
        features.append(jnp.concatenate(parts, axis=1) if len(parts) > 1 else parts[0])
    near, far, own_features, first_away = dense_blocks(
        tile_values[0, 0],
        pltpu.with_memory_space_constraint(tile_coords[0, 0].T, pltpu.HBM),
        tile_count.reshape(-1),
        my_col,
        my_row,
        pltpu.with_memory_space_constraint(features[0], pltpu.HBM),
        co,
        shard_rows,
        max(limit, 48),
    )
    features[0] = own_features
    away, kept = all_products(near, far, features[:3], limit)
    keeps = [*kept, None]
    cames = [swap(v, "col", 1) for v in (first_away, *away)] + [None]
    stages = co.bit_length() - 1
    done = [0] * 4
    turns = [0, 1, 0, 2, 1, 3, 2, 3] if stages == 2 else [0, 1, 2, 3] * stages
    weight_rows = call(
        functools.partial(order_rows, owners),
        jax.ShapeDtypeStruct(layer_weight.shape, BF16),
        [SMEM, VMEM],
        (my_row, layer_weight),
        before=(kept[0],),
    )
    last = weight_rows
    for turn, i in enumerate(turns):
        before = [last]
        if stages == 2 and turn == 5:
            before.append(cames[0])
        if stages == 2 and turn == 7:
            before.append(cames[1])
        cost = COST_F if i in (1, 2) and done[i] == 0 else 0
        keeps[i], last = halved(keeps[i], cames[i], before, cost)
        cames[i] = swap(last, "col", 2 << done[i])
        done[i] += 1
        if turn == 0:
            last_away, keeps[3] = last_products(near, far, features[3], limit, (last,))
            cames[3] = swap(last_away, "col", 1)
            last = keeps[3]
    totals = [[keep, came] for keep, came in zip(keeps, cames)]

    out_groups = ((3,), (2,), (1, 0))
    hidden, agg, grad_pre, grads = layer(
        totals, out_groups, weight_rows, cotangent, (last,)
    )

    places = [[flat.index(2 * k + inner) for k in range(ro)] for inner in range(2)]
    term_shape = (width // 2, width)
    weight_kept, weight_send = call(
        functools.partial(weight_terms, places),
        (jax.ShapeDtypeStruct(term_shape, F32), jax.ShapeDtypeStruct(term_shape, F32)),
        [VMEM] * 2,
        (agg, grad_pre),
    )
    state = {"w": [weight_kept, swap(weight_send, "row", 1)], "last": weight_send}

    def order(*more):
        return [state["last"], *more]

    half_share = (ro, piece // 2, width)

    def weight_core():
        keep, send = call(
            add_and_split,
            (jax.ShapeDtypeStruct(half_share, F32), jax.ShapeDtypeStruct(half_share, BF16)),
            [SMEM, VMEM, VMEM],
            (my_col, *state["w"]),
            [pltpu.VMEM((ro * piece, width), F32)],
            before=order(),
        )
        state["last"] = send
        state["w"] = [keep, swap(send, "col", 1)]

    def weight_side():
        shape = half_share[1:]
        outs = call(
            add_and_spread,
            [jax.ShapeDtypeStruct(shape, F32)] + [jax.ShapeDtypeStruct(shape, BF16)] * (ro - 1),
            [VMEM] * 2,
            tuple(state["w"]),
            before=order(),
        )
        state["last"] = outs[0]
        state["w"] = [outs[0]] + [swap(v, "row", 2 * (k + 1)) for k, v in enumerate(outs[1:])]
        state["bit"] = n_col // 2

    def weight_line():
        bit = state["bit"]
        total = sum_of(state["w"], BF16 if bit > 2 else F32, order())
        state["last"] = total
        state["w"] = [total, swap(total, "col", bit)]
        state["bit"] = bit // 2

    def weight_sum():
        total = sum_of(state["w"], BF16, order(), COST_W)
        state["last"] = total
        state["w"] = [total] + [swap(total, "row", 2 * k) for k in range(1, ro)]

    def weight_stack(axis):
        total = call(
            stack_all,
            jax.ShapeDtypeStruct((len(state["w"]),) + state["w"][0].shape, BF16),
            [VMEM] * len(state["w"]),
            tuple(state["w"]),
            before=order(),
        )
        state["last"] = total
        state["w"] = [total, swap(total, axis, 1)]

    rows = {"C": grads[0], "A": grads[1], "M": grads[2]}
    bits = {"C": n_col // 2, "A": 1, "M": n_col // 2}
    came_rows = {name: swap(rows[name], "col", bits[name]) for name in rows}
    backs = {}

    def join(name, cost=0):
        first, second = rows[name], came_rows[name]
        bit = n_col // 2 if name == "A" and bits[name] == 1 else bits[name] // 2
        bits[name] = bit
        rows[name] = state["last"] = joined(first, second, order(), cost)
        if not (name == "A" and bit == 1):
            came_rows[name] = swap(rows[name], "col", bit)

    def back(members, pair, cost=0, more=()):
        dtypes = [BF16 if chunk[1] else F32 for chunk in members]
        outs = back_of(near, far, pair, dtypes, limit, order(*more), cost)
        state["last"] = outs[0]
        for chunk, out in zip(members, outs):
            backs[chunk] = swap(out, "row", 1) if chunk[1] else out

    arrived = []

    def send_parts(h):
        sent = [p for p, k in enumerate(halves[h]) if k > 0]
        if sent:
            parts = parts_to_send(backs[h, 0], backs[h, 1], sent, piece, order())
            state["last"] = parts[0]
            arrived.extend(swap(v, "row", 2 * halves[h][p]) for p, v in zip(sent, parts))

    weight_core()
    join("A")
    join("C")
    weight_side()
    join("M")
    for _ in range(stages - 1):
        join("C")
    weight_line()
    for _ in range(stages - 1):
        join("A", COST)
    for _ in range(stages - 1):
        weight_line()
    back([(1, 1)], (rows["C"], came_rows["C"]))
    for _ in range(stages - 1):
        join("M")
    weight_sum()
    weight_stack("col")
    join("A", COST_S)
    back([(1, 0)], (rows["A"],))
    send_parts(1)
    back([(0, 1), (0, 0)], (rows["M"], came_rows["M"]), COST_M)
    weight_stack("row")
    send_parts(0)
    state["last"] = marked(state["last"], *arrived, cost=COST)
    grad_features = call(
        finish,
        jax.ShapeDtypeStruct((block_c, piece), BF16),
        [VMEM] * (2 + len(arrived)),
        (backs[0, 0], backs[0, 1], *arrived),
        before=order(),
    )
    grad_weight = call(
        place_shares,
        jax.ShapeDtypeStruct((width, width), F32),
        [SMEM, SMEM, VMEM, VMEM],
        (my_row, my_col, *state["w"]),
    )
    return (hidden, grad_weight, grad_features)


def solution(mesh):
    in_specs = (
        P("col", "row"),
        P(),
        P("row", "col", None, None, None),
        P("row", "col", None, None),
        P("row", "col"),
        P(("row", "col"), None),
    )
    out_specs = (P(("row", "col"), None), P(), P("col", "row"))
    return jax.shard_map(body, mesh=mesh, in_specs=in_specs, out_specs=out_specs, check_vma=False)
```

```python
import functools
import math

import jax
import jax.numpy as jnp
from jax import lax
from jax.experimental import pallas as pl
from jax.experimental.pallas import tpu as pltpu
from jax.sharding import PartitionSpec as P

F32 = jnp.float32
BF16 = jnp.bfloat16
MIB = 1024 * 1024
COST_F = 1_000_000_000
COST, COST_S, COST_W, COST_M = 4_000_000_000, 3_000_000_000, 0, 8_000_000_000
SMEM = pl.BlockSpec(memory_space=pltpu.SMEM)
VMEM = pl.BlockSpec(memory_space=pltpu.VMEM)
ANYWHERE = pl.BlockSpec(memory_space=pl.ANY)


def call(kernel, out_shape, in_specs, operands, scratch=(), limit=16, before=(), cost=0):
    many = isinstance(out_shape, (tuple, list))
    count = len(operands)

    def run(*refs):
        kernel(*refs[:count], *refs[count + len(before) :])

    return pl.pallas_call(
        run,
        out_shape=tuple(out_shape) if many else out_shape,
        in_specs=list(in_specs) + [ANYWHERE] * len(before),
        out_specs=(VMEM,) * len(out_shape) if many else VMEM,
        scratch_shapes=list(scratch),
        compiler_params=pltpu.CompilerParams(vmem_limit_bytes=limit * MIB),
        cost_estimate=pl.CostEstimate(flops=cost, bytes_accessed=0, transcendentals=0),
    )(*operands, *before)


def place_tiles(
    outer,
    shard_tiles,
    count_ref,
    me_ref,
    row_ref,
    coords_hbm,
    tiles_ref,
    features_hbm,
    near_ref,
    far_ref,
    features_ref,
    away_ref,
    coords_ref,
    tile_sem,
    in_sems,
):
    slots, tile, _ = tiles_ref.shape
    coords_copy = pltpu.make_async_copy(coords_hbm, coords_ref, in_sems.at[0])
    features_copy = pltpu.make_async_copy(features_hbm, features_ref, in_sems.at[1])
    coords_copy.start()
    features_copy.start()
    me = me_ref[0]
    count = count_ref[0]
    near_ref[...] = jnp.zeros_like(near_ref)
    far_ref[...] = jnp.zeros_like(far_ref)
    coords_copy.wait()
    shift = shard_tiles.bit_length() - 1

    def start(t, carry):
        dest = coords_ref[0, t]
        rel = lax.shift_right_logical(dest, shift) ^ me
        place, bit = 0, 2
        while bit <= outer:
            moved = (outer // bit).bit_length() - bit.bit_length()
            taken = rel & bit
            place = place | (
                lax.shift_left(taken, moved) if moved >= 0 else lax.shift_right_logical(taken, -moved)
            )
            bit *= 2
        row = lax.shift_left(place, shift) | (dest & (shard_tiles - 1))
        rows = pl.ds(pl.multiple_of(row * tile, tile), tile)
        cols = pl.ds(pl.multiple_of(coords_ref[1, t] * tile, tile), tile)

        @pl.when((rel & 1) == 0)
        def _():
            pltpu.make_async_copy(tiles_ref.at[t], near_ref.at[rows, cols], tile_sem).start()

        @pl.when((rel & 1) != 0)
        def _():
            pltpu.make_async_copy(tiles_ref.at[t], far_ref.at[rows, cols], tile_sem).start()

        return carry

    lax.fori_loop(0, count, start, 0)
    some = 1
    while some <= slots:

        @pl.when((count & some) != 0)
        def _():
            part = tiles_ref.at[pl.ds(0, some)]
            pltpu.make_async_copy(part, part, tile_sem).wait()

        some *= 2
    features_copy.wait()
    step = math.gcd(far_ref.shape[0], 256)
    for row in range(0, far_ref.shape[0], step):
        rows = pl.ds(row, step)
        away = jnp.dot(far_ref[rows, :], features_ref[...], preferred_element_type=F32)
        away_ref[rows, :] = away.astype(away_ref.dtype)


def dense_blocks(tiles, coords, count, me, row, features, outer, shard_rows, limit):
    slots, tile, _ = tiles.shape
    block_c, width = features.shape
    half_rows = outer * shard_rows
    return call(
        functools.partial(place_tiles, outer, shard_rows // tile),
        (
            jax.ShapeDtypeStruct((half_rows, block_c), tiles.dtype),
            jax.ShapeDtypeStruct((half_rows, block_c), tiles.dtype),
            jax.ShapeDtypeStruct(features.shape, BF16),
            jax.ShapeDtypeStruct((half_rows, width), BF16),
        ),
        [SMEM, SMEM, SMEM, ANYWHERE, pl.BlockSpec(memory_space=pltpu.HBM), ANYWHERE],
        (count, me, row, coords, tiles, features),
        [
            pltpu.SMEM(coords.shape, jnp.int32),
            pltpu.SemaphoreType.DMA,
            pltpu.SemaphoreType.DMA((2,)),
        ],
        limit,
    )


def products(near_ref, far_ref, *refs):
    count = len(refs) // 3
    chunk_refs, away_refs = refs[:count], refs[count : 2 * count - 1]
    kept_refs, all_ref = refs[2 * count - 1 : -1], refs[-1]
    width = chunk_refs[0].shape[1]
    for i, chunk in enumerate(chunk_refs):
        all_ref[:, i * width : (i + 1) * width] = chunk[...]
    half_rows = near_ref.shape[0]
    step = math.gcd(half_rows, 256)
    for row in range(0, half_rows, step):
        rows = pl.ds(row, step)
        away = jnp.dot(far_ref[rows, :], all_ref[:, width:], preferred_element_type=F32)
        for i, out in enumerate(away_refs):
            out[rows, :] = away[:, i * width : (i + 1) * width].astype(out.dtype)
    for row in range(0, half_rows, step):
        rows = pl.ds(row, step)
        kept = jnp.dot(near_ref[rows, :], all_ref[...], preferred_element_type=F32)
        for i, out in enumerate(kept_refs):
            out[rows, :] = kept[:, i * width : (i + 1) * width]


def all_products(near, far, features, limit):
    half_rows, block_c = near.shape
    width = features[0].shape[1]
    count = len(features)
    away = jax.ShapeDtypeStruct((half_rows, width), BF16)
    kept = jax.ShapeDtypeStruct((half_rows, width), F32)
    outs = call(
        products,
        [away] * (count - 1) + [kept] * count,
        [VMEM] * (2 + count),
        (near, far, *features),
        [pltpu.VMEM((block_c, count * width), BF16)],
        limit,
    )
    return outs[: count - 1], outs[count - 1 :]


def one_product(near_ref, far_ref, chunk_ref, away_ref, kept_ref):
    half_rows = near_ref.shape[0]
    step = math.gcd(half_rows, 256)
    for ref, out in ((far_ref, away_ref), (near_ref, kept_ref)):
        for row in range(0, half_rows, step):
            rows = pl.ds(row, step)
            values = jnp.dot(ref[rows, :], chunk_ref[...], preferred_element_type=F32)
            out[rows, :] = values.astype(out.dtype)


def last_products(near, far, chunk, limit, before):
    shape = (near.shape[0], chunk.shape[1])
    return call(
        one_product,
        (jax.ShapeDtypeStruct(shape, BF16), jax.ShapeDtypeStruct(shape, F32)),
        [VMEM] * 3,
        (near, far, chunk),
        (),
        limit,
        before=before,
    )


def add_and_halve(kept_ref, came_ref, keep_ref, send_ref):
    rows = keep_ref.shape[0]
    keep_ref[...] = kept_ref[:rows, :] + came_ref[:rows, :].astype(F32)
    send_ref[...] = (kept_ref[rows:, :] + came_ref[rows:, :].astype(F32)).astype(send_ref.dtype)


def halved(kept, came, before, cost=0):
    shape = (kept.shape[0] // 2, kept.shape[1])
    return call(
        add_and_halve,
        (jax.ShapeDtypeStruct(shape, F32), jax.ShapeDtypeStruct(shape, BF16)),
        [VMEM] * 2,
        (kept, came),
        before=before,
        cost=cost,
    )


def add_and_part(kept_ref, came_ref, keep_ref, *send_refs):
    rows = keep_ref.shape[0]
    keep_ref[...] = kept_ref[:rows, :] + came_ref[:rows, :].astype(F32)
    for i, out in enumerate(send_refs):
        part = pl.ds((i + 1) * rows, rows)
        out[...] = (kept_ref[part, :] + came_ref[part, :].astype(F32)).astype(out.dtype)


def parted(kept, came, count, before):
    shape = (kept.shape[0] // count, kept.shape[1])
    outs = call(
        add_and_part,
        [jax.ShapeDtypeStruct(shape, F32)] + [jax.ShapeDtypeStruct(shape, BF16)] * (count - 1),
        [VMEM] * 2,
        (kept, came),
        before=before,
    )
    return outs[0], outs[1:]


def join_two(first_ref, second_ref, out_ref):
    out_ref[pl.ds(0, first_ref.shape[0])] = first_ref[...]
    out_ref[pl.ds(first_ref.shape[0], first_ref.shape[0])] = second_ref[...]


def joined(first, second, before, cost=0):
    shape = (2 * first.shape[0],) + first.shape[1:]
    return call(
        join_two,
        jax.ShapeDtypeStruct(shape, first.dtype),
        [VMEM] * 2,
        (first, second),
        before=before,
        cost=cost,
    )


def join_and_part(first_ref, second_ref, *out_refs):
    count = first_ref.shape[0]
    at = 0
    for out in out_refs:
        rows = pl.ds(at, out.shape[1])
        at += out.shape[1]
        for k in range(count):
            out[k] = first_ref[k, rows, :]
            out[count + k] = second_ref[k, rows, :]


def joined_parts(first, second, heights, before):
    count, _, shard_rows = first.shape
    shapes = [jax.ShapeDtypeStruct((2 * count, height, shard_rows), first.dtype) for height in heights]
    return call(join_and_part, shapes, [VMEM] * 2, (first, second), before=before)


def mark(out_ref):
    out_ref[...] = jnp.zeros_like(out_ref)


def marked(*before, cost=0):
    return call(mark, jax.ShapeDtypeStruct((8, 128), F32), [], (), before=before, cost=cost)


def order_rows(owners, me_ref, weight_ref, out_ref):
    part = weight_ref.shape[0] // len(owners)
    for i, rels in enumerate(owners):
        piece = part // len(rels)
        for j, rel in enumerate(rels):
            source = pl.ds(pl.multiple_of((me_ref[0] ^ rel) * piece, piece), piece)
            out_ref[pl.ds(i * part + j * piece, piece), :] = weight_ref[source, :]


def dense_layer(counts, out_groups, *refs):
    total_refs, refs = refs[: sum(counts)], refs[sum(counts) :]
    rows_ref, cotangent_ref, hidden_ref, agg_ref, grad_pre_ref = refs[:5]
    grad_refs = refs[5:]
    part = rows_ref.shape[0] // len(counts)
    at = 0
    for i, count in enumerate(counts):
        total = total_refs[at][...]
        for ref in total_refs[at + 1 : at + count]:
            total = total + ref[...].astype(F32)
        agg_ref[:, i * part : (i + 1) * part] = total.astype(agg_ref.dtype)
        at += count
    pre_act = jnp.dot(agg_ref[...], rows_ref[...], preferred_element_type=F32)
    slope = jnp.exp(jnp.minimum(pre_act, 0.0))
    positive = pre_act > 0
    hidden_ref[...] = jnp.where(positive, pre_act, slope - 1.0).astype(hidden_ref.dtype)
    slope = jnp.where(positive, F32(1.0), slope)
    grad_pre = (cotangent_ref[...].astype(F32) * slope).astype(grad_pre_ref.dtype)
    grad_pre_ref[...] = grad_pre
    for members, out in zip(out_groups, grad_refs):
        for j, i in enumerate(members):
            out[0, pl.ds(j * part, part), :] = lax.dot_general(
                rows_ref[pl.ds(i * part, part), :],
                grad_pre,
                (((1,), (1,)), ((), ())),
                preferred_element_type=F32,
            ).astype(out.dtype)


def layer(totals, out_groups, weight_rows, cotangent, before):
    shard_rows, width = cotangent.shape
    part = width // len(totals)
    whole = jax.ShapeDtypeStruct((shard_rows, width), BF16)
    grads = [jax.ShapeDtypeStruct((1, len(m) * part, shard_rows), BF16) for m in out_groups]
    counts = [len(terms) for terms in totals]
    outs = call(
        functools.partial(dense_layer, counts, out_groups),
        [whole] * 3 + grads,
        [VMEM] * (sum(counts) + 2),
        (*[term for terms in totals for term in terms], weight_rows, cotangent),
        before=before,
    )
    return outs[0], outs[1], outs[2], outs[3:]


def back_products(count, near_ref, far_ref, *refs):
    rows_refs, out_refs, (left_ref, right_ref) = refs[:count], refs[count:-2], refs[-2:]
    shard_rows = rows_refs[0].shape[2]
    for k in range(left_ref.shape[1] // shard_rows):
        cols = pl.ds(k * shard_rows, shard_rows)
        if count == 2:
            left_ref[:, cols] = rows_refs[0][k]
            right_ref[:, cols] = rows_refs[1][k]
        else:
            left_ref[:, cols] = rows_refs[0][2 * k]
            right_ref[:, cols] = rows_refs[0][2 * k + 1]
    block_c = near_ref.shape[1]
    step = math.gcd(block_c, 256)
    part = out_refs[0].shape[0]
    for col in range(0, block_c, step):
        cols = pl.ds(col, step)
        total = jnp.dot(left_ref[...], near_ref[:, cols], preferred_element_type=F32)
        total = total + jnp.dot(right_ref[...], far_ref[:, cols], preferred_element_type=F32)
        for i, out in enumerate(out_refs):
            out[:, cols] = total[i * part : (i + 1) * part, :].astype(out.dtype)


def back_of(near, far, rows, dtypes, limit, before, cost=0):
    height = rows[0].shape[1]
    shape = (height // len(dtypes), near.shape[1])
    return call(
        functools.partial(back_products, len(rows)),
        [jax.ShapeDtypeStruct(shape, dtype) for dtype in dtypes],
        [VMEM] * (2 + len(rows)),
        (near, far, *rows),
        [pltpu.VMEM((height, near.shape[0]), BF16)] * 2,
        limit,
        before=before,
        cost=cost,
    )


def add_parts(places, own_ref, came_ref, *out_refs):
    piece = out_refs[0].shape[0]
    for place, out in zip(places, out_refs):
        rows = pl.ds(place * piece, piece)
        out[...] = (own_ref[rows, :] + came_ref[rows, :].astype(F32)).astype(out.dtype)


def parts_to_send(own, came, places, piece, before):
    shape = jax.ShapeDtypeStruct((piece, own.shape[1]), BF16)
    return call(
        functools.partial(add_parts, places),
        [shape] * len(places),
        [VMEM] * 2,
        (own, came),
        before=before,
    )


def finish(own_ref, came_ref, *refs):
    out_ref = refs[-1]
    piece = out_ref.shape[1]
    total = own_ref[:piece, :] + came_ref[:piece, :].astype(F32)
    for ref in refs[:-1]:
        total = total + ref[...].astype(F32)
    out_ref[...] = total.T.astype(out_ref.dtype)


def weight_terms(places, agg_ref, grad_pre_ref, *out_refs):
    width = agg_ref.shape[1]
    piece = width // sum(len(group) for group in places)
    for group, out in zip(places, out_refs):
        for i, place in enumerate(group):
            term = lax.dot_general(
                agg_ref[:, place * piece : (place + 1) * piece],
                grad_pre_ref[...],
                (((0,), (0,)), ((), ())),
                preferred_element_type=F32,
            )
            out[pl.ds(i * piece, piece), :] = term.astype(out.dtype)


def add_and_split(side_ref, kept_ref, came_ref, keep_ref, send_ref, total_ref):
    total_ref[...] = kept_ref[...] + came_ref[...]
    half = keep_ref.shape[1]
    side = side_ref[0] & 1
    for k in range(keep_ref.shape[0]):
        mine = pl.ds(pl.multiple_of((2 * k + side) * half, half), half)
        other = pl.ds(pl.multiple_of((2 * k + 1 - side) * half, half), half)
        keep_ref[k] = total_ref[mine, :]
        send_ref[k] = total_ref[other, :].astype(send_ref.dtype)


def add_and_spread(kept_ref, came_ref, keep_ref, *send_refs):
    keep_ref[...] = kept_ref[0] + came_ref[0].astype(F32)
    for k, out in enumerate(send_refs):
        out[...] = (kept_ref[k + 1] + came_ref[k + 1].astype(F32)).astype(out.dtype)


def add_all(*refs):
    terms = [ref[...].astype(F32) for ref in refs[:-1]]
    while len(terms) > 1:
        terms = [sum(terms[i + 1 : i + 2], terms[i]) for i in range(0, len(terms), 2)]
    refs[-1][...] = terms[0].astype(refs[-1].dtype)


def sum_of(terms, dtype, before, cost=0):
    return call(
        add_all,
        jax.ShapeDtypeStruct(terms[0].shape, dtype),
        [VMEM] * len(terms),
        tuple(terms),
        before=before,
        cost=cost,
    )


def stack_all(*refs):
    for i, ref in enumerate(refs[:-1]):
        refs[-1][i] = ref[...]


def place_shares(me_ref, side_ref, own_ref, other_ref, out_ref):
    half = own_ref.shape[2]
    for inner, ref in ((0, own_ref), (1, other_ref)):
        for turn in range(2):
            side = (side_ref[0] ^ turn) & 1
            for k in range(ref.shape[1]):
                place = (me_ref[0] ^ (2 * k + inner)) * 2 + side
                out_ref[pl.ds(pl.multiple_of(place * half, half), half), :] = ref[turn, k].astype(
                    out_ref.dtype
                )


def body(node_features, layer_weight, tile_values, tile_coords, tile_count, cotangent):
    n_row = lax.axis_size("row")
    n_col = lax.axis_size("col")
    ro, co = n_row // 2, n_col // 2
    my_row = lax.axis_index("row").astype(jnp.int32).reshape(1)
    my_col = lax.axis_index("col").astype(jnp.int32).reshape(1)
    shard_rows, width = cotangent.shape
    block_c, piece = node_features.shape
    limit = 12 + (4 * co * shard_rows * block_c) // MIB

    def swap(v, axis, bit):
        size = n_row if axis == "row" else n_col
        return lax.ppermute(v, axis, [(i, i ^ bit) for i in range(size)])

    halves = (range(0, ro // 2), range(ro // 2, ro))
    chunks = [(h, i) for h in range(2) for i in range(2)]
    owners = [[2 * k + i for k in halves[h]] for h, i in chunks]
    flat = [rel for rels in owners for rel in rels]

    features = []
    for rels in owners:
        parts = [swap(node_features, "row", rel) if rel else node_features for rel in rels]
        features.append(jnp.concatenate(parts, axis=1) if len(parts) > 1 else parts[0])
    near, far, own_features, first_away = dense_blocks(
        tile_values[0, 0],
        pltpu.with_memory_space_constraint(tile_coords[0, 0].T, pltpu.HBM),
        tile_count.reshape(-1),
        my_col,
        my_row,
        pltpu.with_memory_space_constraint(features[0], pltpu.HBM),
        co,
        shard_rows,
        max(limit, 48),
    )
    features[0] = own_features
    away, kept = all_products(near, far, features[:3], limit)
    keeps = [*kept, None]
    cames = [swap(v, "col", 1) for v in (first_away, *away)] + [None]
    stages = co.bit_length() - 1
    done = [0] * 4
    turns = [0, 1, 0, 2, 1, 3, 2, 3] if stages == 2 else [0, 1, 2, 3] * stages
    weight_rows = call(
        functools.partial(order_rows, owners),
        jax.ShapeDtypeStruct(layer_weight.shape, BF16),
        [SMEM, VMEM],
        (my_row, layer_weight),
        before=(kept[0],),
    )
    last = weight_rows
    for turn, i in enumerate(turns):
        before = [last]
        if stages == 2 and turn == 5:
            before.append(cames[0])
        if stages == 2 and turn == 7:
            before.append(cames[1])
        cost = COST_F if i in (1, 2) and done[i] == 0 else 0
        keeps[i], last = halved(keeps[i], cames[i], before, cost)
        cames[i] = swap(last, "col", 2 << done[i])
        done[i] += 1
        if turn == 0:
            last_away, keeps[3] = last_products(near, far, features[3], limit, (last,))
            cames[3] = swap(last_away, "col", 1)
            last = keeps[3]
    totals = [[keep, came] for keep, came in zip(keeps, cames)]

    out_groups = ((3,), (2,), (1, 0))
    hidden, agg, grad_pre, grads = layer(
        totals, out_groups, weight_rows, cotangent, (last,)
    )

    places = [[flat.index(2 * k + inner) for k in range(ro)] for inner in range(2)]
    term_shape = (width // 2, width)
    weight_kept, weight_send = call(
        functools.partial(weight_terms, places),
        (jax.ShapeDtypeStruct(term_shape, F32), jax.ShapeDtypeStruct(term_shape, F32)),
        [VMEM] * 2,
        (agg, grad_pre),
    )
    state = {"w": [weight_kept, swap(weight_send, "row", 1)], "last": weight_send}

    def order(*more):
        return [state["last"], *more]

    half_share = (ro, piece // 2, width)

    def weight_core():
        keep, send = call(
            add_and_split,
            (jax.ShapeDtypeStruct(half_share, F32), jax.ShapeDtypeStruct(half_share, BF16)),
            [SMEM, VMEM, VMEM],
            (my_col, *state["w"]),
            [pltpu.VMEM((ro * piece, width), F32)],
            before=order(),
        )
        state["last"] = send
        state["w"] = [keep, swap(send, "col", 1)]

    def weight_side():
        shape = half_share[1:]
        outs = call(
            add_and_spread,
            [jax.ShapeDtypeStruct(shape, F32)] + [jax.ShapeDtypeStruct(shape, BF16)] * (ro - 1),
            [VMEM] * 2,
            tuple(state["w"]),
            before=order(),
        )
        state["last"] = outs[0]
        state["w"] = [outs[0]] + [swap(v, "row", 2 * (k + 1)) for k, v in enumerate(outs[1:])]
        state["bit"] = n_col // 2

    def weight_line():
        bit = state["bit"]
        total = sum_of(state["w"], BF16 if bit > 2 else F32, order())
        state["last"] = total
        state["w"] = [total, swap(total, "col", bit)]
        state["bit"] = bit // 2

    def weight_sum():
        total = sum_of(state["w"], BF16, order(), COST_W)
        state["last"] = total
        state["w"] = [total] + [swap(total, "row", 2 * k) for k in range(1, ro)]

    def weight_stack(axis):
        total = call(
            stack_all,
            jax.ShapeDtypeStruct((len(state["w"]),) + state["w"][0].shape, BF16),
            [VMEM] * len(state["w"]),
            tuple(state["w"]),
            before=order(),
        )
        state["last"] = total
        state["w"] = [total, swap(total, axis, 1)]

    rows = {"C": grads[0], "A": grads[1], "M": grads[2]}
    bits = {"C": n_col // 2, "A": 1, "M": n_col // 2}
    came_rows = {name: swap(rows[name], "col", bits[name]) for name in rows}
    backs = {}

    def join(name, cost=0):
        first, second = rows[name], came_rows[name]
        bit = n_col // 2 if name == "A" and bits[name] == 1 else bits[name] // 2
        bits[name] = bit
        rows[name] = state["last"] = joined(first, second, order(), cost)
        if not (name == "A" and bit == 1):
            came_rows[name] = swap(rows[name], "col", bit)

    def back(members, pair, cost=0, more=()):
        dtypes = [BF16 if chunk[1] else F32 for chunk in members]
        outs = back_of(near, far, pair, dtypes, limit, order(*more), cost)
        state["last"] = outs[0]
        for chunk, out in zip(members, outs):
            backs[chunk] = swap(out, "row", 1) if chunk[1] else out

    arrived = []

    def send_parts(h):
        sent = [p for p, k in enumerate(halves[h]) if k > 0]
        if sent:
            parts = parts_to_send(backs[h, 0], backs[h, 1], sent, piece, order())
            state["last"] = parts[0]
            arrived.extend(swap(v, "row", 2 * halves[h][p]) for p, v in zip(sent, parts))

    weight_core()
    join("A")
    join("C")
    weight_side()
    join("M")
    for _ in range(stages - 1):
        join("C")
    weight_line()
    for _ in range(stages - 1):
        join("A", COST)
    for _ in range(stages - 1):
        join("M")
    for _ in range(stages - 1):
        weight_line()
    back([(1, 1)], (rows["C"], came_rows["C"]))
    weight_sum()
    weight_stack("col")
    join("A", COST_S)
    back([(1, 0)], (rows["A"],))
    send_parts(1)
    back([(0, 1), (0, 0)], (rows["M"], came_rows["M"]), COST_M)
    weight_stack("row")
    send_parts(0)
    state["last"] = marked(state["last"], *arrived, cost=COST)
    grad_features = call(
        finish,
        jax.ShapeDtypeStruct((block_c, piece), BF16),
        [VMEM] * (2 + len(arrived)),
        (backs[0, 0], backs[0, 1], *arrived),
        before=order(),
    )
    grad_weight = call(
        place_shares,
        jax.ShapeDtypeStruct((width, width), F32),
        [SMEM, SMEM, VMEM, VMEM],
        (my_row, my_col, *state["w"]),
    )
    return (hidden, grad_weight, grad_features)


def solution(mesh):
    in_specs = (
        P("col", "row"),
        P(),
        P("row", "col", None, None, None),
        P("row", "col", None, None),
        P("row", "col"),
        P(("row", "col"), None),
    )
    out_specs = (P(("row", "col"), None), P(), P("col", "row"))
    return jax.shard_map(body, mesh=mesh, in_specs=in_specs, out_specs=out_specs, check_vma=False)
```

```python
import functools
import math

import jax
import jax.numpy as jnp
from jax import lax
from jax.experimental import pallas as pl
from jax.experimental.pallas import tpu as pltpu
from jax.sharding import PartitionSpec as P

F32 = jnp.float32
BF16 = jnp.bfloat16
MIB = 1024 * 1024
COST_F, COST_U = 1_000_000_000, 2_000_000_000
COST, COST_S, COST_W, COST_M = 4_000_000_000, 2_000_000_000, 0, 2_000_000_000
SMEM = pl.BlockSpec(memory_space=pltpu.SMEM)
VMEM = pl.BlockSpec(memory_space=pltpu.VMEM)
ANYWHERE = pl.BlockSpec(memory_space=pl.ANY)


def call(kernel, out_shape, in_specs, operands, scratch=(), limit=16, before=(), cost=0):
    many = isinstance(out_shape, (tuple, list))
    count = len(operands)

    def run(*refs):
        kernel(*refs[:count], *refs[count + len(before) :])

    return pl.pallas_call(
        run,
        out_shape=tuple(out_shape) if many else out_shape,
        in_specs=list(in_specs) + [ANYWHERE] * len(before),
        out_specs=(VMEM,) * len(out_shape) if many else VMEM,
        scratch_shapes=list(scratch),
        compiler_params=pltpu.CompilerParams(vmem_limit_bytes=limit * MIB),
        cost_estimate=pl.CostEstimate(flops=cost, bytes_accessed=0, transcendentals=0),
    )(*operands, *before)


def place_tiles(
    outer,
    shard_tiles,
    count_ref,
    me_ref,
    row_ref,
    coords_hbm,
    tiles_ref,
    features_hbm,
    near_ref,
    far_ref,
    features_ref,
    away_ref,
    coords_ref,
    tile_sem,
    in_sems,
):
    slots, tile, _ = tiles_ref.shape
    coords_copy = pltpu.make_async_copy(coords_hbm, coords_ref, in_sems.at[0])
    features_copy = pltpu.make_async_copy(features_hbm, features_ref, in_sems.at[1])
    coords_copy.start()
    features_copy.start()
    me = me_ref[0]
    count = count_ref[0]
    near_ref[...] = jnp.zeros_like(near_ref)
    far_ref[...] = jnp.zeros_like(far_ref)
    coords_copy.wait()
    shift = shard_tiles.bit_length() - 1

    def start(t, carry):
        dest = coords_ref[0, t]
        rel = lax.shift_right_logical(dest, shift) ^ me
        place, bit = 0, 2
        while bit <= outer:
            moved = (outer // bit).bit_length() - bit.bit_length()
            taken = rel & bit
            place = place | (
                lax.shift_left(taken, moved) if moved >= 0 else lax.shift_right_logical(taken, -moved)
            )
            bit *= 2
        row = lax.shift_left(place, shift) | (dest & (shard_tiles - 1))
        rows = pl.ds(pl.multiple_of(row * tile, tile), tile)
        cols = pl.ds(pl.multiple_of(coords_ref[1, t] * tile, tile), tile)

        @pl.when((rel & 1) == 0)
        def _():
            pltpu.make_async_copy(tiles_ref.at[t], near_ref.at[rows, cols], tile_sem).start()

        @pl.when((rel & 1) != 0)
        def _():
            pltpu.make_async_copy(tiles_ref.at[t], far_ref.at[rows, cols], tile_sem).start()

        return carry

    lax.fori_loop(0, count, start, 0)
    some = 1
    while some <= slots:

        @pl.when((count & some) != 0)
        def _():
            part = tiles_ref.at[pl.ds(0, some)]
            pltpu.make_async_copy(part, part, tile_sem).wait()

        some *= 2
    features_copy.wait()
    step = math.gcd(far_ref.shape[0], 256)
    for row in range(0, far_ref.shape[0], step):
        rows = pl.ds(row, step)
        away = jnp.dot(far_ref[rows, :], features_ref[...], preferred_element_type=F32)
        away_ref[rows, :] = away.astype(away_ref.dtype)


def dense_blocks(tiles, coords, count, me, row, features, outer, shard_rows, limit):
    slots, tile, _ = tiles.shape
    block_c, width = features.shape
    half_rows = outer * shard_rows
    return call(
        functools.partial(place_tiles, outer, shard_rows // tile),
        (
            jax.ShapeDtypeStruct((half_rows, block_c), tiles.dtype),
            jax.ShapeDtypeStruct((half_rows, block_c), tiles.dtype),
            jax.ShapeDtypeStruct(features.shape, BF16),
            jax.ShapeDtypeStruct((half_rows, width), BF16),
        ),
        [SMEM, SMEM, SMEM, ANYWHERE, pl.BlockSpec(memory_space=pltpu.HBM), ANYWHERE],
        (count, me, row, coords, tiles, features),
        [
            pltpu.SMEM(coords.shape, jnp.int32),
            pltpu.SemaphoreType.DMA,
            pltpu.SemaphoreType.DMA((2,)),
        ],
        limit,
    )


def products(near_ref, far_ref, *refs):
    count = len(refs) // 3
    chunk_refs, away_refs = refs[:count], refs[count : 2 * count - 1]
    kept_refs, all_ref = refs[2 * count - 1 : -1], refs[-1]
    width = chunk_refs[0].shape[1]
    for i, chunk in enumerate(chunk_refs):
        all_ref[:, i * width : (i + 1) * width] = chunk[...]
    half_rows = near_ref.shape[0]
    step = math.gcd(half_rows, 256)
    for row in range(0, half_rows, step):
        rows = pl.ds(row, step)
        away = jnp.dot(far_ref[rows, :], all_ref[:, width:], preferred_element_type=F32)
        for i, out in enumerate(away_refs):
            out[rows, :] = away[:, i * width : (i + 1) * width].astype(out.dtype)
    for row in range(0, half_rows, step):
        rows = pl.ds(row, step)
        kept = jnp.dot(near_ref[rows, :], all_ref[...], preferred_element_type=F32)
        for i, out in enumerate(kept_refs):
            out[rows, :] = kept[:, i * width : (i + 1) * width]


def all_products(near, far, features, limit):
    half_rows, block_c = near.shape
    width = features[0].shape[1]
    count = len(features)
    away = jax.ShapeDtypeStruct((half_rows, width), BF16)
    kept = jax.ShapeDtypeStruct((half_rows, width), F32)
    outs = call(
        products,
        [away] * (count - 1) + [kept] * count,
        [VMEM] * (2 + count),
        (near, far, *features),
        [pltpu.VMEM((block_c, count * width), BF16)],
        limit,
    )
    return outs[: count - 1], outs[count - 1 :]


def one_product(near_ref, far_ref, chunk_ref, away_ref, kept_ref):
    half_rows = near_ref.shape[0]
    step = math.gcd(half_rows, 256)
    for ref, out in ((far_ref, away_ref), (near_ref, kept_ref)):
        for row in range(0, half_rows, step):
            rows = pl.ds(row, step)
            values = jnp.dot(ref[rows, :], chunk_ref[...], preferred_element_type=F32)
            out[rows, :] = values.astype(out.dtype)


def last_products(near, far, chunk, limit, before):
    shape = (near.shape[0], chunk.shape[1])
    return call(
        one_product,
        (jax.ShapeDtypeStruct(shape, BF16), jax.ShapeDtypeStruct(shape, F32)),
        [VMEM] * 3,
        (near, far, chunk),
        (),
        limit,
        before=before,
    )


def add_and_halve(kept_ref, came_ref, keep_ref, send_ref):
    rows = keep_ref.shape[0]
    keep_ref[...] = kept_ref[:rows, :] + came_ref[:rows, :].astype(F32)
    send_ref[...] = (kept_ref[rows:, :] + came_ref[rows:, :].astype(F32)).astype(send_ref.dtype)


def halved(kept, came, before, cost=0):
    shape = (kept.shape[0] // 2, kept.shape[1])
    return call(
        add_and_halve,
        (jax.ShapeDtypeStruct(shape, F32), jax.ShapeDtypeStruct(shape, BF16)),
        [VMEM] * 2,
        (kept, came),
        before=before,
        cost=cost,
    )


def add_and_part(kept_ref, came_ref, keep_ref, *send_refs):
    rows = keep_ref.shape[0]
    keep_ref[...] = kept_ref[:rows, :] + came_ref[:rows, :].astype(F32)
    for i, out in enumerate(send_refs):
        part = pl.ds((i + 1) * rows, rows)
        out[...] = (kept_ref[part, :] + came_ref[part, :].astype(F32)).astype(out.dtype)


def parted(kept, came, count, before):
    shape = (kept.shape[0] // count, kept.shape[1])
    outs = call(
        add_and_part,
        [jax.ShapeDtypeStruct(shape, F32)] + [jax.ShapeDtypeStruct(shape, BF16)] * (count - 1),
        [VMEM] * 2,
        (kept, came),
        before=before,
    )
    return outs[0], outs[1:]


def join_two(first_ref, second_ref, out_ref):
    out_ref[pl.ds(0, first_ref.shape[0])] = first_ref[...]
    out_ref[pl.ds(first_ref.shape[0], first_ref.shape[0])] = second_ref[...]


def joined(first, second, before, cost=0):
    shape = (2 * first.shape[0],) + first.shape[1:]
    return call(
        join_two,
        jax.ShapeDtypeStruct(shape, first.dtype),
        [VMEM] * 2,
        (first, second),
        before=before,
        cost=cost,
    )


def join_and_part(first_ref, second_ref, *out_refs):
    count = first_ref.shape[0]
    at = 0
    for out in out_refs:
        rows = pl.ds(at, out.shape[1])
        at += out.shape[1]
        for k in range(count):
            out[k] = first_ref[k, rows, :]
            out[count + k] = second_ref[k, rows, :]


def joined_parts(first, second, heights, before):
    count, _, shard_rows = first.shape
    shapes = [jax.ShapeDtypeStruct((2 * count, height, shard_rows), first.dtype) for height in heights]
    return call(join_and_part, shapes, [VMEM] * 2, (first, second), before=before)


def mark(out_ref):
    out_ref[...] = jnp.zeros_like(out_ref)


def marked(*before, cost=0):
    return call(mark, jax.ShapeDtypeStruct((8, 128), F32), [], (), before=before, cost=cost)


def order_rows(owners, me_ref, weight_ref, out_ref):
    part = weight_ref.shape[0] // len(owners)
    for i, rels in enumerate(owners):
        piece = part // len(rels)
        for j, rel in enumerate(rels):
            source = pl.ds(pl.multiple_of((me_ref[0] ^ rel) * piece, piece), piece)
            out_ref[pl.ds(i * part + j * piece, piece), :] = weight_ref[source, :]


def dense_layer(counts, out_groups, *refs):
    total_refs, refs = refs[: sum(counts)], refs[sum(counts) :]
    rows_ref, cotangent_ref, hidden_ref, agg_ref, grad_pre_ref = refs[:5]
    grad_refs = refs[5:]
    part = rows_ref.shape[0] // len(counts)
    at = 0
    for i, count in enumerate(counts):
        total = total_refs[at][...]
        for ref in total_refs[at + 1 : at + count]:
            total = total + ref[...].astype(F32)
        agg_ref[:, i * part : (i + 1) * part] = total.astype(agg_ref.dtype)
        at += count
    pre_act = jnp.dot(agg_ref[...], rows_ref[...], preferred_element_type=F32)
    slope = jnp.exp(jnp.minimum(pre_act, 0.0))
    positive = pre_act > 0
    hidden_ref[...] = jnp.where(positive, pre_act, slope - 1.0).astype(hidden_ref.dtype)
    slope = jnp.where(positive, F32(1.0), slope)
    grad_pre = (cotangent_ref[...].astype(F32) * slope).astype(grad_pre_ref.dtype)
    grad_pre_ref[...] = grad_pre
    for members, out in zip(out_groups, grad_refs):
        for j, i in enumerate(members):
            out[0, pl.ds(j * part, part), :] = lax.dot_general(
                rows_ref[pl.ds(i * part, part), :],
                grad_pre,
                (((1,), (1,)), ((), ())),
                preferred_element_type=F32,
            ).astype(out.dtype)


def layer(totals, out_groups, weight_rows, cotangent, before):
    shard_rows, width = cotangent.shape
    part = width // len(totals)
    whole = jax.ShapeDtypeStruct((shard_rows, width), BF16)
    grads = [jax.ShapeDtypeStruct((1, len(m) * part, shard_rows), BF16) for m in out_groups]
    counts = [len(terms) for terms in totals]
    outs = call(
        functools.partial(dense_layer, counts, out_groups),
        [whole] * 3 + grads,
        [VMEM] * (sum(counts) + 2),
        (*[term for terms in totals for term in terms], weight_rows, cotangent),
        before=before,
    )
    return outs[0], outs[1], outs[2], outs[3:]


def back_products(count, near_ref, far_ref, *refs):
    rows_refs, out_refs, (left_ref, right_ref) = refs[:count], refs[count:-2], refs[-2:]
    shard_rows = rows_refs[0].shape[2]
    for k in range(left_ref.shape[1] // shard_rows):
        cols = pl.ds(k * shard_rows, shard_rows)
        if count == 2:
            left_ref[:, cols] = rows_refs[0][k]
            right_ref[:, cols] = rows_refs[1][k]
        else:
            left_ref[:, cols] = rows_refs[0][2 * k]
            right_ref[:, cols] = rows_refs[0][2 * k + 1]
    block_c = near_ref.shape[1]
    step = math.gcd(block_c, 256)
    part = out_refs[0].shape[0]
    for col in range(0, block_c, step):
        cols = pl.ds(col, step)
        total = jnp.dot(left_ref[...], near_ref[:, cols], preferred_element_type=F32)
        total = total + jnp.dot(right_ref[...], far_ref[:, cols], preferred_element_type=F32)
        for i, out in enumerate(out_refs):
            out[:, cols] = total[i * part : (i + 1) * part, :].astype(out.dtype)


def back_of(near, far, rows, dtypes, limit, before, cost=0):
    height = rows[0].shape[1]
    shape = (height // len(dtypes), near.shape[1])
    return call(
        functools.partial(back_products, len(rows)),
        [jax.ShapeDtypeStruct(shape, dtype) for dtype in dtypes],
        [VMEM] * (2 + len(rows)),
        (near, far, *rows),
        [pltpu.VMEM((height, near.shape[0]), BF16)] * 2,
        limit,
        before=before,
        cost=cost,
    )


def add_parts(places, own_ref, came_ref, *out_refs):
    piece = out_refs[0].shape[0]
    for place, out in zip(places, out_refs):
        rows = pl.ds(place * piece, piece)
        out[...] = (own_ref[rows, :] + came_ref[rows, :].astype(F32)).astype(out.dtype)


def parts_to_send(own, came, places, piece, before):
    shape = jax.ShapeDtypeStruct((piece, own.shape[1]), BF16)
    return call(
        functools.partial(add_parts, places),
        [shape] * len(places),
        [VMEM] * 2,
        (own, came),
        before=before,
    )


def finish(own_ref, came_ref, *refs):
    out_ref = refs[-1]
    piece = out_ref.shape[1]
    total = own_ref[:piece, :] + came_ref[:piece, :].astype(F32)
    for ref in refs[:-1]:
        total = total + ref[...].astype(F32)
    out_ref[...] = total.T.astype(out_ref.dtype)


def weight_terms(places, agg_ref, grad_pre_ref, *out_refs):
    width = agg_ref.shape[1]
    piece = width // sum(len(group) for group in places)
    for group, out in zip(places, out_refs):
        for i, place in enumerate(group):
            term = lax.dot_general(
                agg_ref[:, place * piece : (place + 1) * piece],
                grad_pre_ref[...],
                (((0,), (0,)), ((), ())),
                preferred_element_type=F32,
            )
            out[pl.ds(i * piece, piece), :] = term.astype(out.dtype)


def add_and_split(side_ref, kept_ref, came_ref, keep_ref, send_ref, total_ref):
    total_ref[...] = kept_ref[...] + came_ref[...]
    half = keep_ref.shape[1]
    side = side_ref[0] & 1
    for k in range(keep_ref.shape[0]):
        mine = pl.ds(pl.multiple_of((2 * k + side) * half, half), half)
        other = pl.ds(pl.multiple_of((2 * k + 1 - side) * half, half), half)
        keep_ref[k] = total_ref[mine, :]
        send_ref[k] = total_ref[other, :].astype(send_ref.dtype)


def add_and_spread(kept_ref, came_ref, keep_ref, *send_refs):
    keep_ref[...] = kept_ref[0] + came_ref[0].astype(F32)
    for k, out in enumerate(send_refs):
        out[...] = (kept_ref[k + 1] + came_ref[k + 1].astype(F32)).astype(out.dtype)


def add_all(*refs):
    terms = [ref[...].astype(F32) for ref in refs[:-1]]
    while len(terms) > 1:
        terms = [sum(terms[i + 1 : i + 2], terms[i]) for i in range(0, len(terms), 2)]
    refs[-1][...] = terms[0].astype(refs[-1].dtype)


def sum_of(terms, dtype, before, cost=0):
    return call(
        add_all,
        jax.ShapeDtypeStruct(terms[0].shape, dtype),
        [VMEM] * len(terms),
        tuple(terms),
        before=before,
        cost=cost,
    )


def stack_all(*refs):
    for i, ref in enumerate(refs[:-1]):
        refs[-1][i] = ref[...]


def place_shares(me_ref, side_ref, own_ref, other_ref, out_ref):
    half = own_ref.shape[2]
    for inner, ref in ((0, own_ref), (1, other_ref)):
        for turn in range(2):
            side = (side_ref[0] ^ turn) & 1
            for k in range(ref.shape[1]):
                place = (me_ref[0] ^ (2 * k + inner)) * 2 + side
                out_ref[pl.ds(pl.multiple_of(place * half, half), half), :] = ref[turn, k].astype(
                    out_ref.dtype
                )


def body(node_features, layer_weight, tile_values, tile_coords, tile_count, cotangent):
    n_row = lax.axis_size("row")
    n_col = lax.axis_size("col")
    ro, co = n_row // 2, n_col // 2
    my_row = lax.axis_index("row").astype(jnp.int32).reshape(1)
    my_col = lax.axis_index("col").astype(jnp.int32).reshape(1)
    shard_rows, width = cotangent.shape
    block_c, piece = node_features.shape
    limit = 12 + (4 * co * shard_rows * block_c) // MIB

    def swap(v, axis, bit):
        size = n_row if axis == "row" else n_col
        return lax.ppermute(v, axis, [(i, i ^ bit) for i in range(size)])

    halves = (range(0, ro // 2), range(ro // 2, ro))
    chunks = [(h, i) for h in range(2) for i in range(2)]
    owners = [[2 * k + i for k in halves[h]] for h, i in chunks]
    flat = [rel for rels in owners for rel in rels]

    features = []
    for rels in owners:
        parts = [swap(node_features, "row", rel) if rel else node_features for rel in rels]
        features.append(jnp.concatenate(parts, axis=1) if len(parts) > 1 else parts[0])
    near, far, own_features, first_away = dense_blocks(
        tile_values[0, 0],
        pltpu.with_memory_space_constraint(tile_coords[0, 0].T, pltpu.HBM),
        tile_count.reshape(-1),
        my_col,
        my_row,
        pltpu.with_memory_space_constraint(features[0], pltpu.HBM),
        co,
        shard_rows,
        max(limit, 48),
    )
    features[0] = own_features
    away, kept = all_products(near, far, features[:3], limit)
    keeps = [*kept, None]
    cames = [swap(v, "col", 1) for v in (first_away, *away)] + [None]
    stages = co.bit_length() - 1
    done = [0] * 4
    turns = [0, 1, 0, 2, 1, 3, 2, 3] if stages == 2 else [0, 1, 2, 3] * stages
    weight_rows = call(
        functools.partial(order_rows, owners),
        jax.ShapeDtypeStruct(layer_weight.shape, BF16),
        [SMEM, VMEM],
        (my_row, layer_weight),
        before=(kept[0],),
    )
    last = weight_rows
    for turn, i in enumerate(turns):
        before = [last]
        if stages == 2 and turn == 6:
            before.extend(cames[:2])
        cost = COST_F if i in (1, 2) and done[i] == 0 else COST_U if turn == 6 else 0
        keeps[i], last = halved(keeps[i], cames[i], before, cost)
        cames[i] = swap(last, "col", 2 << done[i])
        done[i] += 1
        if turn == 0:
            last_away, keeps[3] = last_products(near, far, features[3], limit, (last,))
            cames[3] = swap(last_away, "col", 1)
            last = keeps[3]
    totals = [[keep, came] for keep, came in zip(keeps, cames)]

    out_groups = ((3,), (2,), (1, 0))
    hidden, agg, grad_pre, grads = layer(
        totals, out_groups, weight_rows, cotangent, (last,)
    )

    places = [[flat.index(2 * k + inner) for k in range(ro)] for inner in range(2)]
    term_shape = (width // 2, width)
    weight_kept, weight_send = call(
        functools.partial(weight_terms, places),
        (jax.ShapeDtypeStruct(term_shape, F32), jax.ShapeDtypeStruct(term_shape, F32)),
        [VMEM] * 2,
        (agg, grad_pre),
    )
    state = {"w": [weight_kept, swap(weight_send, "row", 1)], "last": weight_send}

    def order(*more):
        return [state["last"], *more]

    half_share = (ro, piece // 2, width)

    def weight_core():
        keep, send = call(
            add_and_split,
            (jax.ShapeDtypeStruct(half_share, F32), jax.ShapeDtypeStruct(half_share, BF16)),
            [SMEM, VMEM, VMEM],
            (my_col, *state["w"]),
            [pltpu.VMEM((ro * piece, width), F32)],
            before=order(),
        )
        state["last"] = send
        state["w"] = [keep, swap(send, "col", 1)]

    def weight_side():
        shape = half_share[1:]
        outs = call(
            add_and_spread,
            [jax.ShapeDtypeStruct(shape, F32)] + [jax.ShapeDtypeStruct(shape, BF16)] * (ro - 1),
            [VMEM] * 2,
            tuple(state["w"]),
            before=order(),
        )
        state["last"] = outs[0]
        state["w"] = [outs[0]] + [swap(v, "row", 2 * (k + 1)) for k, v in enumerate(outs[1:])]
        state["bit"] = n_col // 2

    def weight_line():
        bit = state["bit"]
        total = sum_of(state["w"], BF16 if bit > 2 else F32, order())
        state["last"] = total
        state["w"] = [total, swap(total, "col", bit)]
        state["bit"] = bit // 2

    def weight_sum():
        total = sum_of(state["w"], BF16, order(), COST_W)
        state["last"] = total
        state["w"] = [total] + [swap(total, "row", 2 * k) for k in range(1, ro)]

    def weight_stack(axis):
        total = call(
            stack_all,
            jax.ShapeDtypeStruct((len(state["w"]),) + state["w"][0].shape, BF16),
            [VMEM] * len(state["w"]),
            tuple(state["w"]),
            before=order(),
        )
        state["last"] = total
        state["w"] = [total, swap(total, axis, 1)]

    rows = {"C": grads[0], "A": grads[1], "M": grads[2]}
    bits = {"C": n_col // 2, "A": 1, "M": n_col // 2}
    came_rows = {name: swap(rows[name], "col", bits[name]) for name in rows}
    backs = {}

    def join(name, cost=0):
        first, second = rows[name], came_rows[name]
        bit = n_col // 2 if name == "A" and bits[name] == 1 else bits[name] // 2
        bits[name] = bit
        rows[name] = state["last"] = joined(first, second, order(), cost)
        if not (name == "A" and bit == 1):
            came_rows[name] = swap(rows[name], "col", bit)

    def back(members, pair, cost=0, more=()):
        dtypes = [BF16 if chunk[1] else F32 for chunk in members]
        outs = back_of(near, far, pair, dtypes, limit, order(*more), cost)
        state["last"] = outs[0]
        for chunk, out in zip(members, outs):
            backs[chunk] = swap(out, "row", 1) if chunk[1] else out

    arrived = []

    def send_parts(h):
        sent = [p for p, k in enumerate(halves[h]) if k > 0]
        if sent:
            parts = parts_to_send(backs[h, 0], backs[h, 1], sent, piece, order())
            state["last"] = parts[0]
            arrived.extend(swap(v, "row", 2 * halves[h][p]) for p, v in zip(sent, parts))

    weight_core()
    join("A")
    join("C")
    weight_side()
    join("M")
    for _ in range(stages - 1):
        join("C")
    weight_line()
    for _ in range(stages - 1):
        join("A", COST)
    for _ in range(stages - 1):
        join("M")
    for _ in range(stages - 1):
        weight_line()
    back([(1, 1)], (rows["C"], came_rows["C"]))
    join("A", COST_S)
    back([(1, 0)], (rows["A"],))
    send_parts(1)
    weight_sum()
    weight_stack("col")
    back([(0, 1), (0, 0)], (rows["M"], came_rows["M"]), COST_M)
    weight_stack("row")
    send_parts(0)
    state["last"] = marked(state["last"], *arrived, cost=COST)
    grad_features = call(
        finish,
        jax.ShapeDtypeStruct((block_c, piece), BF16),
        [VMEM] * (2 + len(arrived)),
        (backs[0, 0], backs[0, 1], *arrived),
        before=order(),
    )
    grad_weight = call(
        place_shares,
        jax.ShapeDtypeStruct((width, width), F32),
        [SMEM, SMEM, VMEM, VMEM],
        (my_row, my_col, *state["w"]),
    )
    return (hidden, grad_weight, grad_features)


def solution(mesh):
    in_specs = (
        P("col", "row"),
        P(),
        P("row", "col", None, None, None),
        P("row", "col", None, None),
        P("row", "col"),
        P(("row", "col"), None),
    )
    out_specs = (P(("row", "col"), None), P(), P("col", "row"))
    return jax.shard_map(body, mesh=mesh, in_specs=in_specs, out_specs=out_specs, check_vma=False)
```

```python
import functools
import math

import jax
import jax.numpy as jnp
from jax import lax
from jax.experimental import pallas as pl
from jax.experimental.pallas import tpu as pltpu
from jax.sharding import PartitionSpec as P

F32 = jnp.float32
BF16 = jnp.bfloat16
MIB = 1024 * 1024
COST_F, COST_U = 1_000_000_000, 2_000_000_000
COST, COST_S, COST_W, COST_M = 4_000_000_000, 2_000_000_000, 0, 2_000_000_000
COST_L, COST_K = 3_000_000_000, 2_000_000_000
SMEM = pl.BlockSpec(memory_space=pltpu.SMEM)
VMEM = pl.BlockSpec(memory_space=pltpu.VMEM)
ANYWHERE = pl.BlockSpec(memory_space=pl.ANY)


def call(kernel, out_shape, in_specs, operands, scratch=(), limit=16, before=(), cost=0):
    many = isinstance(out_shape, (tuple, list))
    count = len(operands)

    def run(*refs):
        kernel(*refs[:count], *refs[count + len(before) :])

    return pl.pallas_call(
        run,
        out_shape=tuple(out_shape) if many else out_shape,
        in_specs=list(in_specs) + [ANYWHERE] * len(before),
        out_specs=(VMEM,) * len(out_shape) if many else VMEM,
        scratch_shapes=list(scratch),
        compiler_params=pltpu.CompilerParams(vmem_limit_bytes=limit * MIB),
        cost_estimate=pl.CostEstimate(flops=cost, bytes_accessed=0, transcendentals=0),
    )(*operands, *before)


def place_tiles(
    outer,
    shard_tiles,
    count_ref,
    me_ref,
    row_ref,
    coords_hbm,
    tiles_ref,
    features_hbm,
    near_ref,
    far_ref,
    features_ref,
    away_ref,
    coords_ref,
    tile_sem,
    in_sems,
):
    slots, tile, _ = tiles_ref.shape
    coords_copy = pltpu.make_async_copy(coords_hbm, coords_ref, in_sems.at[0])
    features_copy = pltpu.make_async_copy(features_hbm, features_ref, in_sems.at[1])
    coords_copy.start()
    features_copy.start()
    me = me_ref[0]
    count = count_ref[0]
    near_ref[...] = jnp.zeros_like(near_ref)
    far_ref[...] = jnp.zeros_like(far_ref)
    coords_copy.wait()
    shift = shard_tiles.bit_length() - 1

    def start(t, carry):
        dest = coords_ref[0, t]
        rel = lax.shift_right_logical(dest, shift) ^ me
        place, bit = 0, 2
        while bit <= outer:
            moved = (outer // bit).bit_length() - bit.bit_length()
            taken = rel & bit
            place = place | (
                lax.shift_left(taken, moved) if moved >= 0 else lax.shift_right_logical(taken, -moved)
            )
            bit *= 2
        row = lax.shift_left(place, shift) | (dest & (shard_tiles - 1))
        rows = pl.ds(pl.multiple_of(row * tile, tile), tile)
        cols = pl.ds(pl.multiple_of(coords_ref[1, t] * tile, tile), tile)

        @pl.when((rel & 1) == 0)
        def _():
            pltpu.make_async_copy(tiles_ref.at[t], near_ref.at[rows, cols], tile_sem).start()

        @pl.when((rel & 1) != 0)
        def _():
            pltpu.make_async_copy(tiles_ref.at[t], far_ref.at[rows, cols], tile_sem).start()

        return carry

    lax.fori_loop(0, count, start, 0)
    some = 1
    while some <= slots:

        @pl.when((count & some) != 0)
        def _():
            part = tiles_ref.at[pl.ds(0, some)]
            pltpu.make_async_copy(part, part, tile_sem).wait()

        some *= 2
    features_copy.wait()
    step = math.gcd(far_ref.shape[0], 256)
    for row in range(0, far_ref.shape[0], step):
        rows = pl.ds(row, step)
        away = jnp.dot(far_ref[rows, :], features_ref[...], preferred_element_type=F32)
        away_ref[rows, :] = away.astype(away_ref.dtype)


def dense_blocks(tiles, coords, count, me, row, features, outer, shard_rows, limit):
    slots, tile, _ = tiles.shape
    block_c, width = features.shape
    half_rows = outer * shard_rows
    return call(
        functools.partial(place_tiles, outer, shard_rows // tile),
        (
            jax.ShapeDtypeStruct((half_rows, block_c), tiles.dtype),
            jax.ShapeDtypeStruct((half_rows, block_c), tiles.dtype),
            jax.ShapeDtypeStruct(features.shape, BF16),
            jax.ShapeDtypeStruct((half_rows, width), BF16),
        ),
        [SMEM, SMEM, SMEM, ANYWHERE, pl.BlockSpec(memory_space=pltpu.HBM), ANYWHERE],
        (count, me, row, coords, tiles, features),
        [
            pltpu.SMEM(coords.shape, jnp.int32),
            pltpu.SemaphoreType.DMA,
            pltpu.SemaphoreType.DMA((2,)),
        ],
        limit,
    )


def products(near_ref, far_ref, *refs):
    count = len(refs) // 3
    chunk_refs, away_refs = refs[:count], refs[count : 2 * count - 1]
    kept_refs, all_ref = refs[2 * count - 1 : -1], refs[-1]
    width = chunk_refs[0].shape[1]
    for i, chunk in enumerate(chunk_refs):
        all_ref[:, i * width : (i + 1) * width] = chunk[...]
    half_rows = near_ref.shape[0]
    step = math.gcd(half_rows, 256)
    for row in range(0, half_rows, step):
        rows = pl.ds(row, step)
        away = jnp.dot(far_ref[rows, :], all_ref[:, width:], preferred_element_type=F32)
        for i, out in enumerate(away_refs):
            out[rows, :] = away[:, i * width : (i + 1) * width].astype(out.dtype)
    for row in range(0, half_rows, step):
        rows = pl.ds(row, step)
        kept = jnp.dot(near_ref[rows, :], all_ref[...], preferred_element_type=F32)
        for i, out in enumerate(kept_refs):
            out[rows, :] = kept[:, i * width : (i + 1) * width]


def all_products(near, far, features, limit):
    half_rows, block_c = near.shape
    width = features[0].shape[1]
    count = len(features)
    away = jax.ShapeDtypeStruct((half_rows, width), BF16)
    kept = jax.ShapeDtypeStruct((half_rows, width), F32)
    outs = call(
        products,
        [away] * (count - 1) + [kept] * count,
        [VMEM] * (2 + count),
        (near, far, *features),
        [pltpu.VMEM((block_c, count * width), BF16)],
        limit,
    )
    return outs[: count - 1], outs[count - 1 :]


def one_product(near_ref, far_ref, chunk_ref, away_ref, kept_ref):
    half_rows = near_ref.shape[0]
    step = math.gcd(half_rows, 256)
    for ref, out in ((far_ref, away_ref), (near_ref, kept_ref)):
        for row in range(0, half_rows, step):
            rows = pl.ds(row, step)
            values = jnp.dot(ref[rows, :], chunk_ref[...], preferred_element_type=F32)
            out[rows, :] = values.astype(out.dtype)


def last_products(near, far, chunk, limit, before):
    shape = (near.shape[0], chunk.shape[1])
    return call(
        one_product,
        (jax.ShapeDtypeStruct(shape, BF16), jax.ShapeDtypeStruct(shape, F32)),
        [VMEM] * 3,
        (near, far, chunk),
        (),
        limit,
        before=before,
    )


def add_and_halve(kept_ref, came_ref, keep_ref, send_ref):
    rows = keep_ref.shape[0]
    keep_ref[...] = kept_ref[:rows, :] + came_ref[:rows, :].astype(F32)
    send_ref[...] = (kept_ref[rows:, :] + came_ref[rows:, :].astype(F32)).astype(send_ref.dtype)


def halved(kept, came, before, cost=0):
    shape = (kept.shape[0] // 2, kept.shape[1])
    return call(
        add_and_halve,
        (jax.ShapeDtypeStruct(shape, F32), jax.ShapeDtypeStruct(shape, BF16)),
        [VMEM] * 2,
        (kept, came),
        before=before,
        cost=cost,
    )


def add_and_part(kept_ref, came_ref, keep_ref, *send_refs):
    rows = keep_ref.shape[0]
    keep_ref[...] = kept_ref[:rows, :] + came_ref[:rows, :].astype(F32)
    for i, out in enumerate(send_refs):
        part = pl.ds((i + 1) * rows, rows)
        out[...] = (kept_ref[part, :] + came_ref[part, :].astype(F32)).astype(out.dtype)


def parted(kept, came, count, before):
    shape = (kept.shape[0] // count, kept.shape[1])
    outs = call(
        add_and_part,
        [jax.ShapeDtypeStruct(shape, F32)] + [jax.ShapeDtypeStruct(shape, BF16)] * (count - 1),
        [VMEM] * 2,
        (kept, came),
        before=before,
    )
    return outs[0], outs[1:]


def join_two(first_ref, second_ref, out_ref):
    out_ref[pl.ds(0, first_ref.shape[0])] = first_ref[...]
    out_ref[pl.ds(first_ref.shape[0], first_ref.shape[0])] = second_ref[...]


def joined(first, second, before, cost=0):
    shape = (2 * first.shape[0],) + first.shape[1:]
    return call(
        join_two,
        jax.ShapeDtypeStruct(shape, first.dtype),
        [VMEM] * 2,
        (first, second),
        before=before,
        cost=cost,
    )


def join_and_part(first_ref, second_ref, *out_refs):
    count = first_ref.shape[0]
    at = 0
    for out in out_refs:
        rows = pl.ds(at, out.shape[1])
        at += out.shape[1]
        for k in range(count):
            out[k] = first_ref[k, rows, :]
            out[count + k] = second_ref[k, rows, :]


def joined_parts(first, second, heights, before):
    count, _, shard_rows = first.shape
    shapes = [jax.ShapeDtypeStruct((2 * count, height, shard_rows), first.dtype) for height in heights]
    return call(join_and_part, shapes, [VMEM] * 2, (first, second), before=before)


def mark(out_ref):
    out_ref[...] = jnp.zeros_like(out_ref)


def marked(*before, cost=0):
    return call(mark, jax.ShapeDtypeStruct((8, 128), F32), [], (), before=before, cost=cost)


def order_rows(owners, me_ref, weight_ref, out_ref):
    part = weight_ref.shape[0] // len(owners)
    for i, rels in enumerate(owners):
        piece = part // len(rels)
        for j, rel in enumerate(rels):
            source = pl.ds(pl.multiple_of((me_ref[0] ^ rel) * piece, piece), piece)
            out_ref[pl.ds(i * part + j * piece, piece), :] = weight_ref[source, :]


def dense_layer(counts, out_groups, *refs):
    total_refs, refs = refs[: sum(counts)], refs[sum(counts) :]
    rows_ref, cotangent_ref, hidden_ref, agg_ref, grad_pre_ref = refs[:5]
    grad_refs = refs[5:]
    part = rows_ref.shape[0] // len(counts)
    at = 0
    for i, count in enumerate(counts):
        total = total_refs[at][...]
        for ref in total_refs[at + 1 : at + count]:
            total = total + ref[...].astype(F32)
        agg_ref[:, i * part : (i + 1) * part] = total.astype(agg_ref.dtype)
        at += count
    pre_act = jnp.dot(agg_ref[...], rows_ref[...], preferred_element_type=F32)
    slope = jnp.exp(jnp.minimum(pre_act, 0.0))
    positive = pre_act > 0
    hidden_ref[...] = jnp.where(positive, pre_act, slope - 1.0).astype(hidden_ref.dtype)
    slope = jnp.where(positive, F32(1.0), slope)
    grad_pre = (cotangent_ref[...].astype(F32) * slope).astype(grad_pre_ref.dtype)
    grad_pre_ref[...] = grad_pre
    for members, out in zip(out_groups, grad_refs):
        for j, i in enumerate(members):
            out[0, pl.ds(j * part, part), :] = lax.dot_general(
                rows_ref[pl.ds(i * part, part), :],
                grad_pre,
                (((1,), (1,)), ((), ())),
                preferred_element_type=F32,
            ).astype(out.dtype)


def layer(totals, out_groups, weight_rows, cotangent, before):
    shard_rows, width = cotangent.shape
    part = width // len(totals)
    whole = jax.ShapeDtypeStruct((shard_rows, width), BF16)
    grads = [jax.ShapeDtypeStruct((1, len(m) * part, shard_rows), BF16) for m in out_groups]
    counts = [len(terms) for terms in totals]
    outs = call(
        functools.partial(dense_layer, counts, out_groups),
        [whole] * 3 + grads,
        [VMEM] * (sum(counts) + 2),
        (*[term for terms in totals for term in terms], weight_rows, cotangent),
        before=before,
    )
    return outs[0], outs[1], outs[2], outs[3:]


def back_products(count, near_ref, far_ref, *refs):
    rows_refs, out_refs, (left_ref, right_ref) = refs[:count], refs[count:-2], refs[-2:]
    shard_rows = rows_refs[0].shape[2]
    for k in range(left_ref.shape[1] // shard_rows):
        cols = pl.ds(k * shard_rows, shard_rows)
        if count == 2:
            left_ref[:, cols] = rows_refs[0][k]
            right_ref[:, cols] = rows_refs[1][k]
        else:
            left_ref[:, cols] = rows_refs[0][2 * k]
            right_ref[:, cols] = rows_refs[0][2 * k + 1]
    block_c = near_ref.shape[1]
    step = math.gcd(block_c, 256)
    part = out_refs[0].shape[0]
    for col in range(0, block_c, step):
        cols = pl.ds(col, step)
        total = jnp.dot(left_ref[...], near_ref[:, cols], preferred_element_type=F32)
        total = total + jnp.dot(right_ref[...], far_ref[:, cols], preferred_element_type=F32)
        for i, out in enumerate(out_refs):
            out[:, cols] = total[i * part : (i + 1) * part, :].astype(out.dtype)


def back_of(near, far, rows, dtypes, limit, before, cost=0):
    height = rows[0].shape[1]
    shape = (height // len(dtypes), near.shape[1])
    return call(
        functools.partial(back_products, len(rows)),
        [jax.ShapeDtypeStruct(shape, dtype) for dtype in dtypes],
        [VMEM] * (2 + len(rows)),
        (near, far, *rows),
        [pltpu.VMEM((height, near.shape[0]), BF16)] * 2,
        limit,
        before=before,
        cost=cost,
    )


def add_parts(places, own_ref, came_ref, *out_refs):
    piece = out_refs[0].shape[0]
    for place, out in zip(places, out_refs):
        rows = pl.ds(place * piece, piece)
        out[...] = (own_ref[rows, :] + came_ref[rows, :].astype(F32)).astype(out.dtype)


def parts_to_send(own, came, places, piece, before):
    shape = jax.ShapeDtypeStruct((piece, own.shape[1]), BF16)
    return call(
        functools.partial(add_parts, places),
        [shape] * len(places),
        [VMEM] * 2,
        (own, came),
        before=before,
    )


def finish(own_ref, came_ref, *refs):
    out_ref = refs[-1]
    piece = out_ref.shape[1]
    total = own_ref[:piece, :] + came_ref[:piece, :].astype(F32)
    for ref in refs[:-1]:
        total = total + ref[...].astype(F32)
    out_ref[...] = total.T.astype(out_ref.dtype)


def weight_terms(places, agg_ref, grad_pre_ref, *out_refs):
    width = agg_ref.shape[1]
    piece = width // sum(len(group) for group in places)
    for group, out in zip(places, out_refs):
        for i, place in enumerate(group):
            term = lax.dot_general(
                agg_ref[:, place * piece : (place + 1) * piece],
                grad_pre_ref[...],
                (((0,), (0,)), ((), ())),
                preferred_element_type=F32,
            )
            out[pl.ds(i * piece, piece), :] = term.astype(out.dtype)


def add_and_split(side_ref, kept_ref, came_ref, keep_ref, send_ref, total_ref):
    total_ref[...] = kept_ref[...] + came_ref[...]
    half = keep_ref.shape[1]
    side = side_ref[0] & 1
    for k in range(keep_ref.shape[0]):
        mine = pl.ds(pl.multiple_of((2 * k + side) * half, half), half)
        other = pl.ds(pl.multiple_of((2 * k + 1 - side) * half, half), half)
        keep_ref[k] = total_ref[mine, :]
        send_ref[k] = total_ref[other, :].astype(send_ref.dtype)


def add_and_spread(kept_ref, came_ref, keep_ref, *send_refs):
    keep_ref[...] = kept_ref[0] + came_ref[0].astype(F32)
    for k, out in enumerate(send_refs):
        out[...] = (kept_ref[k + 1] + came_ref[k + 1].astype(F32)).astype(out.dtype)


def add_all(*refs):
    terms = [ref[...].astype(F32) for ref in refs[:-1]]
    while len(terms) > 1:
        terms = [sum(terms[i + 1 : i + 2], terms[i]) for i in range(0, len(terms), 2)]
    refs[-1][...] = terms[0].astype(refs[-1].dtype)


def sum_of(terms, dtype, before, cost=0):
    return call(
        add_all,
        jax.ShapeDtypeStruct(terms[0].shape, dtype),
        [VMEM] * len(terms),
        tuple(terms),
        before=before,
        cost=cost,
    )


def stack_all(*refs):
    for i, ref in enumerate(refs[:-1]):
        refs[-1][i] = ref[...]


def place_shares(me_ref, side_ref, own_ref, other_ref, out_ref):
    half = own_ref.shape[2]
    for inner, ref in ((0, own_ref), (1, other_ref)):
        for turn in range(2):
            side = (side_ref[0] ^ turn) & 1
            for k in range(ref.shape[1]):
                place = (me_ref[0] ^ (2 * k + inner)) * 2 + side
                out_ref[pl.ds(pl.multiple_of(place * half, half), half), :] = ref[turn, k].astype(
                    out_ref.dtype
                )


def body(node_features, layer_weight, tile_values, tile_coords, tile_count, cotangent):
    n_row = lax.axis_size("row")
    n_col = lax.axis_size("col")
    ro, co = n_row // 2, n_col // 2
    my_row = lax.axis_index("row").astype(jnp.int32).reshape(1)
    my_col = lax.axis_index("col").astype(jnp.int32).reshape(1)
    shard_rows, width = cotangent.shape
    block_c, piece = node_features.shape
    limit = 12 + (4 * co * shard_rows * block_c) // MIB

    def swap(v, axis, bit):
        size = n_row if axis == "row" else n_col
        return lax.ppermute(v, axis, [(i, i ^ bit) for i in range(size)])

    halves = (range(0, ro // 2), range(ro // 2, ro))
    chunks = [(h, i) for h in range(2) for i in range(2)]
    owners = [[2 * k + i for k in halves[h]] for h, i in chunks]
    flat = [rel for rels in owners for rel in rels]

    features = []
    for rels in owners:
        parts = [swap(node_features, "row", rel) if rel else node_features for rel in rels]
        features.append(jnp.concatenate(parts, axis=1) if len(parts) > 1 else parts[0])
    near, far, own_features, first_away = dense_blocks(
        tile_values[0, 0],
        pltpu.with_memory_space_constraint(tile_coords[0, 0].T, pltpu.HBM),
        tile_count.reshape(-1),
        my_col,
        my_row,
        pltpu.with_memory_space_constraint(features[0], pltpu.HBM),
        co,
        shard_rows,
        max(limit, 48),
    )
    features[0] = own_features
    away, kept = all_products(near, far, features[:3], limit)
    keeps = [*kept, None]
    cames = [swap(v, "col", 1) for v in (first_away, *away)] + [None]
    stages = co.bit_length() - 1
    done = [0] * 4
    turns = [0, 1, 0, 2, 1, 3, 2, 3] if stages == 2 else [0, 1, 2, 3] * stages
    weight_rows = call(
        functools.partial(order_rows, owners),
        jax.ShapeDtypeStruct(layer_weight.shape, BF16),
        [SMEM, VMEM],
        (my_row, layer_weight),
        before=(kept[0],),
    )
    last = weight_rows
    for turn, i in enumerate(turns):
        before = [last]
        if stages == 2 and turn == 6:
            before.extend(cames[:2])
        cost = COST_F if i in (1, 2) and done[i] == 0 else COST_U if turn == 6 else 0
        keeps[i], last = halved(keeps[i], cames[i], before, cost)
        cames[i] = swap(last, "col", 2 << done[i])
        done[i] += 1
        if turn == 0:
            last_away, keeps[3] = last_products(near, far, features[3], limit, (last,))
            cames[3] = swap(last_away, "col", 1)
            last = keeps[3]
    totals = [[keep, came] for keep, came in zip(keeps, cames)]

    out_groups = ((3,), (2,), (1, 0))
    hidden, agg, grad_pre, grads = layer(
        totals, out_groups, weight_rows, cotangent, (last,)
    )

    places = [[flat.index(2 * k + inner) for k in range(ro)] for inner in range(2)]
    term_shape = (width // 2, width)
    weight_kept, weight_send = call(
        functools.partial(weight_terms, places),
        (jax.ShapeDtypeStruct(term_shape, F32), jax.ShapeDtypeStruct(term_shape, F32)),
        [VMEM] * 2,
        (agg, grad_pre),
    )
    state = {"w": [weight_kept, swap(weight_send, "row", 1)], "last": weight_send}

    def order(*more):
        return [state["last"], *more]

    half_share = (ro, piece // 2, width)

    def weight_core():
        keep, send = call(
            add_and_split,
            (jax.ShapeDtypeStruct(half_share, F32), jax.ShapeDtypeStruct(half_share, BF16)),
            [SMEM, VMEM, VMEM],
            (my_col, *state["w"]),
            [pltpu.VMEM((ro * piece, width), F32)],
            before=order(),
        )
        state["last"] = send
        state["w"] = [keep, swap(send, "col", 1)]

    def weight_side():
        shape = half_share[1:]
        outs = call(
            add_and_spread,
            [jax.ShapeDtypeStruct(shape, F32)] + [jax.ShapeDtypeStruct(shape, BF16)] * (ro - 1),
            [VMEM] * 2,
            tuple(state["w"]),
            before=order(),
        )
        state["last"] = outs[0]
        state["w"] = [outs[0]] + [swap(v, "row", 2 * (k + 1)) for k, v in enumerate(outs[1:])]
        state["bit"] = n_col // 2

    def weight_line(cost=0):
        bit = state["bit"]
        total = sum_of(state["w"], BF16 if bit > 2 else F32, order(), cost)
        state["last"] = total
        state["w"] = [total, swap(total, "col", bit)]
        state["bit"] = bit // 2

    def weight_sum():
        total = sum_of(state["w"], BF16, order(), COST_W)
        state["last"] = total
        state["w"] = [total] + [swap(total, "row", 2 * k) for k in range(1, ro)]

    def weight_stack(axis, cost=0):
        total = call(
            stack_all,
            jax.ShapeDtypeStruct((len(state["w"]),) + state["w"][0].shape, BF16),
            [VMEM] * len(state["w"]),
            tuple(state["w"]),
            before=order(),
            cost=cost,
        )
        state["last"] = total
        state["w"] = [total, swap(total, axis, 1)]

    rows = {"C": grads[0], "A": grads[1], "M": grads[2]}
    bits = {"C": n_col // 2, "A": 1, "M": n_col // 2}
    came_rows = {name: swap(rows[name], "col", bits[name]) for name in rows}
    backs = {}

    def join(name, cost=0):
        first, second = rows[name], came_rows[name]
        bit = n_col // 2 if name == "A" and bits[name] == 1 else bits[name] // 2
        bits[name] = bit
        rows[name] = state["last"] = joined(first, second, order(), cost)
        if not (name == "A" and bit == 1):
            came_rows[name] = swap(rows[name], "col", bit)

    def back(members, pair, cost=0, more=()):
        dtypes = [BF16 if chunk[1] else F32 for chunk in members]
        outs = back_of(near, far, pair, dtypes, limit, order(*more), cost)
        state["last"] = outs[0]
        for chunk, out in zip(members, outs):
            backs[chunk] = swap(out, "row", 1) if chunk[1] else out

    arrived = []

    def send_parts(h):
        sent = [p for p, k in enumerate(halves[h]) if k > 0]
        if sent:
            parts = parts_to_send(backs[h, 0], backs[h, 1], sent, piece, order())
            state["last"] = parts[0]
            arrived.extend(swap(v, "row", 2 * halves[h][p]) for p, v in zip(sent, parts))

    weight_core()
    join("A")
    join("C")
    weight_side()
    join("M")
    for _ in range(stages - 1):
        join("C")
    weight_line()
    for _ in range(stages - 1):
        join("A", COST)
    for _ in range(stages - 1):
        join("M")
    for _ in range(stages - 1):
        weight_line(COST_L)
    back([(1, 1)], (rows["C"], came_rows["C"]))
    weight_sum()
    join("A", COST_S)
    back([(1, 0)], (rows["A"],))
    send_parts(1)
    weight_stack("col", COST_K)
    back([(0, 1), (0, 0)], (rows["M"], came_rows["M"]), COST_M)
    weight_stack("row")
    send_parts(0)
    state["last"] = marked(state["last"], *arrived, cost=COST)
    grad_features = call(
        finish,
        jax.ShapeDtypeStruct((block_c, piece), BF16),
        [VMEM] * (2 + len(arrived)),
        (backs[0, 0], backs[0, 1], *arrived),
        before=order(),
    )
    grad_weight = call(
        place_shares,
        jax.ShapeDtypeStruct((width, width), F32),
        [SMEM, SMEM, VMEM, VMEM],
        (my_row, my_col, *state["w"]),
    )
    return (hidden, grad_weight, grad_features)


def solution(mesh):
    in_specs = (
        P("col", "row"),
        P(),
        P("row", "col", None, None, None),
        P("row", "col", None, None),
        P("row", "col"),
        P(("row", "col"), None),
    )
    out_specs = (P(("row", "col"), None), P(), P("col", "row"))
    return jax.shard_map(body, mesh=mesh, in_specs=in_specs, out_specs=out_specs, check_vma=False)
```

```python
import functools
import math

import jax
import jax.numpy as jnp
from jax import lax
from jax.experimental import pallas as pl
from jax.experimental.pallas import tpu as pltpu
from jax.sharding import PartitionSpec as P

F32 = jnp.float32
BF16 = jnp.bfloat16
MIB = 1024 * 1024
COST_F, COST_U = 1_000_000_000, 2_000_000_000
COST, COST_S, COST_W, COST_M = 4_000_000_000, 2_000_000_000, 0, 2_000_000_000
COST_L, COST_K = 3_000_000_000, 2_000_000_000
SMEM = pl.BlockSpec(memory_space=pltpu.SMEM)
VMEM = pl.BlockSpec(memory_space=pltpu.VMEM)
ANYWHERE = pl.BlockSpec(memory_space=pl.ANY)


def call(kernel, out_shape, in_specs, operands, scratch=(), limit=16, before=(), cost=0):
    many = isinstance(out_shape, (tuple, list))
    count = len(operands)

    def run(*refs):
        kernel(*refs[:count], *refs[count + len(before) :])

    return pl.pallas_call(
        run,
        out_shape=tuple(out_shape) if many else out_shape,
        in_specs=list(in_specs) + [ANYWHERE] * len(before),
        out_specs=(VMEM,) * len(out_shape) if many else VMEM,
        scratch_shapes=list(scratch),
        compiler_params=pltpu.CompilerParams(vmem_limit_bytes=limit * MIB),
        cost_estimate=pl.CostEstimate(flops=cost, bytes_accessed=0, transcendentals=0),
    )(*operands, *before)


def place_tiles(
    outer,
    shard_tiles,
    count_ref,
    me_ref,
    row_ref,
    coords_hbm,
    tiles_ref,
    features_hbm,
    near_ref,
    far_ref,
    features_ref,
    away_ref,
    coords_ref,
    tile_sem,
    in_sems,
):
    slots, tile, _ = tiles_ref.shape
    coords_copy = pltpu.make_async_copy(coords_hbm, coords_ref, in_sems.at[0])
    features_copy = pltpu.make_async_copy(features_hbm, features_ref, in_sems.at[1])
    coords_copy.start()
    features_copy.start()
    me = me_ref[0]
    count = count_ref[0]
    near_ref[...] = jnp.zeros_like(near_ref)
    far_ref[...] = jnp.zeros_like(far_ref)
    coords_copy.wait()
    shift = shard_tiles.bit_length() - 1

    def start(t, carry):
        dest = coords_ref[0, t]
        rel = lax.shift_right_logical(dest, shift) ^ me
        place, bit = 0, 2
        while bit <= outer:
            moved = (outer // bit).bit_length() - bit.bit_length()
            taken = rel & bit
            place = place | (
                lax.shift_left(taken, moved) if moved >= 0 else lax.shift_right_logical(taken, -moved)
            )
            bit *= 2
        row = lax.shift_left(place, shift) | (dest & (shard_tiles - 1))
        rows = pl.ds(pl.multiple_of(row * tile, tile), tile)
        cols = pl.ds(pl.multiple_of(coords_ref[1, t] * tile, tile), tile)

        @pl.when((rel & 1) == 0)
        def _():
            pltpu.make_async_copy(tiles_ref.at[t], near_ref.at[rows, cols], tile_sem).start()

        @pl.when((rel & 1) != 0)
        def _():
            pltpu.make_async_copy(tiles_ref.at[t], far_ref.at[rows, cols], tile_sem).start()

        return carry

    lax.fori_loop(0, count, start, 0)
    some = 1
    while some <= slots:

        @pl.when((count & some) != 0)
        def _():
            part = tiles_ref.at[pl.ds(0, some)]
            pltpu.make_async_copy(part, part, tile_sem).wait()

        some *= 2
    features_copy.wait()
    step = math.gcd(far_ref.shape[0], 256)
    for row in range(0, far_ref.shape[0], step):
        rows = pl.ds(row, step)
        away = jnp.dot(far_ref[rows, :], features_ref[...], preferred_element_type=F32)
        away_ref[rows, :] = away.astype(away_ref.dtype)


def dense_blocks(tiles, coords, count, me, row, features, outer, shard_rows, limit):
    slots, tile, _ = tiles.shape
    block_c, width = features.shape
    half_rows = outer * shard_rows
    return call(
        functools.partial(place_tiles, outer, shard_rows // tile),
        (
            jax.ShapeDtypeStruct((half_rows, block_c), tiles.dtype),
            jax.ShapeDtypeStruct((half_rows, block_c), tiles.dtype),
            jax.ShapeDtypeStruct(features.shape, BF16),
            jax.ShapeDtypeStruct((half_rows, width), BF16),
        ),
        [SMEM, SMEM, SMEM, ANYWHERE, pl.BlockSpec(memory_space=pltpu.HBM), ANYWHERE],
        (count, me, row, coords, tiles, features),
        [
            pltpu.SMEM(coords.shape, jnp.int32),
            pltpu.SemaphoreType.DMA,
            pltpu.SemaphoreType.DMA((2,)),
        ],
        limit,
    )


def products(near_ref, far_ref, *refs):
    count = len(refs) // 3
    chunk_refs, away_refs = refs[:count], refs[count : 2 * count - 1]
    kept_refs, all_ref = refs[2 * count - 1 : -1], refs[-1]
    width = chunk_refs[0].shape[1]
    for i, chunk in enumerate(chunk_refs):
        all_ref[:, i * width : (i + 1) * width] = chunk[...]
    half_rows = near_ref.shape[0]
    step = math.gcd(half_rows, 256)
    for row in range(0, half_rows, step):
        rows = pl.ds(row, step)
        away = jnp.dot(far_ref[rows, :], all_ref[:, width:], preferred_element_type=F32)
        for i, out in enumerate(away_refs):
            out[rows, :] = away[:, i * width : (i + 1) * width].astype(out.dtype)
    for row in range(0, half_rows, step):
        rows = pl.ds(row, step)
        kept = jnp.dot(near_ref[rows, :], all_ref[...], preferred_element_type=F32)
        for i, out in enumerate(kept_refs):
            out[rows, :] = kept[:, i * width : (i + 1) * width]


def all_products(near, far, features, limit):
    half_rows, block_c = near.shape
    width = features[0].shape[1]
    count = len(features)
    away = jax.ShapeDtypeStruct((half_rows, width), BF16)
    kept = jax.ShapeDtypeStruct((half_rows, width), F32)
    outs = call(
        products,
        [away] * (count - 1) + [kept] * count,
        [VMEM] * (2 + count),
        (near, far, *features),
        [pltpu.VMEM((block_c, count * width), BF16)],
        limit,
    )
    return outs[: count - 1], outs[count - 1 :]


def one_product(near_ref, far_ref, chunk_ref, away_ref, kept_ref):
    half_rows = near_ref.shape[0]
    step = math.gcd(half_rows, 256)
    for ref, out in ((far_ref, away_ref), (near_ref, kept_ref)):
        for row in range(0, half_rows, step):
            rows = pl.ds(row, step)
            values = jnp.dot(ref[rows, :], chunk_ref[...], preferred_element_type=F32)
            out[rows, :] = values.astype(out.dtype)


def last_products(near, far, chunk, limit, before):
    shape = (near.shape[0], chunk.shape[1])
    return call(
        one_product,
        (jax.ShapeDtypeStruct(shape, BF16), jax.ShapeDtypeStruct(shape, F32)),
        [VMEM] * 3,
        (near, far, chunk),
        (),
        limit,
        before=before,
    )


def add_and_halve(kept_ref, came_ref, keep_ref, send_ref):
    rows = keep_ref.shape[0]
    keep_ref[...] = kept_ref[:rows, :] + came_ref[:rows, :].astype(F32)
    send_ref[...] = (kept_ref[rows:, :] + came_ref[rows:, :].astype(F32)).astype(send_ref.dtype)


def halved(kept, came, before, cost=0):
    shape = (kept.shape[0] // 2, kept.shape[1])
    return call(
        add_and_halve,
        (jax.ShapeDtypeStruct(shape, F32), jax.ShapeDtypeStruct(shape, BF16)),
        [VMEM] * 2,
        (kept, came),
        before=before,
        cost=cost,
    )


def add_and_part(kept_ref, came_ref, keep_ref, *send_refs):
    rows = keep_ref.shape[0]
    keep_ref[...] = kept_ref[:rows, :] + came_ref[:rows, :].astype(F32)
    for i, out in enumerate(send_refs):
        part = pl.ds((i + 1) * rows, rows)
        out[...] = (kept_ref[part, :] + came_ref[part, :].astype(F32)).astype(out.dtype)


def parted(kept, came, count, before):
    shape = (kept.shape[0] // count, kept.shape[1])
    outs = call(
        add_and_part,
        [jax.ShapeDtypeStruct(shape, F32)] + [jax.ShapeDtypeStruct(shape, BF16)] * (count - 1),
        [VMEM] * 2,
        (kept, came),
        before=before,
    )
    return outs[0], outs[1:]


def join_two(first_ref, second_ref, out_ref):
    out_ref[pl.ds(0, first_ref.shape[0])] = first_ref[...]
    out_ref[pl.ds(first_ref.shape[0], first_ref.shape[0])] = second_ref[...]


def joined(first, second, before, cost=0):
    shape = (2 * first.shape[0],) + first.shape[1:]
    return call(
        join_two,
        jax.ShapeDtypeStruct(shape, first.dtype),
        [VMEM] * 2,
        (first, second),
        before=before,
        cost=cost,
    )


def join_and_part(first_ref, second_ref, *out_refs):
    count = first_ref.shape[0]
    at = 0
    for out in out_refs:
        rows = pl.ds(at, out.shape[1])
        at += out.shape[1]
        for k in range(count):
            out[k] = first_ref[k, rows, :]
            out[count + k] = second_ref[k, rows, :]


def joined_parts(first, second, heights, before):
    count, _, shard_rows = first.shape
    shapes = [jax.ShapeDtypeStruct((2 * count, height, shard_rows), first.dtype) for height in heights]
    return call(join_and_part, shapes, [VMEM] * 2, (first, second), before=before)


def mark(out_ref):
    out_ref[...] = jnp.zeros_like(out_ref)


def marked(*before, cost=0):
    return call(mark, jax.ShapeDtypeStruct((8, 128), F32), [], (), before=before, cost=cost)


def order_rows(owners, me_ref, weight_ref, out_ref):
    part = weight_ref.shape[0] // len(owners)
    for i, rels in enumerate(owners):
        piece = part // len(rels)
        for j, rel in enumerate(rels):
            source = pl.ds(pl.multiple_of((me_ref[0] ^ rel) * piece, piece), piece)
            out_ref[pl.ds(i * part + j * piece, piece), :] = weight_ref[source, :]


def dense_layer(counts, out_groups, *refs):
    total_refs, refs = refs[: sum(counts)], refs[sum(counts) :]
    rows_ref, cotangent_ref, hidden_ref, agg_ref, grad_pre_ref = refs[:5]
    grad_refs = refs[5:]
    part = rows_ref.shape[0] // len(counts)
    at = 0
    for i, count in enumerate(counts):
        total = total_refs[at][...]
        for ref in total_refs[at + 1 : at + count]:
            total = total + ref[...].astype(F32)
        agg_ref[:, i * part : (i + 1) * part] = total.astype(agg_ref.dtype)
        at += count
    pre_act = jnp.dot(agg_ref[...], rows_ref[...], preferred_element_type=F32)
    slope = jnp.exp(jnp.minimum(pre_act, 0.0))
    positive = pre_act > 0
    hidden_ref[...] = jnp.where(positive, pre_act, slope - 1.0).astype(hidden_ref.dtype)
    slope = jnp.where(positive, F32(1.0), slope)
    grad_pre = (cotangent_ref[...].astype(F32) * slope).astype(grad_pre_ref.dtype)
    grad_pre_ref[...] = grad_pre
    for members, out in zip(out_groups, grad_refs):
        for j, i in enumerate(members):
            out[0, pl.ds(j * part, part), :] = lax.dot_general(
                rows_ref[pl.ds(i * part, part), :],
                grad_pre,
                (((1,), (1,)), ((), ())),
                preferred_element_type=F32,
            ).astype(out.dtype)


def layer(totals, out_groups, weight_rows, cotangent, before):
    shard_rows, width = cotangent.shape
    part = width // len(totals)
    whole = jax.ShapeDtypeStruct((shard_rows, width), BF16)
    grads = [jax.ShapeDtypeStruct((1, len(m) * part, shard_rows), BF16) for m in out_groups]
    counts = [len(terms) for terms in totals]
    outs = call(
        functools.partial(dense_layer, counts, out_groups),
        [whole] * 3 + grads,
        [VMEM] * (sum(counts) + 2),
        (*[term for terms in totals for term in terms], weight_rows, cotangent),
        before=before,
    )
    return outs[0], outs[1], outs[2], outs[3:]


def back_products(count, near_ref, far_ref, *refs):
    rows_refs, out_refs, (left_ref, right_ref) = refs[:count], refs[count:-2], refs[-2:]
    shard_rows = rows_refs[0].shape[2]
    for k in range(left_ref.shape[1] // shard_rows):
        cols = pl.ds(k * shard_rows, shard_rows)
        if count == 2:
            left_ref[:, cols] = rows_refs[0][k]
            right_ref[:, cols] = rows_refs[1][k]
        else:
            left_ref[:, cols] = rows_refs[0][2 * k]
            right_ref[:, cols] = rows_refs[0][2 * k + 1]
    block_c = near_ref.shape[1]
    step = math.gcd(block_c, 256)
    part = out_refs[0].shape[0]
    for col in range(0, block_c, step):
        cols = pl.ds(col, step)
        total = jnp.dot(left_ref[...], near_ref[:, cols], preferred_element_type=F32)
        total = total + jnp.dot(right_ref[...], far_ref[:, cols], preferred_element_type=F32)
        for i, out in enumerate(out_refs):
            out[:, cols] = total[i * part : (i + 1) * part, :].astype(out.dtype)


def back_of(near, far, rows, dtypes, limit, before, cost=0):
    height = rows[0].shape[1]
    shape = (height // len(dtypes), near.shape[1])
    return call(
        functools.partial(back_products, len(rows)),
        [jax.ShapeDtypeStruct(shape, dtype) for dtype in dtypes],
        [VMEM] * (2 + len(rows)),
        (near, far, *rows),
        [pltpu.VMEM((height, near.shape[0]), BF16)] * 2,
        limit,
        before=before,
        cost=cost,
    )


def add_parts(places, own_ref, came_ref, *out_refs):
    piece = out_refs[0].shape[0]
    for place, out in zip(places, out_refs):
        rows = pl.ds(place * piece, piece)
        out[...] = (own_ref[rows, :] + came_ref[rows, :].astype(F32)).astype(out.dtype)


def parts_to_send(own, came, places, piece, before):
    shape = jax.ShapeDtypeStruct((piece, own.shape[1]), BF16)
    return call(
        functools.partial(add_parts, places),
        [shape] * len(places),
        [VMEM] * 2,
        (own, came),
        before=before,
    )


def finish(own_ref, came_ref, *refs):
    out_ref = refs[-1]
    piece = out_ref.shape[1]
    total = own_ref[:piece, :] + came_ref[:piece, :].astype(F32)
    for ref in refs[:-1]:
        total = total + ref[...].astype(F32)
    out_ref[...] = total.T.astype(out_ref.dtype)


def weight_terms(places, agg_ref, grad_pre_ref, *out_refs):
    width = agg_ref.shape[1]
    piece = width // sum(len(group) for group in places)
    for group, out in zip(places, out_refs):
        for i, place in enumerate(group):
            term = lax.dot_general(
                agg_ref[:, place * piece : (place + 1) * piece],
                grad_pre_ref[...],
                (((0,), (0,)), ((), ())),
                preferred_element_type=F32,
            )
            out[pl.ds(i * piece, piece), :] = term.astype(out.dtype)


def add_and_split(side_ref, kept_ref, came_ref, keep_ref, send_ref, total_ref):
    total_ref[...] = kept_ref[...] + came_ref[...]
    half = keep_ref.shape[1]
    side = side_ref[0] & 1
    for k in range(keep_ref.shape[0]):
        mine = pl.ds(pl.multiple_of((2 * k + side) * half, half), half)
        other = pl.ds(pl.multiple_of((2 * k + 1 - side) * half, half), half)
        keep_ref[k] = total_ref[mine, :]
        send_ref[k] = total_ref[other, :].astype(send_ref.dtype)


def add_and_spread(kept_ref, came_ref, keep_ref, *send_refs):
    keep_ref[...] = kept_ref[0] + came_ref[0].astype(F32)
    for k, out in enumerate(send_refs):
        out[...] = (kept_ref[k + 1] + came_ref[k + 1].astype(F32)).astype(out.dtype)


def add_all(*refs):
    terms = [ref[...].astype(F32) for ref in refs[:-1]]
    while len(terms) > 1:
        terms = [sum(terms[i + 1 : i + 2], terms[i]) for i in range(0, len(terms), 2)]
    refs[-1][...] = terms[0].astype(refs[-1].dtype)


def sum_of(terms, dtype, before, cost=0):
    return call(
        add_all,
        jax.ShapeDtypeStruct(terms[0].shape, dtype),
        [VMEM] * len(terms),
        tuple(terms),
        before=before,
        cost=cost,
    )


def stack_all(*refs):
    for i, ref in enumerate(refs[:-1]):
        refs[-1][i] = ref[...]


def place_shares(me_ref, side_ref, own_ref, other_ref, out_ref):
    half = own_ref.shape[2]
    for inner, ref in ((0, own_ref), (1, other_ref)):
        for turn in range(2):
            side = (side_ref[0] ^ turn) & 1
            for k in range(ref.shape[1]):
                place = (me_ref[0] ^ (2 * k + inner)) * 2 + side
                out_ref[pl.ds(pl.multiple_of(place * half, half), half), :] = ref[turn, k].astype(
                    out_ref.dtype
                )


def body(node_features, layer_weight, tile_values, tile_coords, tile_count, cotangent):
    n_row = lax.axis_size("row")
    n_col = lax.axis_size("col")
    ro, co = n_row // 2, n_col // 2
    my_row = lax.axis_index("row").astype(jnp.int32).reshape(1)
    my_col = lax.axis_index("col").astype(jnp.int32).reshape(1)
    shard_rows, width = cotangent.shape
    block_c, piece = node_features.shape
    limit = 12 + (4 * co * shard_rows * block_c) // MIB

    def swap(v, axis, bit):
        size = n_row if axis == "row" else n_col
        return lax.ppermute(v, axis, [(i, i ^ bit) for i in range(size)])

    halves = (range(0, ro // 2), range(ro // 2, ro))
    chunks = [(h, i) for h in range(2) for i in range(2)]
    owners = [[2 * k + i for k in halves[h]] for h, i in chunks]
    flat = [rel for rels in owners for rel in rels]

    def arriving(source, rels):
        parts = [swap(source, "row", rel) if rel else source for rel in rels]
        return jnp.concatenate(parts, axis=1) if len(parts) > 1 else parts[0]

    features = [arriving(node_features, rels) for rels in owners[:2]]
    near, far, own_features, first_away = dense_blocks(
        tile_values[0, 0],
        pltpu.with_memory_space_constraint(tile_coords[0, 0].T, pltpu.HBM),
        tile_count.reshape(-1),
        my_col,
        my_row,
        pltpu.with_memory_space_constraint(features[0], pltpu.HBM),
        co,
        shard_rows,
        max(limit, 48),
    )
    features[0] = own_features
    features += [arriving(own_features if ro == 2 else node_features, rels) for rels in owners[2:]]
    away, kept = all_products(near, far, features[:2], limit)

    keeps = [*kept, None, None]
    cames = [swap(v, "col", 1) for v in (first_away, *away)] + [None, None]
    stages = co.bit_length() - 1
    done = [0] * 4
    turns = [0, 1, 0, 2, 1, 3, 2, 3] if stages == 2 else [0, 1, 2, 3] * stages
    weight_rows = call(
        functools.partial(order_rows, owners),
        jax.ShapeDtypeStruct(layer_weight.shape, BF16),
        [SMEM, VMEM],
        (my_row, layer_weight),
        before=(kept[0],),
    )
    last = weight_rows
    for turn, i in enumerate(turns):
        before = [last]
        if stages == 2 and turn == 6:
            before.extend(cames[:2])
        cost = COST_F if i in (1, 2) and done[i] == 0 else COST_U if turn == 6 else 0
        keeps[i], last = halved(keeps[i], cames[i], before, cost)
        cames[i] = swap(last, "col", 2 << done[i])
        done[i] += 1
        if turn < 2:
            next_away, keeps[turn + 2] = last_products(near, far, features[turn + 2], limit, (last,))
            cames[turn + 2] = swap(next_away, "col", 1)
            last = keeps[turn + 2]
    totals = [[keep, came] for keep, came in zip(keeps, cames)]

    out_groups = ((3,), (2,), (1, 0))
    hidden, agg, grad_pre, grads = layer(
        totals, out_groups, weight_rows, cotangent, (last,)
    )

    places = [[flat.index(2 * k + inner) for k in range(ro)] for inner in range(2)]
    term_shape = (width // 2, width)
    weight_kept, weight_send = call(
        functools.partial(weight_terms, places),
        (jax.ShapeDtypeStruct(term_shape, F32), jax.ShapeDtypeStruct(term_shape, F32)),
        [VMEM] * 2,
        (agg, grad_pre),
    )
    state = {"w": [weight_kept, swap(weight_send, "row", 1)], "last": weight_send}

    def order(*more):
        return [state["last"], *more]

    half_share = (ro, piece // 2, width)

    def weight_core():
        keep, send = call(
            add_and_split,
            (jax.ShapeDtypeStruct(half_share, F32), jax.ShapeDtypeStruct(half_share, BF16)),
            [SMEM, VMEM, VMEM],
            (my_col, *state["w"]),
            [pltpu.VMEM((ro * piece, width), F32)],
            before=order(),
        )
        state["last"] = send
        state["w"] = [keep, swap(send, "col", 1)]

    def weight_side():
        shape = half_share[1:]
        outs = call(
            add_and_spread,
            [jax.ShapeDtypeStruct(shape, F32)] + [jax.ShapeDtypeStruct(shape, BF16)] * (ro - 1),
            [VMEM] * 2,
            tuple(state["w"]),
            before=order(),
        )
        state["last"] = outs[0]
        state["w"] = [outs[0]] + [swap(v, "row", 2 * (k + 1)) for k, v in enumerate(outs[1:])]
        state["bit"] = n_col // 2

    def weight_line(cost=0):
        bit = state["bit"]
        total = sum_of(state["w"], BF16 if bit > 2 else F32, order(), cost)
        state["last"] = total
        state["w"] = [total, swap(total, "col", bit)]
        state["bit"] = bit // 2

    def weight_sum():
        total = sum_of(state["w"], BF16, order(), COST_W)
        state["last"] = total
        state["w"] = [total] + [swap(total, "row", 2 * k) for k in range(1, ro)]

    def weight_stack(axis, cost=0):
        total = call(
            stack_all,
            jax.ShapeDtypeStruct((len(state["w"]),) + state["w"][0].shape, BF16),
            [VMEM] * len(state["w"]),
            tuple(state["w"]),
            before=order(),
            cost=cost,
        )
        state["last"] = total
        state["w"] = [total, swap(total, axis, 1)]

    rows = {"C": grads[0], "A": grads[1], "M": grads[2]}
    bits = {"C": n_col // 2, "A": 1, "M": n_col // 2}
    came_rows = {name: swap(rows[name], "col", bits[name]) for name in rows}
    backs = {}

    def join(name, cost=0):
        first, second = rows[name], came_rows[name]
        bit = n_col // 2 if name == "A" and bits[name] == 1 else bits[name] // 2
        bits[name] = bit
        rows[name] = state["last"] = joined(first, second, order(), cost)
        if not (name == "A" and bit == 1):
            came_rows[name] = swap(rows[name], "col", bit)

    def back(members, pair, cost=0, more=()):
        dtypes = [BF16 if chunk[1] else F32 for chunk in members]
        outs = back_of(near, far, pair, dtypes, limit, order(*more), cost)
        state["last"] = outs[0]
        for chunk, out in zip(members, outs):
            backs[chunk] = swap(out, "row", 1) if chunk[1] else out

    arrived = []

    def send_parts(h):
        sent = [p for p, k in enumerate(halves[h]) if k > 0]
        if sent:
            parts = parts_to_send(backs[h, 0], backs[h, 1], sent, piece, order())
            state["last"] = parts[0]
            arrived.extend(swap(v, "row", 2 * halves[h][p]) for p, v in zip(sent, parts))

    weight_core()
    join("A")
    join("C")
    weight_side()
    join("M")
    for _ in range(stages - 1):
        join("C")
    weight_line()
    for _ in range(stages - 1):
        join("A", COST)
    for _ in range(stages - 1):
        join("M")
    for _ in range(stages - 1):
        weight_line(COST_L)
    back([(1, 1)], (rows["C"], came_rows["C"]))
    weight_sum()
    join("A", COST_S)
    back([(1, 0)], (rows["A"],))
    send_parts(1)
    weight_stack("col", COST_K)
    back([(0, 1), (0, 0)], (rows["M"], came_rows["M"]), COST_M)
    weight_stack("row")
    send_parts(0)
    state["last"] = marked(state["last"], *arrived, cost=COST)
    grad_features = call(
        finish,
        jax.ShapeDtypeStruct((block_c, piece), BF16),
        [VMEM] * (2 + len(arrived)),
        (backs[0, 0], backs[0, 1], *arrived),
        before=order(),
    )
    grad_weight = call(
        place_shares,
        jax.ShapeDtypeStruct((width, width), F32),
        [SMEM, SMEM, VMEM, VMEM],
        (my_row, my_col, *state["w"]),
    )
    return (hidden, grad_weight, grad_features)


def solution(mesh):
    in_specs = (
        P("col", "row"),
        P(),
        P("row", "col", None, None, None),
        P("row", "col", None, None),
        P("row", "col"),
        P(("row", "col"), None),
    )
    out_specs = (P(("row", "col"), None), P(), P("col", "row"))
    return jax.shard_map(body, mesh=mesh, in_specs=in_specs, out_specs=out_specs, check_vma=False)
```

```python
import functools
import math

import jax
import jax.numpy as jnp
from jax import lax
from jax.experimental import pallas as pl
from jax.experimental.pallas import tpu as pltpu
from jax.sharding import PartitionSpec as P

F32 = jnp.float32
BF16 = jnp.bfloat16
MIB = 1024 * 1024
COST_F, COST_U = 1_000_000_000, 2_000_000_000
COST, COST_S, COST_W, COST_M = 4_000_000_000, 2_000_000_000, 0, 2_000_000_000
COST_L, COST_K = 3_000_000_000, 2_000_000_000
SMEM = pl.BlockSpec(memory_space=pltpu.SMEM)
VMEM = pl.BlockSpec(memory_space=pltpu.VMEM)
ANYWHERE = pl.BlockSpec(memory_space=pl.ANY)


def call(kernel, out_shape, in_specs, operands, scratch=(), limit=16, before=(), cost=0):
    many = isinstance(out_shape, (tuple, list))
    count = len(operands)

    def run(*refs):
        kernel(*refs[:count], *refs[count + len(before) :])

    return pl.pallas_call(
        run,
        out_shape=tuple(out_shape) if many else out_shape,
        in_specs=list(in_specs) + [ANYWHERE] * len(before),
        out_specs=(VMEM,) * len(out_shape) if many else VMEM,
        scratch_shapes=list(scratch),
        compiler_params=pltpu.CompilerParams(vmem_limit_bytes=limit * MIB),
        cost_estimate=pl.CostEstimate(flops=cost, bytes_accessed=0, transcendentals=0),
    )(*operands, *before)


def place_tiles(
    outer,
    shard_tiles,
    count_ref,
    me_ref,
    row_ref,
    coords_hbm,
    tiles_ref,
    features_hbm,
    near_ref,
    far_ref,
    features_ref,
    away_ref,
    coords_ref,
    tile_sem,
    in_sems,
):
    slots, tile, _ = tiles_ref.shape
    coords_copy = pltpu.make_async_copy(coords_hbm, coords_ref, in_sems.at[0])
    features_copy = pltpu.make_async_copy(features_hbm, features_ref, in_sems.at[1])
    coords_copy.start()
    features_copy.start()
    me = me_ref[0]
    count = count_ref[0]
    near_ref[...] = jnp.zeros_like(near_ref)
    far_ref[...] = jnp.zeros_like(far_ref)
    coords_copy.wait()
    shift = shard_tiles.bit_length() - 1

    def start(t, carry):
        dest = coords_ref[0, t]
        rel = lax.shift_right_logical(dest, shift) ^ me
        place, bit = 0, 2
        while bit <= outer:
            moved = (outer // bit).bit_length() - bit.bit_length()
            taken = rel & bit
            place = place | (
                lax.shift_left(taken, moved) if moved >= 0 else lax.shift_right_logical(taken, -moved)
            )
            bit *= 2
        row = lax.shift_left(place, shift) | (dest & (shard_tiles - 1))
        rows = pl.ds(pl.multiple_of(row * tile, tile), tile)
        cols = pl.ds(pl.multiple_of(coords_ref[1, t] * tile, tile), tile)

        @pl.when((rel & 1) == 0)
        def _():
            pltpu.make_async_copy(tiles_ref.at[t], near_ref.at[rows, cols], tile_sem).start()

        @pl.when((rel & 1) != 0)
        def _():
            pltpu.make_async_copy(tiles_ref.at[t], far_ref.at[rows, cols], tile_sem).start()

        return carry

    lax.fori_loop(0, count, start, 0)
    some = 1
    while some <= slots:

        @pl.when((count & some) != 0)
        def _():
            part = tiles_ref.at[pl.ds(0, some)]
            pltpu.make_async_copy(part, part, tile_sem).wait()

        some *= 2
    features_copy.wait()
    step = math.gcd(far_ref.shape[0], 256)
    for row in range(0, far_ref.shape[0], step):
        rows = pl.ds(row, step)
        away = jnp.dot(far_ref[rows, :], features_ref[...], preferred_element_type=F32)
        away_ref[rows, :] = away.astype(away_ref.dtype)


def dense_blocks(tiles, coords, count, me, row, features, outer, shard_rows, limit):
    slots, tile, _ = tiles.shape
    block_c, width = features.shape
    half_rows = outer * shard_rows
    return call(
        functools.partial(place_tiles, outer, shard_rows // tile),
        (
            jax.ShapeDtypeStruct((half_rows, block_c), tiles.dtype),
            jax.ShapeDtypeStruct((half_rows, block_c), tiles.dtype),
            jax.ShapeDtypeStruct(features.shape, BF16),
            jax.ShapeDtypeStruct((half_rows, width), BF16),
        ),
        [SMEM, SMEM, SMEM, ANYWHERE, pl.BlockSpec(memory_space=pltpu.HBM), ANYWHERE],
        (count, me, row, coords, tiles, features),
        [
            pltpu.SMEM(coords.shape, jnp.int32),
            pltpu.SemaphoreType.DMA,
            pltpu.SemaphoreType.DMA((2,)),
        ],
        limit,
    )


def products(near_ref, far_ref, *refs):
    count = len(refs) // 3
    chunk_refs, away_refs = refs[:count], refs[count : 2 * count - 1]
    kept_refs, all_ref = refs[2 * count - 1 : -1], refs[-1]
    width = chunk_refs[0].shape[1]
    for i, chunk in enumerate(chunk_refs):
        all_ref[:, i * width : (i + 1) * width] = chunk[...]
    half_rows = near_ref.shape[0]
    step = math.gcd(half_rows, 256)
    for row in range(0, half_rows, step):
        rows = pl.ds(row, step)
        away = jnp.dot(far_ref[rows, :], all_ref[:, width:], preferred_element_type=F32)
        for i, out in enumerate(away_refs):
            out[rows, :] = away[:, i * width : (i + 1) * width].astype(out.dtype)
    for row in range(0, half_rows, step):
        rows = pl.ds(row, step)
        kept = jnp.dot(near_ref[rows, :], all_ref[...], preferred_element_type=F32)
        for i, out in enumerate(kept_refs):
            out[rows, :] = kept[:, i * width : (i + 1) * width]


def all_products(near, far, features, limit):
    half_rows, block_c = near.shape
    width = features[0].shape[1]
    count = len(features)
    away = jax.ShapeDtypeStruct((half_rows, width), BF16)
    kept = jax.ShapeDtypeStruct((half_rows, width), F32)
    outs = call(
        products,
        [away] * (count - 1) + [kept] * count,
        [VMEM] * (2 + count),
        (near, far, *features),
        [pltpu.VMEM((block_c, count * width), BF16)],
        limit,
    )
    return outs[: count - 1], outs[count - 1 :]


def one_product(near_ref, far_ref, chunk_ref, away_ref, kept_ref):
    half_rows = near_ref.shape[0]
    step = math.gcd(half_rows, 256)
    for ref, out in ((far_ref, away_ref), (near_ref, kept_ref)):
        for row in range(0, half_rows, step):
            rows = pl.ds(row, step)
            values = jnp.dot(ref[rows, :], chunk_ref[...], preferred_element_type=F32)
            out[rows, :] = values.astype(out.dtype)


def last_products(near, far, chunk, limit, before):
    shape = (near.shape[0], chunk.shape[1])
    return call(
        one_product,
        (jax.ShapeDtypeStruct(shape, BF16), jax.ShapeDtypeStruct(shape, F32)),
        [VMEM] * 3,
        (near, far, chunk),
        (),
        limit,
        before=before,
    )


def add_and_halve(kept_ref, came_ref, keep_ref, send_ref):
    rows = keep_ref.shape[0]
    keep_ref[...] = kept_ref[:rows, :] + came_ref[:rows, :].astype(F32)
    send_ref[...] = (kept_ref[rows:, :] + came_ref[rows:, :].astype(F32)).astype(send_ref.dtype)


def halved(kept, came, before, cost=0):
    shape = (kept.shape[0] // 2, kept.shape[1])
    return call(
        add_and_halve,
        (jax.ShapeDtypeStruct(shape, F32), jax.ShapeDtypeStruct(shape, BF16)),
        [VMEM] * 2,
        (kept, came),
        before=before,
        cost=cost,
    )


def add_and_part(kept_ref, came_ref, keep_ref, *send_refs):
    rows = keep_ref.shape[0]
    keep_ref[...] = kept_ref[:rows, :] + came_ref[:rows, :].astype(F32)
    for i, out in enumerate(send_refs):
        part = pl.ds((i + 1) * rows, rows)
        out[...] = (kept_ref[part, :] + came_ref[part, :].astype(F32)).astype(out.dtype)


def parted(kept, came, count, before):
    shape = (kept.shape[0] // count, kept.shape[1])
    outs = call(
        add_and_part,
        [jax.ShapeDtypeStruct(shape, F32)] + [jax.ShapeDtypeStruct(shape, BF16)] * (count - 1),
        [VMEM] * 2,
        (kept, came),
        before=before,
    )
    return outs[0], outs[1:]


def join_two(first_ref, second_ref, out_ref):
    out_ref[pl.ds(0, first_ref.shape[0])] = first_ref[...]
    out_ref[pl.ds(first_ref.shape[0], first_ref.shape[0])] = second_ref[...]


def joined(first, second, before, cost=0):
    shape = (2 * first.shape[0],) + first.shape[1:]
    return call(
        join_two,
        jax.ShapeDtypeStruct(shape, first.dtype),
        [VMEM] * 2,
        (first, second),
        before=before,
        cost=cost,
    )


def join_and_part(first_ref, second_ref, *out_refs):
    count = first_ref.shape[0]
    at = 0
    for out in out_refs:
        rows = pl.ds(at, out.shape[1])
        at += out.shape[1]
        for k in range(count):
            out[k] = first_ref[k, rows, :]
            out[count + k] = second_ref[k, rows, :]


def joined_parts(first, second, heights, before):
    count, _, shard_rows = first.shape
    shapes = [jax.ShapeDtypeStruct((2 * count, height, shard_rows), first.dtype) for height in heights]
    return call(join_and_part, shapes, [VMEM] * 2, (first, second), before=before)


def mark(out_ref):
    out_ref[...] = jnp.zeros_like(out_ref)


def marked(*before, cost=0):
    return call(mark, jax.ShapeDtypeStruct((8, 128), F32), [], (), before=before, cost=cost)


def order_rows(owners, me_ref, weight_ref, out_ref):
    part = weight_ref.shape[0] // len(owners)
    for i, rels in enumerate(owners):
        piece = part // len(rels)
        for j, rel in enumerate(rels):
            source = pl.ds(pl.multiple_of((me_ref[0] ^ rel) * piece, piece), piece)
            out_ref[pl.ds(i * part + j * piece, piece), :] = weight_ref[source, :]


def dense_layer(counts, out_groups, *refs):
    total_refs, refs = refs[: sum(counts)], refs[sum(counts) :]
    rows_ref, cotangent_ref, hidden_ref, agg_ref, grad_pre_ref = refs[:5]
    grad_refs = refs[5:]
    part = rows_ref.shape[0] // len(counts)
    at = 0
    for i, count in enumerate(counts):
        total = total_refs[at][...]
        for ref in total_refs[at + 1 : at + count]:
            total = total + ref[...].astype(F32)
        agg_ref[:, i * part : (i + 1) * part] = total.astype(agg_ref.dtype)
        at += count
    pre_act = jnp.dot(agg_ref[...], rows_ref[...], preferred_element_type=F32)
    slope = jnp.exp(jnp.minimum(pre_act, 0.0))
    positive = pre_act > 0
    hidden_ref[...] = jnp.where(positive, pre_act, slope - 1.0).astype(hidden_ref.dtype)
    slope = jnp.where(positive, F32(1.0), slope)
    grad_pre = (cotangent_ref[...].astype(F32) * slope).astype(grad_pre_ref.dtype)
    grad_pre_ref[...] = grad_pre
    for members, out in zip(out_groups, grad_refs):
        for j, i in enumerate(members):
            out[0, pl.ds(j * part, part), :] = lax.dot_general(
                rows_ref[pl.ds(i * part, part), :],
                grad_pre,
                (((1,), (1,)), ((), ())),
                preferred_element_type=F32,
            ).astype(out.dtype)


def layer(totals, out_groups, weight_rows, cotangent, before):
    shard_rows, width = cotangent.shape
    part = width // len(totals)
    whole = jax.ShapeDtypeStruct((shard_rows, width), BF16)
    grads = [jax.ShapeDtypeStruct((1, len(m) * part, shard_rows), BF16) for m in out_groups]
    counts = [len(terms) for terms in totals]
    outs = call(
        functools.partial(dense_layer, counts, out_groups),
        [whole] * 3 + grads,
        [VMEM] * (sum(counts) + 2),
        (*[term for terms in totals for term in terms], weight_rows, cotangent),
        before=before,
    )
    return outs[0], outs[1], outs[2], outs[3:]


def back_products(count, near_ref, far_ref, *refs):
    rows_refs, out_refs, (left_ref, right_ref) = refs[:count], refs[count:-2], refs[-2:]
    shard_rows = rows_refs[0].shape[2]
    for k in range(left_ref.shape[1] // shard_rows):
        cols = pl.ds(k * shard_rows, shard_rows)
        if count == 2:
            left_ref[:, cols] = rows_refs[0][k]
            right_ref[:, cols] = rows_refs[1][k]
        else:
            left_ref[:, cols] = rows_refs[0][2 * k]
            right_ref[:, cols] = rows_refs[0][2 * k + 1]
    block_c = near_ref.shape[1]
    step = math.gcd(block_c, 256)
    part = out_refs[0].shape[0]
    for col in range(0, block_c, step):
        cols = pl.ds(col, step)
        total = jnp.dot(left_ref[...], near_ref[:, cols], preferred_element_type=F32)
        total = total + jnp.dot(right_ref[...], far_ref[:, cols], preferred_element_type=F32)
        for i, out in enumerate(out_refs):
            out[:, cols] = total[i * part : (i + 1) * part, :].astype(out.dtype)


def back_of(near, far, rows, dtypes, limit, before, cost=0):
    height = rows[0].shape[1]
    shape = (height // len(dtypes), near.shape[1])
    return call(
        functools.partial(back_products, len(rows)),
        [jax.ShapeDtypeStruct(shape, dtype) for dtype in dtypes],
        [VMEM] * (2 + len(rows)),
        (near, far, *rows),
        [pltpu.VMEM((height, near.shape[0]), BF16)] * 2,
        limit,
        before=before,
        cost=cost,
    )


def add_parts(places, own_ref, came_ref, *out_refs):
    piece = out_refs[0].shape[0]
    for place, out in zip(places, out_refs):
        rows = pl.ds(place * piece, piece)
        out[...] = (own_ref[rows, :] + came_ref[rows, :].astype(F32)).astype(out.dtype)


def parts_to_send(own, came, places, piece, before):
    shape = jax.ShapeDtypeStruct((piece, own.shape[1]), BF16)
    return call(
        functools.partial(add_parts, places),
        [shape] * len(places),
        [VMEM] * 2,
        (own, came),
        before=before,
    )


def finish(own_ref, came_ref, *refs):
    out_ref = refs[-1]
    piece = out_ref.shape[1]
    total = own_ref[:piece, :] + came_ref[:piece, :].astype(F32)
    for ref in refs[:-1]:
        total = total + ref[...].astype(F32)
    out_ref[...] = total.T.astype(out_ref.dtype)


def weight_terms(places, agg_ref, grad_pre_ref, *out_refs):
    width = agg_ref.shape[1]
    piece = width // sum(len(group) for group in places)
    for group, out in zip(places, out_refs):
        for i, place in enumerate(group):
            term = lax.dot_general(
                agg_ref[:, place * piece : (place + 1) * piece],
                grad_pre_ref[...],
                (((0,), (0,)), ((), ())),
                preferred_element_type=F32,
            )
            out[pl.ds(i * piece, piece), :] = term.astype(out.dtype)


def add_and_split(side_ref, kept_ref, came_ref, keep_ref, send_ref, total_ref):
    total_ref[...] = kept_ref[...] + came_ref[...]
    half = keep_ref.shape[1]
    side = side_ref[0] & 1
    for k in range(keep_ref.shape[0]):
        mine = pl.ds(pl.multiple_of((2 * k + side) * half, half), half)
        other = pl.ds(pl.multiple_of((2 * k + 1 - side) * half, half), half)
        keep_ref[k] = total_ref[mine, :]
        send_ref[k] = total_ref[other, :].astype(send_ref.dtype)


def add_and_spread(kept_ref, came_ref, keep_ref, *send_refs):
    keep_ref[...] = kept_ref[0] + came_ref[0].astype(F32)
    for k, out in enumerate(send_refs):
        out[...] = (kept_ref[k + 1] + came_ref[k + 1].astype(F32)).astype(out.dtype)


def add_all(*refs):
    terms = [ref[...].astype(F32) for ref in refs[:-1]]
    while len(terms) > 1:
        terms = [sum(terms[i + 1 : i + 2], terms[i]) for i in range(0, len(terms), 2)]
    refs[-1][...] = terms[0].astype(refs[-1].dtype)


def sum_of(terms, dtype, before, cost=0):
    return call(
        add_all,
        jax.ShapeDtypeStruct(terms[0].shape, dtype),
        [VMEM] * len(terms),
        tuple(terms),
        before=before,
        cost=cost,
    )


def stack_all(*refs):
    for i, ref in enumerate(refs[:-1]):
        refs[-1][i] = ref[...]


def place_shares(me_ref, side_ref, own_ref, other_ref, out_ref):
    half = own_ref.shape[2]
    for inner, ref in ((0, own_ref), (1, other_ref)):
        for turn in range(2):
            side = (side_ref[0] ^ turn) & 1
            for k in range(ref.shape[1]):
                place = (me_ref[0] ^ (2 * k + inner)) * 2 + side
                out_ref[pl.ds(pl.multiple_of(place * half, half), half), :] = ref[turn, k].astype(
                    out_ref.dtype
                )


def finish_both(me_ref, side_ref, own_ref, other_ref, *refs):
    place_shares(me_ref, side_ref, own_ref, other_ref, refs[-2])
    finish(*refs[:-2], refs[-1])


def body(node_features, layer_weight, tile_values, tile_coords, tile_count, cotangent):
    n_row = lax.axis_size("row")
    n_col = lax.axis_size("col")
    ro, co = n_row // 2, n_col // 2
    my_row = lax.axis_index("row").astype(jnp.int32).reshape(1)
    my_col = lax.axis_index("col").astype(jnp.int32).reshape(1)
    shard_rows, width = cotangent.shape
    block_c, piece = node_features.shape
    limit = 12 + (4 * co * shard_rows * block_c) // MIB

    def swap(v, axis, bit):
        size = n_row if axis == "row" else n_col
        return lax.ppermute(v, axis, [(i, i ^ bit) for i in range(size)])

    halves = (range(0, ro // 2), range(ro // 2, ro))
    chunks = [(h, i) for h in range(2) for i in range(2)]
    owners = [[2 * k + i for k in halves[h]] for h, i in chunks]
    flat = [rel for rels in owners for rel in rels]

    def arriving(source, rels):
        parts = [swap(source, "row", rel) if rel else source for rel in rels]
        return jnp.concatenate(parts, axis=1) if len(parts) > 1 else parts[0]

    features = [arriving(node_features, rels) for rels in owners[:2]]
    near, far, own_features, first_away = dense_blocks(
        tile_values[0, 0],
        pltpu.with_memory_space_constraint(tile_coords[0, 0].T, pltpu.HBM),
        tile_count.reshape(-1),
        my_col,
        my_row,
        pltpu.with_memory_space_constraint(features[0], pltpu.HBM),
        co,
        shard_rows,
        max(limit, 48),
    )
    features[0] = own_features
    features += [arriving(own_features if ro == 2 else node_features, rels) for rels in owners[2:]]
    away, kept = all_products(near, far, features[:2], limit)

    keeps = [*kept, None, None]
    cames = [swap(v, "col", 1) for v in (first_away, *away)] + [None, None]
    stages = co.bit_length() - 1
    done = [0] * 4
    turns = [0, 1, 0, 2, 1, 3, 2, 3] if stages == 2 else [0, 1, 2, 3] * stages
    weight_rows = call(
        functools.partial(order_rows, owners),
        jax.ShapeDtypeStruct(layer_weight.shape, BF16),
        [SMEM, VMEM],
        (my_row, layer_weight),
        before=(kept[0],),
    )
    last = weight_rows
    for turn, i in enumerate(turns):
        before = [last]
        if stages == 2 and turn == 6:
            before.extend(cames[:2])
        cost = COST_F if i in (1, 2) and done[i] == 0 else COST_U if turn == 6 else 0
        keeps[i], last = halved(keeps[i], cames[i], before, cost)
        cames[i] = swap(last, "col", 2 << done[i])
        done[i] += 1
        if turn < 2:
            next_away, keeps[turn + 2] = last_products(near, far, features[turn + 2], limit, (last,))
            cames[turn + 2] = swap(next_away, "col", 1)
            last = keeps[turn + 2]
    totals = [[keep, came] for keep, came in zip(keeps, cames)]

    out_groups = ((3,), (2,), (1, 0))
    hidden, agg, grad_pre, grads = layer(
        totals, out_groups, weight_rows, cotangent, (last,)
    )

    places = [[flat.index(2 * k + inner) for k in range(ro)] for inner in range(2)]
    term_shape = (width // 2, width)
    weight_kept, weight_send = call(
        functools.partial(weight_terms, places),
        (jax.ShapeDtypeStruct(term_shape, F32), jax.ShapeDtypeStruct(term_shape, F32)),
        [VMEM] * 2,
        (agg, grad_pre),
    )
    state = {"w": [weight_kept, swap(weight_send, "row", 1)], "last": weight_send}

    def order(*more):
        return [state["last"], *more]

    half_share = (ro, piece // 2, width)

    def weight_core():
        keep, send = call(
            add_and_split,
            (jax.ShapeDtypeStruct(half_share, F32), jax.ShapeDtypeStruct(half_share, BF16)),
            [SMEM, VMEM, VMEM],
            (my_col, *state["w"]),
            [pltpu.VMEM((ro * piece, width), F32)],
            before=order(),
        )
        state["last"] = send
        state["w"] = [keep, swap(send, "col", 1)]

    def weight_side():
        shape = half_share[1:]
        outs = call(
            add_and_spread,
            [jax.ShapeDtypeStruct(shape, F32)] + [jax.ShapeDtypeStruct(shape, BF16)] * (ro - 1),
            [VMEM] * 2,
            tuple(state["w"]),
            before=order(),
        )
        state["last"] = outs[0]
        state["w"] = [outs[0]] + [swap(v, "row", 2 * (k + 1)) for k, v in enumerate(outs[1:])]
        state["bit"] = n_col // 2

    def weight_line(cost=0):
        bit = state["bit"]
        total = sum_of(state["w"], BF16 if bit > 2 else F32, order(), cost)
        state["last"] = total
        state["w"] = [total, swap(total, "col", bit)]
        state["bit"] = bit // 2

    def weight_sum():
        total = sum_of(state["w"], BF16, order(), COST_W)
        state["last"] = total
        state["w"] = [total] + [swap(total, "row", 2 * k) for k in range(1, ro)]

    def weight_stack(axis, cost=0):
        total = call(
            stack_all,
            jax.ShapeDtypeStruct((len(state["w"]),) + state["w"][0].shape, BF16),
            [VMEM] * len(state["w"]),
            tuple(state["w"]),
            before=order(),
            cost=cost,
        )
        state["last"] = total
        state["w"] = [total, swap(total, axis, 1)]

    rows = {"C": grads[0], "A": grads[1], "M": grads[2]}
    bits = {"C": n_col // 2, "A": 1, "M": n_col // 2}
    came_rows = {name: swap(rows[name], "col", bits[name]) for name in rows}
    backs = {}

    def join(name, cost=0):
        first, second = rows[name], came_rows[name]
        bit = n_col // 2 if name == "A" and bits[name] == 1 else bits[name] // 2
        bits[name] = bit
        rows[name] = state["last"] = joined(first, second, order(), cost)
        if not (name == "A" and bit == 1):
            came_rows[name] = swap(rows[name], "col", bit)

    def back(members, pair, cost=0, more=()):
        dtypes = [BF16 if chunk[1] else F32 for chunk in members]
        outs = back_of(near, far, pair, dtypes, limit, order(*more), cost)
        state["last"] = outs[0]
        for chunk, out in zip(members, outs):
            backs[chunk] = swap(out, "row", 1) if chunk[1] else out

    arrived = []

    def send_parts(h):
        sent = [p for p, k in enumerate(halves[h]) if k > 0]
        if sent:
            parts = parts_to_send(backs[h, 0], backs[h, 1], sent, piece, order())
            state["last"] = parts[0]
            arrived.extend(swap(v, "row", 2 * halves[h][p]) for p, v in zip(sent, parts))

    weight_core()
    join("A")
    join("C")
    weight_side()
    join("M")
    for _ in range(stages - 1):
        join("C")
    weight_line()
    for _ in range(stages - 1):
        join("A", COST)
    for _ in range(stages - 1):
        join("M")
    for _ in range(stages - 1):
        weight_line(COST_L)
    back([(1, 1)], (rows["C"], came_rows["C"]))
    weight_sum()
    join("A", COST_S)
    back([(1, 0)], (rows["A"],))
    send_parts(1)
    weight_stack("col", COST_K)
    back([(0, 1), (0, 0)], (rows["M"], came_rows["M"]), COST_M)
    weight_stack("row")
    send_parts(0)
    state["last"] = marked(state["last"], *arrived, cost=COST)
    grad_weight, grad_features = call(
        finish_both,
        (
            jax.ShapeDtypeStruct((width, width), F32),
            jax.ShapeDtypeStruct((block_c, piece), BF16),
        ),
        [SMEM, SMEM] + [VMEM] * (4 + len(arrived)),
        (my_row, my_col, *state["w"], backs[0, 0], backs[0, 1], *arrived),
        before=order(),
    )
    return (hidden, grad_weight, grad_features)


def solution(mesh):
    in_specs = (
        P("col", "row"),
        P(),
        P("row", "col", None, None, None),
        P("row", "col", None, None),
        P("row", "col"),
        P(("row", "col"), None),
    )
    out_specs = (P(("row", "col"), None), P(), P("col", "row"))
    return jax.shard_map(body, mesh=mesh, in_specs=in_specs, out_specs=out_specs, check_vma=False)
```

```python
import functools
import math

import jax
import jax.numpy as jnp
from jax import lax
from jax.experimental import pallas as pl
from jax.experimental.pallas import tpu as pltpu
from jax.sharding import PartitionSpec as P

F32 = jnp.float32
BF16 = jnp.bfloat16
MIB = 1024 * 1024
COST_F, COST_U = 1_000_000_000, 2_000_000_000
COST, COST_S, COST_W, COST_M = 4_000_000_000, 2_000_000_000, 0, 2_000_000_000
COST_L, COST_K = 3_000_000_000, 2_000_000_000
SMEM = pl.BlockSpec(memory_space=pltpu.SMEM)
VMEM = pl.BlockSpec(memory_space=pltpu.VMEM)
ANYWHERE = pl.BlockSpec(memory_space=pl.ANY)


def call(kernel, out_shape, in_specs, operands, scratch=(), limit=16, before=(), cost=0):
    many = isinstance(out_shape, (tuple, list))
    count = len(operands)

    def run(*refs):
        kernel(*refs[:count], *refs[count + len(before) :])

    return pl.pallas_call(
        run,
        out_shape=tuple(out_shape) if many else out_shape,
        in_specs=list(in_specs) + [ANYWHERE] * len(before),
        out_specs=(VMEM,) * len(out_shape) if many else VMEM,
        scratch_shapes=list(scratch),
        compiler_params=pltpu.CompilerParams(vmem_limit_bytes=limit * MIB),
        cost_estimate=pl.CostEstimate(flops=cost, bytes_accessed=0, transcendentals=0),
    )(*operands, *before)


def place_tiles(
    outer,
    shard_tiles,
    count_ref,
    me_ref,
    row_ref,
    coords_hbm,
    tiles_ref,
    features_hbm,
    near_ref,
    far_ref,
    features_ref,
    away_ref,
    coords_ref,
    tile_sem,
    in_sems,
):
    slots, tile, _ = tiles_ref.shape
    coords_copy = pltpu.make_async_copy(coords_hbm, coords_ref, in_sems.at[0])
    features_copy = pltpu.make_async_copy(features_hbm, features_ref, in_sems.at[1])
    coords_copy.start()
    features_copy.start()
    me = me_ref[0]
    count = count_ref[0]
    near_ref[...] = jnp.zeros_like(near_ref)
    far_ref[...] = jnp.zeros_like(far_ref)
    coords_copy.wait()
    shift = shard_tiles.bit_length() - 1

    def start(t, carry):
        dest = coords_ref[0, t]
        rel = lax.shift_right_logical(dest, shift) ^ me
        place, bit = 0, 2
        while bit <= outer:
            moved = (outer // bit).bit_length() - bit.bit_length()
            taken = rel & bit
            place = place | (
                lax.shift_left(taken, moved) if moved >= 0 else lax.shift_right_logical(taken, -moved)
            )
            bit *= 2
        row = lax.shift_left(place, shift) | (dest & (shard_tiles - 1))
        rows = pl.ds(pl.multiple_of(row * tile, tile), tile)
        cols = pl.ds(pl.multiple_of(coords_ref[1, t] * tile, tile), tile)

        @pl.when((rel & 1) == 0)
        def _():
            pltpu.make_async_copy(tiles_ref.at[t], near_ref.at[rows, cols], tile_sem).start()

        @pl.when((rel & 1) != 0)
        def _():
            pltpu.make_async_copy(tiles_ref.at[t], far_ref.at[rows, cols], tile_sem).start()

        return carry

    lax.fori_loop(0, count, start, 0)
    some = 1
    while some <= slots:

        @pl.when((count & some) != 0)
        def _():
            part = tiles_ref.at[pl.ds(0, some)]
            pltpu.make_async_copy(part, part, tile_sem).wait()

        some *= 2
    features_copy.wait()
    step = math.gcd(far_ref.shape[0], 256)
    for row in range(0, far_ref.shape[0], step):
        rows = pl.ds(row, step)
        away = jnp.dot(far_ref[rows, :], features_ref[...], preferred_element_type=F32)
        away_ref[rows, :] = away.astype(away_ref.dtype)


def dense_blocks(tiles, coords, count, me, row, features, outer, shard_rows, limit):
    slots, tile, _ = tiles.shape
    block_c, width = features.shape
    half_rows = outer * shard_rows
    return call(
        functools.partial(place_tiles, outer, shard_rows // tile),
        (
            jax.ShapeDtypeStruct((half_rows, block_c), tiles.dtype),
            jax.ShapeDtypeStruct((half_rows, block_c), tiles.dtype),
            jax.ShapeDtypeStruct(features.shape, BF16),
            jax.ShapeDtypeStruct((half_rows, width), BF16),
        ),
        [SMEM, SMEM, SMEM, ANYWHERE, pl.BlockSpec(memory_space=pltpu.HBM), ANYWHERE],
        (count, me, row, coords, tiles, features),
        [
            pltpu.SMEM(coords.shape, jnp.int32),
            pltpu.SemaphoreType.DMA,
            pltpu.SemaphoreType.DMA((2,)),
        ],
        limit,
    )


def products(near_ref, far_ref, *refs):
    count = len(refs) // 3
    chunk_refs, away_refs = refs[:count], refs[count : 2 * count - 1]
    kept_refs, all_ref = refs[2 * count - 1 : -1], refs[-1]
    width = chunk_refs[0].shape[1]
    for i, chunk in enumerate(chunk_refs):
        all_ref[:, i * width : (i + 1) * width] = chunk[...]
    half_rows = near_ref.shape[0]
    step = math.gcd(half_rows, 256)
    for row in range(0, half_rows, step):
        rows = pl.ds(row, step)
        away = jnp.dot(far_ref[rows, :], all_ref[:, width:], preferred_element_type=F32)
        for i, out in enumerate(away_refs):
            out[rows, :] = away[:, i * width : (i + 1) * width].astype(out.dtype)
    for row in range(0, half_rows, step):
        rows = pl.ds(row, step)
        kept = jnp.dot(near_ref[rows, :], all_ref[...], preferred_element_type=F32)
        for i, out in enumerate(kept_refs):
            out[rows, :] = kept[:, i * width : (i + 1) * width]


def all_products(near, far, features, limit):
    half_rows, block_c = near.shape
    width = features[0].shape[1]
    count = len(features)
    away = jax.ShapeDtypeStruct((half_rows, width), BF16)
    kept = jax.ShapeDtypeStruct((half_rows, width), F32)
    outs = call(
        products,
        [away] * (count - 1) + [kept] * count,
        [VMEM] * (2 + count),
        (near, far, *features),
        [pltpu.VMEM((block_c, count * width), BF16)],
        limit,
    )
    return outs[: count - 1], outs[count - 1 :]


def one_product(near_ref, far_ref, chunk_ref, away_ref, kept_ref):
    half_rows = near_ref.shape[0]
    step = math.gcd(half_rows, 256)
    for ref, out in ((far_ref, away_ref), (near_ref, kept_ref)):
        for row in range(0, half_rows, step):
            rows = pl.ds(row, step)
            values = jnp.dot(ref[rows, :], chunk_ref[...], preferred_element_type=F32)
            out[rows, :] = values.astype(out.dtype)


def last_products(near, far, chunk, limit, before):
    shape = (near.shape[0], chunk.shape[1])
    return call(
        one_product,
        (jax.ShapeDtypeStruct(shape, BF16), jax.ShapeDtypeStruct(shape, F32)),
        [VMEM] * 3,
        (near, far, chunk),
        (),
        limit,
        before=before,
    )


def add_and_halve(kept_ref, came_ref, keep_ref, send_ref):
    rows = keep_ref.shape[0]
    keep_ref[...] = kept_ref[:rows, :] + came_ref[:rows, :].astype(F32)
    send_ref[...] = (kept_ref[rows:, :] + came_ref[rows:, :].astype(F32)).astype(send_ref.dtype)


def halved(kept, came, before, cost=0):
    shape = (kept.shape[0] // 2, kept.shape[1])
    return call(
        add_and_halve,
        (jax.ShapeDtypeStruct(shape, F32), jax.ShapeDtypeStruct(shape, BF16)),
        [VMEM] * 2,
        (kept, came),
        before=before,
        cost=cost,
    )


def add_and_part(kept_ref, came_ref, keep_ref, *send_refs):
    rows = keep_ref.shape[0]
    keep_ref[...] = kept_ref[:rows, :] + came_ref[:rows, :].astype(F32)
    for i, out in enumerate(send_refs):
        part = pl.ds((i + 1) * rows, rows)
        out[...] = (kept_ref[part, :] + came_ref[part, :].astype(F32)).astype(out.dtype)


def parted(kept, came, count, before):
    shape = (kept.shape[0] // count, kept.shape[1])
    outs = call(
        add_and_part,
        [jax.ShapeDtypeStruct(shape, F32)] + [jax.ShapeDtypeStruct(shape, BF16)] * (count - 1),
        [VMEM] * 2,
        (kept, came),
        before=before,
    )
    return outs[0], outs[1:]


def join_two(first_ref, second_ref, out_ref):
    out_ref[pl.ds(0, first_ref.shape[0])] = first_ref[...]
    out_ref[pl.ds(first_ref.shape[0], first_ref.shape[0])] = second_ref[...]


def joined(first, second, before, cost=0):
    shape = (2 * first.shape[0],) + first.shape[1:]
    return call(
        join_two,
        jax.ShapeDtypeStruct(shape, first.dtype),
        [VMEM] * 2,
        (first, second),
        before=before,
        cost=cost,
    )


def join_and_part(first_ref, second_ref, *out_refs):
    count = first_ref.shape[0]
    at = 0
    for out in out_refs:
        rows = pl.ds(at, out.shape[1])
        at += out.shape[1]
        for k in range(count):
            out[k] = first_ref[k, rows, :]
            out[count + k] = second_ref[k, rows, :]


def joined_parts(first, second, heights, before):
    count, _, shard_rows = first.shape
    shapes = [jax.ShapeDtypeStruct((2 * count, height, shard_rows), first.dtype) for height in heights]
    return call(join_and_part, shapes, [VMEM] * 2, (first, second), before=before)


def mark(out_ref):
    out_ref[...] = jnp.zeros_like(out_ref)


def marked(*before, cost=0):
    return call(mark, jax.ShapeDtypeStruct((8, 128), F32), [], (), before=before, cost=cost)


def order_rows(owners, me_ref, weight_ref, out_ref):
    part = weight_ref.shape[0] // len(owners)
    for i, rels in enumerate(owners):
        piece = part // len(rels)
        for j, rel in enumerate(rels):
            source = pl.ds(pl.multiple_of((me_ref[0] ^ rel) * piece, piece), piece)
            out_ref[pl.ds(i * part + j * piece, piece), :] = weight_ref[source, :]


def dense_layer(counts, out_groups, *refs):
    total_refs, refs = refs[: sum(counts)], refs[sum(counts) :]
    rows_ref, cotangent_ref, hidden_ref, agg_ref, grad_pre_ref = refs[:5]
    grad_refs = refs[5:]
    part = rows_ref.shape[0] // len(counts)
    at = 0
    for i, count in enumerate(counts):
        total = total_refs[at][...]
        for ref in total_refs[at + 1 : at + count]:
            total = total + ref[...].astype(F32)
        agg_ref[:, i * part : (i + 1) * part] = total.astype(agg_ref.dtype)
        at += count
    pre_act = jnp.dot(agg_ref[...], rows_ref[...], preferred_element_type=F32)
    slope = jnp.exp(jnp.minimum(pre_act, 0.0))
    positive = pre_act > 0
    hidden_ref[...] = jnp.where(positive, pre_act, slope - 1.0).astype(hidden_ref.dtype)
    slope = jnp.where(positive, F32(1.0), slope)
    grad_pre = (cotangent_ref[...].astype(F32) * slope).astype(grad_pre_ref.dtype)
    grad_pre_ref[...] = grad_pre
    for members, out in zip(out_groups, grad_refs):
        for j, i in enumerate(members):
            out[0, pl.ds(j * part, part), :] = lax.dot_general(
                rows_ref[pl.ds(i * part, part), :],
                grad_pre,
                (((1,), (1,)), ((), ())),
                preferred_element_type=F32,
            ).astype(out.dtype)


def layer(totals, out_groups, weight_rows, cotangent, before):
    shard_rows, width = cotangent.shape
    part = width // len(totals)
    whole = jax.ShapeDtypeStruct((shard_rows, width), BF16)
    grads = [jax.ShapeDtypeStruct((1, len(m) * part, shard_rows), BF16) for m in out_groups]
    counts = [len(terms) for terms in totals]
    outs = call(
        functools.partial(dense_layer, counts, out_groups),
        [whole] * 3 + grads,
        [VMEM] * (sum(counts) + 2),
        (*[term for terms in totals for term in terms], weight_rows, cotangent),
        before=before,
    )
    return outs[0], outs[1], outs[2], outs[3:]


def back_products(count, near_ref, far_ref, *refs):
    rows_refs, out_refs, (left_ref, right_ref) = refs[:count], refs[count:-2], refs[-2:]
    shard_rows = rows_refs[0].shape[2]
    for k in range(left_ref.shape[1] // shard_rows):
        cols = pl.ds(k * shard_rows, shard_rows)
        if count == 2:
            left_ref[:, cols] = rows_refs[0][k]
            right_ref[:, cols] = rows_refs[1][k]
        else:
            left_ref[:, cols] = rows_refs[0][2 * k]
            right_ref[:, cols] = rows_refs[0][2 * k + 1]
    block_c = near_ref.shape[1]
    step = math.gcd(block_c, 256)
    part = out_refs[0].shape[0]
    for col in range(0, block_c, step):
        cols = pl.ds(col, step)
        total = jnp.dot(left_ref[...], near_ref[:, cols], preferred_element_type=F32)
        total = total + jnp.dot(right_ref[...], far_ref[:, cols], preferred_element_type=F32)
        for i, out in enumerate(out_refs):
            out[:, cols] = total[i * part : (i + 1) * part, :].astype(out.dtype)


def back_of(near, far, rows, dtypes, limit, before, cost=0):
    height = rows[0].shape[1]
    shape = (height // len(dtypes), near.shape[1])
    return call(
        functools.partial(back_products, len(rows)),
        [jax.ShapeDtypeStruct(shape, dtype) for dtype in dtypes],
        [VMEM] * (2 + len(rows)),
        (near, far, *rows),
        [pltpu.VMEM((height, near.shape[0]), BF16)] * 2,
        limit,
        before=before,
        cost=cost,
    )


def add_parts(places, own_ref, came_ref, *out_refs):
    piece = out_refs[0].shape[0]
    for place, out in zip(places, out_refs):
        rows = pl.ds(place * piece, piece)
        out[...] = (own_ref[rows, :] + came_ref[rows, :].astype(F32)).astype(out.dtype)


def parts_to_send(own, came, places, piece, before):
    shape = jax.ShapeDtypeStruct((piece, own.shape[1]), BF16)
    return call(
        functools.partial(add_parts, places),
        [shape] * len(places),
        [VMEM] * 2,
        (own, came),
        before=before,
    )


def finish(own_ref, came_ref, *refs):
    out_ref = refs[-1]
    piece = out_ref.shape[1]
    total = own_ref[:piece, :] + came_ref[:piece, :].astype(F32)
    for ref in refs[:-1]:
        total = total + ref[...].astype(F32)
    out_ref[...] = total.T.astype(out_ref.dtype)


def weight_terms(places, agg_ref, grad_pre_ref, *out_refs):
    width = agg_ref.shape[1]
    piece = width // sum(len(group) for group in places)
    for group, out in zip(places, out_refs):
        for i, place in enumerate(group):
            term = lax.dot_general(
                agg_ref[:, place * piece : (place + 1) * piece],
                grad_pre_ref[...],
                (((0,), (0,)), ((), ())),
                preferred_element_type=F32,
            )
            out[pl.ds(i * piece, piece), :] = term.astype(out.dtype)


def add_and_split(side_ref, kept_ref, came_ref, keep_ref, send_ref, total_ref):
    total_ref[...] = kept_ref[...] + came_ref[...]
    half = keep_ref.shape[1]
    side = side_ref[0] & 1
    for k in range(keep_ref.shape[0]):
        mine = pl.ds(pl.multiple_of((2 * k + side) * half, half), half)
        other = pl.ds(pl.multiple_of((2 * k + 1 - side) * half, half), half)
        keep_ref[k] = total_ref[mine, :]
        send_ref[k] = total_ref[other, :].astype(send_ref.dtype)


def add_and_spread(kept_ref, came_ref, keep_ref, *send_refs):
    keep_ref[...] = kept_ref[0] + came_ref[0].astype(F32)
    for k, out in enumerate(send_refs):
        out[...] = (kept_ref[k + 1] + came_ref[k + 1].astype(F32)).astype(out.dtype)


def add_all(*refs):
    terms = [ref[...].astype(F32) for ref in refs[:-1]]
    while len(terms) > 1:
        terms = [sum(terms[i + 1 : i + 2], terms[i]) for i in range(0, len(terms), 2)]
    refs[-1][...] = terms[0].astype(refs[-1].dtype)


def sum_of(terms, dtype, before, cost=0):
    return call(
        add_all,
        jax.ShapeDtypeStruct(terms[0].shape, dtype),
        [VMEM] * len(terms),
        tuple(terms),
        before=before,
        cost=cost,
    )


def stack_all(*refs):
    for i, ref in enumerate(refs[:-1]):
        refs[-1][i] = ref[...]


def place_shares(me_ref, side_ref, own_ref, other_ref, out_ref):
    half = own_ref.shape[2]
    for inner, ref in ((0, own_ref), (1, other_ref)):
        for turn in range(2):
            side = (side_ref[0] ^ turn) & 1
            for k in range(ref.shape[1]):
                place = (me_ref[0] ^ (2 * k + inner)) * 2 + side
                out_ref[pl.ds(pl.multiple_of(place * half, half), half), :] = ref[turn, k].astype(
                    out_ref.dtype
                )


def body(node_features, layer_weight, tile_values, tile_coords, tile_count, cotangent):
    n_row = lax.axis_size("row")
    n_col = lax.axis_size("col")
    ro, co = n_row // 2, n_col // 2
    my_row = lax.axis_index("row").astype(jnp.int32).reshape(1)
    my_col = lax.axis_index("col").astype(jnp.int32).reshape(1)
    shard_rows, width = cotangent.shape
    block_c, piece = node_features.shape
    limit = 12 + (4 * co * shard_rows * block_c) // MIB

    def swap(v, axis, bit):
        size = n_row if axis == "row" else n_col
        return lax.ppermute(v, axis, [(i, i ^ bit) for i in range(size)])

    halves = (range(0, ro // 2), range(ro // 2, ro))
    chunks = [(h, i) for h in range(2) for i in range(2)]
    owners = [[2 * k + i for k in halves[h]] for h, i in chunks]
    flat = [rel for rels in owners for rel in rels]

    def arriving(source, rels):
        parts = [swap(source, "row", rel) if rel else source for rel in rels]
        return jnp.concatenate(parts, axis=1) if len(parts) > 1 else parts[0]

    features = [arriving(node_features, rels) for rels in owners[:2]]
    near, far, own_features, first_away = dense_blocks(
        tile_values[0, 0],
        pltpu.with_memory_space_constraint(tile_coords[0, 0].T, pltpu.HBM),
        tile_count.reshape(-1),
        my_col,
        my_row,
        pltpu.with_memory_space_constraint(features[0], pltpu.HBM),
        co,
        shard_rows,
        max(limit, 48),
    )
    features[0] = own_features
    features += [arriving(own_features if ro == 2 else node_features, rels) for rels in owners[2:]]
    away, kept = all_products(near, far, features[:2], limit)

    keeps = [*kept, None, None]
    cames = [swap(v, "col", 1) for v in (first_away, *away)] + [None, None]
    stages = co.bit_length() - 1
    done = [0] * 4
    turns = [0, 1, 0, 2, 1, 3, 2, 3] if stages == 2 else [0, 1, 2, 3] * stages
    weight_rows = call(
        functools.partial(order_rows, owners),
        jax.ShapeDtypeStruct(layer_weight.shape, BF16),
        [SMEM, VMEM],
        (my_row, layer_weight),
        before=(kept[0],),
    )
    last = weight_rows
    for turn, i in enumerate(turns):
        before = [last]
        if stages == 2 and turn == 6:
            before.extend(cames[:2])
        cost = COST_F if i in (1, 2) and done[i] == 0 else COST_U if turn == 6 else 0
        keeps[i], last = halved(keeps[i], cames[i], before, cost)
        cames[i] = swap(last, "col", 2 << done[i])
        done[i] += 1
        if turn < 2:
            next_away, keeps[turn + 2] = last_products(near, far, features[turn + 2], limit, (last,))
            cames[turn + 2] = swap(next_away, "col", 1)
            last = keeps[turn + 2]
    totals = [[keep, came] for keep, came in zip(keeps, cames)]

    out_groups = ((3,), (2,), (1, 0))
    hidden, agg, grad_pre, grads = layer(
        totals, out_groups, weight_rows, cotangent, (last,)
    )

    places = [[flat.index(2 * k + inner) for k in range(ro)] for inner in range(2)]
    term_shape = (width // 2, width)
    weight_kept, weight_send = call(
        functools.partial(weight_terms, places),
        (jax.ShapeDtypeStruct(term_shape, F32), jax.ShapeDtypeStruct(term_shape, F32)),
        [VMEM] * 2,
        (agg, grad_pre),
    )
    state = {"w": [weight_kept, swap(weight_send, "row", 1)], "last": weight_send}

    def order(*more):
        return [state["last"], *more]

    half_share = (ro, piece // 2, width)

    def weight_core():
        keep, send = call(
            add_and_split,
            (jax.ShapeDtypeStruct(half_share, F32), jax.ShapeDtypeStruct(half_share, BF16)),
            [SMEM, VMEM, VMEM],
            (my_col, *state["w"]),
            [pltpu.VMEM((ro * piece, width), F32)],
            before=order(),
        )
        state["last"] = send
        state["w"] = [keep, swap(send, "col", 1)]

    def weight_side():
        shape = half_share[1:]
        outs = call(
            add_and_spread,
            [jax.ShapeDtypeStruct(shape, F32)] + [jax.ShapeDtypeStruct(shape, BF16)] * (ro - 1),
            [VMEM] * 2,
            tuple(state["w"]),
            before=order(),
        )
        state["last"] = outs[0]
        state["w"] = [outs[0]] + [swap(v, "row", 2 * (k + 1)) for k, v in enumerate(outs[1:])]
        state["bit"] = n_col // 2

    def weight_line(cost=0):
        bit = state["bit"]
        total = sum_of(state["w"], BF16 if bit > 2 else F32, order(), cost)
        state["last"] = total
        state["w"] = [total, swap(total, "col", bit)]
        state["bit"] = bit // 2

    def weight_sum():
        total = sum_of(state["w"], BF16, order(), COST_W)
        state["last"] = total
        state["w"] = [total] + [swap(total, "row", 2 * k) for k in range(1, ro)]

    def weight_stack(axis, cost=0):
        total = call(
            stack_all,
            jax.ShapeDtypeStruct((len(state["w"]),) + state["w"][0].shape, BF16),
            [VMEM] * len(state["w"]),
            tuple(state["w"]),
            before=order(),
            cost=cost,
        )
        state["last"] = total
        state["w"] = [total, swap(total, axis, 1)]

    rows = {"C": grads[0], "A": grads[1], "M": grads[2]}
    bits = {"C": n_col // 2, "A": 1, "M": n_col // 2}
    came_rows = {name: swap(rows[name], "col", bits[name]) for name in rows}
    backs = {}

    def join(name, cost=0):
        first, second = rows[name], came_rows[name]
        bit = n_col // 2 if name == "A" and bits[name] == 1 else bits[name] // 2
        bits[name] = bit
        rows[name] = state["last"] = joined(first, second, order(), cost)
        if not (name == "A" and bit == 1):
            came_rows[name] = swap(rows[name], "col", bit)

    def back(members, pair, cost=0, more=()):
        dtypes = [BF16 if chunk[1] else F32 for chunk in members]
        outs = back_of(near, far, pair, dtypes, limit, order(*more), cost)
        state["last"] = outs[0]
        for chunk, out in zip(members, outs):
            backs[chunk] = swap(out, "row", 1) if chunk[1] else out

    arrived = []

    def send_parts(h):
        sent = [p for p, k in enumerate(halves[h]) if k > 0]
        if sent:
            parts = parts_to_send(backs[h, 0], backs[h, 1], sent, piece, order())
            state["last"] = parts[0]
            arrived.extend(swap(v, "row", 2 * halves[h][p]) for p, v in zip(sent, parts))

    weight_core()
    join("C")
    weight_side()
    join("A")
    join("M")
    for _ in range(stages - 1):
        join("C")
    weight_line()
    for _ in range(stages - 1):
        join("A", COST)
    for _ in range(stages - 1):
        join("M")
    for _ in range(stages - 1):
        weight_line(COST_L)
    back([(1, 1)], (rows["C"], came_rows["C"]))
    weight_sum()
    join("A", COST_S)
    back([(1, 0)], (rows["A"],))
    send_parts(1)
    weight_stack("col", COST_K)
    back([(0, 1), (0, 0)], (rows["M"], came_rows["M"]), COST_M)
    weight_stack("row")
    send_parts(0)
    state["last"] = marked(state["last"], *arrived, cost=COST)
    grad_features = call(
        finish,
        jax.ShapeDtypeStruct((block_c, piece), BF16),
        [VMEM] * (2 + len(arrived)),
        (backs[0, 0], backs[0, 1], *arrived),
        before=order(),
    )
    grad_weight = call(
        place_shares,
        jax.ShapeDtypeStruct((width, width), F32),
        [SMEM, SMEM, VMEM, VMEM],
        (my_row, my_col, *state["w"]),
    )
    return (hidden, grad_weight, grad_features)


def solution(mesh):
    in_specs = (
        P("col", "row"),
        P(),
        P("row", "col", None, None, None),
        P("row", "col", None, None),
        P("row", "col"),
        P(("row", "col"), None),
    )
    out_specs = (P(("row", "col"), None), P(), P("col", "row"))
    return jax.shard_map(body, mesh=mesh, in_specs=in_specs, out_specs=out_specs, check_vma=False)
```
